32 devices in a mesh: sector: 4 (over z), tm: 2 (over x), space: 4 (over y, core).
Axes of the slice: x: 2, y: 2, z: 4, core: 2. Of those that a mesh axis runs over, the one named last changes fastest.
Arguments:
- records: bfloat16 [16, 592, 3, 8192], P('sector', 'tm', None, 'space'), may hold values from -6 to 6
- block_start: int32 [16], replicated, may hold values from 0 to 231, as said below
- slab_index: int32 [8192], P('space'), may hold values from 0 to 15
- weight_table: float32 [16], replicated, may hold values from 0.25 to 4
Outputs:
- mode_fields: bfloat16 [8, 32, 2, 8, 3, 8192], P(None, ('sector', 'tm'), None, None, None, 'space')
- energy: float32 [8, 32, 8], P(None, ('sector', 'tm'))
The draws below stay inside these ranges and needn't reach their ends.
Inputs may be any that keep to these rules, and one draw needn't show every extreme that they name: `block_start`: block j of each record (j < 8) starts at j * 32 plus 0 to 7 snapshots.
All inputs are finite; a program needn't handle non-finite values.
Results may differ from the reference program's by a relative error of at most 0.02.
Values may be sent and summed in bfloat16 or wider, within the bound.
No kernel may reach another device: no remote copies, remote signals or barrier semaphores. Data moves between devices by JAX's collectives and lax.ppermute only.
A program may use at most 128 MiB of HBM per device.

```python
import math
import jax
import jax.numpy as jnp
from jax import lax

NFFT = 64
NFREQ = 32
SECTORS = 16
ORDERS = 8
FIELDS = 3
MODES = 8
SUBIT = 4
NSLAB = 16
BLK_DEV = 8
TREC = 296
BLOCKS = 16
TIME = 592
CELLS = 8192


def draw_block_start(key, part):
    jitter = jax.random.randint(key, (BLOCKS,), 0, NFFT // 8, dtype=jnp.int32)
    jitter = jitter.at[0].set(0).at[BLOCKS - 1].set(NFFT // 8 - 1)
    base = jnp.arange(BLOCKS, dtype=jnp.int32) % BLK_DEV * (NFFT // 2)
    return (base + jitter).astype(jnp.int32)


def with_ends(entries, own_key, smallest, high):
    extent = entries.shape
    index_at = [jax.random.randint(jax.random.fold_in(own_key, axis), (), 0, extent[axis]) for axis in range(len(extent))]
    entries = entries.at[tuple(index_at)].set(smallest)
    longest = extent.index(max(extent))
    index_at[longest] = (index_at[longest] + 1) % extent[longest]
    return entries.at[tuple(index_at)].set(high)


def shard_levels(own_key, shape, pieces, low, top_value):
    gain, own = 1.0, jax.random.fold_in(own_key, 6)
    for position, shards_of in pieces:
        heights = jnp.exp(jax.random.uniform(jax.random.fold_in(own, position), (shards_of,), jnp.float32, low / len(pieces), top_value / len(pieces)))
        gain = gain * jnp.repeat(heights, shape[position] // shards_of).reshape([-1 if axis == position else 1 for axis in range(len(shape))])
    return gain


def noise(rng, extent, deviation, bound, shards=(), held_as=jnp.bfloat16):
    entries = jax.random.normal(rng, extent, jnp.float32) * deviation
    if len(shards) > 0:
        entries = shard_levels(rng, extent, shards, -0.22, 0.18) * entries
    return jnp.clip(entries, min=-bound, max=bound).astype(held_as)


def setup_inputs(seed: int = 0) -> dict:
    seeds = jax.random.split(jax.random.key(seed), 5)
    return {
        "records": noise(seeds[0], (SECTORS, TIME, FIELDS, CELLS), 1.0, 6.0, ((0, 4), (1, 2), (3, 4))),
        "block_start": draw_block_start(jax.random.fold_in(seeds[4], 71), 0),
        "slab_index": with_ends(jax.random.randint(seeds[2], (CELLS,), 0, NSLAB), jax.random.fold_in(seeds[2], 1), 0, NSLAB - 1).astype(jnp.int32),
        "weight_table": jnp.clip(jnp.exp(jax.random.uniform(seeds[3], (NSLAB,), jnp.float32, math.log(0.25), math.log(4.0))), 0.25, 4.0),
    }


EPSILON = 1e-06

def time_table(length, freq_count):
    steps_t = jnp.arange(length, dtype=jnp.float32)
    freq_f = jnp.arange(freq_count, dtype=jnp.float32)
    window = 0.5 - 0.5 * jnp.cos(2.0 * math.pi * steps_t / length)
    angles = 2.0 * math.pi * freq_f[:, None] * steps_t[None, :] / length
    both = jnp.stack([window * jnp.cos(angles), -window * jnp.sin(angles)])
    return (both / math.sqrt(length)).astype(jnp.bfloat16)

def order_table(orders, sectors):
    order_m = jnp.arange(orders, dtype=jnp.float32)[:, None]
    sector_s = jnp.arange(sectors, dtype=jnp.float32)[None, :]
    angles = 2.0 * math.pi * order_m * sector_s / sectors
    cosine = jnp.cos(angles)
    sine_part = jnp.sin(angles)
    upper_row = jnp.stack([cosine, sine_part], -1)
    lower_row = jnp.stack([-sine_part, cosine], -1)
    return (jnp.stack([upper_row, lower_row], 1) / math.sqrt(sectors)).astype(jnp.bfloat16)

def matmul_high(left_side, right_side):
    return jnp.matmul(left_side, right_side, precision=lax.Precision.HIGHEST)

def subspace(gram_re, gram_im):
    order_size = gram_re.shape[-1]
    basis_re = jnp.broadcast_to(jnp.eye(order_size, MODES, dtype=jnp.float32), gram_re.shape[:-1] + (MODES,))
    basis_im = jnp.zeros_like(basis_re)
    for sweep in range(SUBIT):
        image_re = matmul_high(gram_re, basis_re) - matmul_high(gram_im, basis_im)
        image_im = matmul_high(gram_re, basis_im) + matmul_high(gram_im, basis_re)
        done_re = []
        done_im = []
        for column in range(MODES):
            vec_re = image_re[..., column]
            vec_im = image_im[..., column]
            for earlier in range(column):
                old_re = done_re[earlier]
                old_im = done_im[earlier]
                proj_re = lax.optimization_barrier(jnp.sum(old_re * vec_re + old_im * vec_im, -1, keepdims=True))
                proj_im = lax.optimization_barrier(jnp.sum(old_re * vec_im - old_im * vec_re, -1, keepdims=True))
                vec_re = vec_re - (proj_re * old_re - proj_im * old_im)
                vec_im = vec_im - (proj_re * old_im + proj_im * old_re)
            length_v = jnp.sqrt(lax.optimization_barrier(jnp.sum(vec_re * vec_re + vec_im * vec_im, -1, keepdims=True)) + EPSILON)
            done_re.append(vec_re / length_v)
            done_im.append(vec_im / length_v)
        basis_re = jnp.stack(done_re, -1)
        basis_im = jnp.stack(done_im, -1)
    return (basis_re, basis_im)

def reference(records, block_start, slab_index, weight_table):
    time_basis = time_table(NFFT, NFREQ).astype(jnp.float32)
    azimuth = order_table(ORDERS, SECTORS).astype(jnp.float32)
    weight = weight_table[slab_index]
    cell_total = FIELDS * CELLS
    starts_abs = jnp.arange(BLOCKS, dtype=jnp.int32) // BLK_DEV * TREC + block_start.astype(jnp.int32)

    def one_freq(freq):
        freq_row = lax.dynamic_index_in_dim(time_basis, freq, 1, keepdims=False)

        def one_block(start_at):
            segment = lax.dynamic_slice_in_dim(records, start_at, NFFT, 1).astype(jnp.float32)
            return jnp.einsum('ct,stkx->sckx', freq_row, segment).astype(jnp.bfloat16)
        spectra = lax.map(one_block, starts_abs)
        spectra = lax.optimization_barrier(spectra).astype(jnp.float32)
        coeffs = jnp.einsum('mcse,bsekx->mcbkx', azimuth, spectra).astype(jnp.bfloat16)
        coeffs = lax.optimization_barrier(coeffs)
        coeffs_wide = coeffs.astype(jnp.float32)
        weighted = lax.optimization_barrier((coeffs_wide * weight).astype(jnp.bfloat16)).astype(jnp.float32)
        products = jnp.einsum('mcbkx,mdekx->mcbde', weighted, coeffs_wide)
        gram_re = products[:, 0, :, 0, :] + products[:, 1, :, 1, :]
        gram_im = products[:, 0, :, 1, :] - products[:, 1, :, 0, :]
        basis_re, basis_im = subspace(gram_re, gram_im)
        image_re = matmul_high(gram_re, basis_re) - matmul_high(gram_im, basis_im)
        image_im = matmul_high(gram_re, basis_im) + matmul_high(gram_im, basis_re)
        energy = lax.optimization_barrier(jnp.sum(basis_re * image_re + basis_im * image_im, -2)) / cell_total
        short_re = lax.optimization_barrier(basis_re.astype(jnp.bfloat16)).astype(jnp.float32)
        short_im = lax.optimization_barrier(basis_im.astype(jnp.bfloat16)).astype(jnp.float32)
        first_row = jnp.stack([short_re, short_im], -2)
        second_row = jnp.stack([-short_im, short_re], -2)
        mixing = jnp.stack([first_row, second_row], 1)
        fields_out = jnp.einsum('mcbkx,mcbdj->mdjkx', coeffs_wide, mixing)
        factor = lax.rsqrt(energy)[:, None, :, None, None] * jnp.sqrt(weight)
        return ((fields_out * factor).astype(jnp.bfloat16), energy)
    mode_fields, energy = lax.map(one_freq, jnp.arange(NFREQ, dtype=jnp.int32))
    return (jnp.transpose(mode_fields, (1, 0, 2, 3, 4, 5)), jnp.transpose(energy, (1, 0, 2)))
```

```python
import functools
import math

import jax
import jax.numpy as jnp
from jax import lax
from jax.experimental import pallas as pl
from jax.experimental.pallas import tpu as pltpu
from jax.sharding import PartitionSpec as P

NFFT = 64
NFREQ = 32
MODES = 8
SUBIT = 4
LANES = 128
EPSILON = 1e-06
VMEM_LIMIT = 48 * 1024 * 1024


def time_table(length, freq_count):
    steps_t = jnp.arange(length, dtype=jnp.float32)
    freq_f = jnp.arange(freq_count, dtype=jnp.float32)
    window = 0.5 - 0.5 * jnp.cos(2.0 * math.pi * steps_t / length)
    angles = 2.0 * math.pi * freq_f[:, None] * steps_t[None, :] / length
    both = jnp.stack([window * jnp.cos(angles), -window * jnp.sin(angles)])
    return (both / math.sqrt(length)).astype(jnp.bfloat16)


def order_table(orders, sectors):
    order_m = jnp.arange(orders, dtype=jnp.float32)[:, None]
    sector_s = jnp.arange(sectors, dtype=jnp.float32)[None, :]
    angles = 2.0 * math.pi * order_m * sector_s / sectors
    cosine = jnp.cos(angles)
    sine_part = jnp.sin(angles)
    upper_row = jnp.stack([cosine, sine_part], -1)
    lower_row = jnp.stack([-sine_part, cosine], -1)
    return (jnp.stack([upper_row, lower_row], 1) / math.sqrt(sectors)).astype(jnp.bfloat16)


def placed_time_basis(block_start, tm_count, rec_len):
    blocks = block_start.shape[0] // tm_count
    basis = time_table(NFFT, NFREQ)
    place = (
        block_start[:, None, None] + jnp.arange(NFFT, dtype=jnp.int32)[None, :, None]
        == jnp.arange(rec_len, dtype=jnp.int32)[None, None, :]
    ).astype(jnp.bfloat16)
    table = jnp.einsum(
        "eft,jbtu->jfebu",
        basis,
        place.reshape(tm_count, blocks, NFFT, rec_len),
        preferred_element_type=jnp.float32,
    ).astype(jnp.bfloat16)
    return table.reshape(tm_count, NFREQ * 2 * blocks, rec_len)


def coeff_kernel(sectors, freqs, time_ref, azimuth_ref, weight_ref, before_ref, record_ref,
                 coeff_ref, gram_ref, spectra):
    step = pl.program_id(0)
    tm_count = time_ref.shape[0]
    rows = azimuth_ref.shape[0]
    depth = azimuth_ref.shape[1] // sectors
    columns = record_ref.shape[-1]

    @pl.when(step < sectors)
    def _():
        parts = [
            jnp.dot(time_ref[j], record_ref[0, j, 0], preferred_element_type=jnp.float32)
            for j in range(tm_count)
        ]
        block_rows = depth // (2 * tm_count)
        joined = jnp.stack([x.reshape(-1, block_rows, columns) for x in parts], 1)
        spectra[step] = joined.reshape(spectra.shape[1:]).astype(jnp.bfloat16)

    @pl.when(step >= sectors)
    def _():
        first = (step - sectors) * freqs
        blocks = depth // 2
        packed = LANES // depth
        lane = lax.broadcasted_iota(jnp.int32, (blocks, LANES), 1)
        owner = lax.broadcasted_iota(jnp.int32, (depth, LANES), 1) // depth
        for n in range(freqs):
            at = pl.multiple_of((first + n) * depth, depth)
            own = spectra[:, pl.ds(at, depth), :].reshape(sectors * depth, columns)
            coeffs = jnp.dot(
                azimuth_ref[...], own, preferred_element_type=jnp.float32
            ).astype(jnp.bfloat16)
            coeff_ref[n] = coeffs
            weighted = (coeffs.astype(jnp.float32) * weight_ref[...]).astype(jnp.bfloat16)
            products = lax.dot_general(
                weighted, coeffs, (((1,), (1,)), ((), ())), preferred_element_type=jnp.float32
            )
            for g in range(rows // LANES):
                part = products[g * LANES:(g + 1) * LANES, g * LANES:(g + 1) * LANES]
                own_order = jnp.zeros((depth, LANES), jnp.float32)
                for q in range(packed):
                    own_order = jnp.where(owner == q, part[q * depth:(q + 1) * depth], own_order)
                upper, lower = own_order[:blocks], own_order[blocks:]
                crossed = jnp.where(
                    lane % depth < blocks,
                    pltpu.roll(lower, LANES - blocks, 1),
                    -pltpu.roll(lower, blocks, 1),
                )
                gram_ref[n, g] = before_ref[n, g] + upper + crossed


def coeffs_and_gram(arrived, time_basis, azimuth, weight, before):
    sec_count, tm_count, sec_local, rec_len, columns = arrived.shape
    sectors = sec_count * sec_local
    rows = azimuth.shape[0]
    depth = azimuth.shape[1] // sectors
    freqs = 4
    steps = NFREQ // freqs
    later = lambda i: jnp.maximum(i - sectors, 0)
    early = lambda i: jnp.minimum(i, sectors - 1)
    gram_block = (freqs,) + before.shape[1:]
    flops = 2 * columns * (
        sectors * tm_count * time_basis.shape[1] * rec_len
        + NFREQ * rows * sectors * depth
        + NFREQ * rows * rows
    )
    return pl.pallas_call(
        functools.partial(coeff_kernel, sectors, freqs),
        grid=(sectors + steps,),
        in_specs=[
            pl.BlockSpec(time_basis.shape, lambda i: (0, 0, 0)),
            pl.BlockSpec(azimuth.shape, lambda i: (0, 0)),
            pl.BlockSpec(weight.shape, lambda i: (0, 0)),
            pl.BlockSpec(gram_block, lambda i: (later(i), 0, 0, 0)),
            pl.BlockSpec(
                (1, tm_count, 1, rec_len, columns),
                lambda i: (early(i) // sec_local, 0, early(i) % sec_local, 0, 0),
            ),
        ],
        out_specs=[
            pl.BlockSpec((freqs, rows, columns), lambda i: (later(i), 0, 0)),
            pl.BlockSpec(gram_block, lambda i: (later(i), 0, 0, 0)),
        ],
        out_shape=[
            jax.ShapeDtypeStruct((NFREQ, rows, columns), jnp.bfloat16),
            jax.ShapeDtypeStruct(before.shape, jnp.float32),
        ],
        scratch_shapes=[pltpu.VMEM((sectors, NFREQ * depth, columns), jnp.bfloat16)],
        compiler_params=pltpu.CompilerParams(vmem_limit_bytes=VMEM_LIMIT),
        cost_estimate=pl.CostEstimate(
            flops=flops, bytes_accessed=2 * (arrived.size + NFREQ * rows * columns), transcendentals=0
        ),
        name="coeffs_and_gram",
    )(time_basis, azimuth, weight, before, arrived)


def subspace_kernel(cell_total, re_ref, im_ref, basis_ref, energy_ref):
    size = re_ref.shape[0]
    column_re = [re_ref[q] for q in range(size)]
    column_im = [im_ref[q] for q in range(size)]

    def image_of(vec_re, vec_im):
        out_re, out_im = [], []
        for j in range(MODES):
            sum_re = jnp.zeros_like(column_re[0])
            sum_im = jnp.zeros_like(column_re[0])
            for q in range(size):
                at_re, at_im = vec_re[j][q:q + 1], vec_im[j][q:q + 1]
                sum_re += column_re[q] * at_re - column_im[q] * at_im
                sum_im += column_re[q] * at_im + column_im[q] * at_re
            out_re.append(sum_re)
            out_im.append(sum_im)
        return out_re, out_im

    total = lambda x: jnp.sum(x, 0, keepdims=True)
    vec_re, vec_im = column_re[:MODES], column_im[:MODES]
    for sweep in range(SUBIT):
        if sweep > 0:
            vec_re, vec_im = image_of(vec_re, vec_im)
        vec_re, vec_im = list(vec_re), list(vec_im)
        for i in range(MODES):
            scale = 1.0 / jnp.sqrt(total(vec_re[i] * vec_re[i] + vec_im[i] * vec_im[i]) + EPSILON)
            own_re, own_im = vec_re[i] * scale, vec_im[i] * scale
            vec_re[i], vec_im[i] = own_re, own_im
            for j in range(i + 1, MODES):
                proj_re = total(own_re * vec_re[j] + own_im * vec_im[j])
                proj_im = total(own_re * vec_im[j] - own_im * vec_re[j])
                vec_re[j] = vec_re[j] - (proj_re * own_re - proj_im * own_im)
                vec_im[j] = vec_im[j] - (proj_re * own_im + proj_im * own_re)
    image_re, image_im = image_of(vec_re, vec_im)
    for j in range(MODES):
        basis_ref[0, j] = vec_re[j]
        basis_ref[1, j] = vec_im[j]
        energy_ref[j:j + 1] = total(vec_re[j] * image_re[j] + vec_im[j] * image_im[j]) / cell_total


def subspace(gram_re, gram_im, cell_total):
    size, _, pairs = gram_re.shape
    return pl.pallas_call(
        functools.partial(subspace_kernel, float(cell_total)),
        out_shape=[
            jax.ShapeDtypeStruct((2, MODES, size, pairs), jnp.float32),
            jax.ShapeDtypeStruct((MODES, pairs), jnp.float32),
        ],
        name="subspace",
    )(gram_re, gram_im)


def mix_kernel(orders, coeff_ref, mixing_ref, factor_ref, root_ref, out_ref):
    freqs, rows, depth = mixing_ref.shape
    total = orders * depth
    row = lax.broadcasted_iota(jnp.int32, (rows, total), 0) // (rows // orders)
    column = lax.broadcasted_iota(jnp.int32, (rows, total), 1) // depth
    for n in range(freqs):
        wide = jnp.concatenate([mixing_ref[n]] * orders, axis=1)
        wide = jnp.where(row == column, wide, jnp.zeros_like(wide))
        fields = jnp.dot(wide, coeff_ref[n], preferred_element_type=jnp.float32)
        out_ref[0, n] = (fields * (factor_ref[n] * root_ref[...])).astype(jnp.bfloat16)


def mix(coeffs, mixing, factor, root_weight, owners, orders):
    _, rows, columns = coeffs.shape
    out_rows, depth = mixing.shape[1:]
    freqs = NFREQ // owners
    return pl.pallas_call(
        functools.partial(mix_kernel, orders),
        grid=(owners,),
        in_specs=[
            pl.BlockSpec((freqs, rows, columns), lambda i: (i, 0, 0)),
            pl.BlockSpec((freqs, out_rows, depth), lambda i: (i, 0, 0)),
            pl.BlockSpec((freqs, out_rows, 1), lambda i: (i, 0, 0)),
            pl.BlockSpec(root_weight.shape, lambda i: (0, 0)),
        ],
        out_specs=pl.BlockSpec((1, freqs, out_rows, columns), lambda i: (i, 0, 0, 0)),
        out_shape=jax.ShapeDtypeStruct((owners, freqs, out_rows, columns), jnp.bfloat16),
        compiler_params=pltpu.CompilerParams(vmem_limit_bytes=VMEM_LIMIT),
        cost_estimate=pl.CostEstimate(
            flops=2 * NFREQ * out_rows * rows * columns,
            bytes_accessed=2 * NFREQ * (rows + out_rows) * columns,
            transcendentals=0,
        ),
        name="mix",
    )(coeffs, mixing, factor, root_weight)


def pack_kernel(record_ref, out_ref):
    owners, _, _, part = out_ref.shape
    for d in range(owners):
        out_ref[d, 0] = record_ref[0, 0, :, d * part:(d + 1) * part]


def pack(by_field, k, owners):
    sec_local, _, rec_len, cells = by_field.shape
    part = cells // owners
    return pl.pallas_call(
        pack_kernel,
        grid=(sec_local,),
        in_specs=[pl.BlockSpec((1, 1, rec_len, cells), lambda i: (i, k, 0, 0))],
        out_specs=pl.BlockSpec((owners, 1, rec_len, part), lambda i: (0, i, 0, 0)),
        out_shape=jax.ShapeDtypeStruct((owners, sec_local, rec_len, part), by_field.dtype),
        compiler_params=pltpu.CompilerParams(vmem_limit_bytes=VMEM_LIMIT),
        cost_estimate=pl.CostEstimate(
            flops=0, bytes_accessed=4 * sec_local * rec_len * cells, transcendentals=0
        ),
        name="pack",
    )(by_field)


def unpack_kernel(piece_ref, *refs):
    out_ref = refs[-1]
    owners, part = piece_ref.shape[0], piece_ref.shape[-1]
    for d in range(owners):
        out_ref[:, 0, :, 0, :, d * part:(d + 1) * part] = piece_ref[d, 0]


def unpack(pieces, k, fields, whole):
    owners, freqs, orders, two, modes, part = pieces.shape
    shape = (orders, freqs, two, fields, modes, owners * part)
    inputs = [pieces] if whole is None else [pieces, whole]
    in_specs = [
        pl.BlockSpec((owners, 1, orders, two, modes, part), lambda i: (0, i, 0, 0, 0, 0)),
        pl.BlockSpec(memory_space=pl.ANY),
    ]
    return pl.pallas_call(
        unpack_kernel,
        grid=(freqs,),
        in_specs=in_specs[:len(inputs)],
        out_specs=pl.BlockSpec(
            (orders, 1, two, 1, modes, owners * part), lambda i: (0, i, 0, k, 0, 0)
        ),
        out_shape=jax.ShapeDtypeStruct(shape, pieces.dtype),
        input_output_aliases={} if whole is None else {1: 0},
        compiler_params=pltpu.CompilerParams(vmem_limit_bytes=VMEM_LIMIT),
        cost_estimate=pl.CostEstimate(flops=0, bytes_accessed=4 * pieces.size, transcendentals=0),
        name="unpack",
    )(*inputs)


def local(records, block_start, slab_index, weight_table):
    sec_local, rec_len, fields, cell_local = records.shape
    sec_count = lax.axis_size("sector")
    tm_count = lax.axis_size("tm")
    space_count = lax.axis_size("space")
    owners = sec_count * tm_count
    owner_axes = ("sector", "tm")
    sectors = sec_local * sec_count
    orders = sectors // 2
    blocks = block_start.shape[0]
    depth = 2 * blocks
    part = cell_local // owners
    own_freqs = NFREQ // owners
    me = lax.axis_index("sector") * tm_count + lax.axis_index("tm")

    by_field = jnp.transpose(records, (0, 2, 1, 3))
    arrived = []
    for k in range(fields):
        send = pack(by_field, k, owners)
        got = lax.all_to_all(send, owner_axes, split_axis=0, concat_axis=0, tiled=True)
        arrived.append(got.reshape(sec_count, tm_count, sec_local, rec_len, part))

    time_basis = placed_time_basis(block_start, tm_count, rec_len)
    azimuth = jnp.einsum(
        "mcse,bd->mcbsed",
        order_table(orders, sectors),
        jnp.eye(blocks, dtype=jnp.bfloat16),
    ).reshape(orders * depth, sectors * depth)
    own_slab = lax.dynamic_slice_in_dim(slab_index, me * part, part)
    weight = jnp.sum(
        jnp.where(
            own_slab[None, :] == jnp.arange(weight_table.shape[0], dtype=jnp.int32)[:, None],
            weight_table[:, None],
            0.0,
        ),
        0,
        keepdims=True,
    )

    groups = orders * depth // LANES
    gram = jnp.zeros((NFREQ, groups, blocks, LANES), jnp.float32)
    coeffs = []
    for k in range(fields):
        own, gram = coeffs_and_gram(arrived[k], time_basis, azimuth, weight, gram)
        coeffs.append(own)

    if own_freqs % space_count == 0:
        axes = owner_axes + ("space",)
    else:
        gram = lax.psum(gram, "space")
        axes = owner_axes
    solvers = math.prod(lax.axis_size(a) for a in axes)
    solved = NFREQ // solvers
    gram = gram.reshape((solvers, solved) + gram.shape[1:])
    gram = lax.all_to_all(gram, axes, split_axis=0, concat_axis=0, tiled=True)
    gram = jnp.sum(gram, 0).reshape(solved, groups, blocks, LANES // depth, 2, blocks)
    gram = jnp.transpose(gram, (4, 5, 2, 0, 1, 3)).reshape(2, blocks, blocks, solved * orders)
    basis, energy = subspace(gram[0], gram[1], fields * cell_local * space_count)

    short = basis.astype(jnp.bfloat16).reshape(2, MODES, blocks, solved, orders)
    short = jnp.transpose(short, (3, 4, 0, 1, 2))
    short_re, short_im = short[:, :, 0], short[:, :, 1]
    mixing = jnp.stack(
        [jnp.concatenate([short_re, -short_im], -1), jnp.concatenate([short_im, short_re], -1)], 2
    ).reshape(solved, orders * 2 * MODES * depth)
    energy = jnp.transpose(energy.reshape(MODES, solved, orders), (1, 2, 0)).reshape(solved, -1)
    high = energy.astype(jnp.bfloat16)
    rest = energy - high.astype(jnp.float32)
    middle = rest.astype(jnp.bfloat16)
    low = (rest - middle.astype(jnp.float32)).astype(jnp.bfloat16)
    packet = jnp.concatenate([mixing, high, middle, low], 1)
    width = -(-packet.shape[1] // LANES) * LANES
    packet = jnp.pad(packet, ((0, 0), (0, width - packet.shape[1])))
    packet = packet.reshape(1, solved, width // LANES, LANES)
    packet = jnp.broadcast_to(packet, (solvers,) + packet.shape[1:])
    packet = lax.all_to_all(packet, axes, split_axis=0, concat_axis=0, tiled=True)
    packet = packet.reshape(NFREQ, width)
    count = orders * MODES
    mixing = packet[:, :orders * 2 * MODES * depth].reshape(NFREQ, orders * 2 * MODES, depth)
    tail = packet[:, orders * 2 * MODES * depth:].astype(jnp.float32)
    energy = (tail[:, :count] + tail[:, count:2 * count]) + tail[:, 2 * count:3 * count]
    energy = energy.reshape(NFREQ, orders, MODES)
    factor = jnp.broadcast_to(
        lax.rsqrt(energy)[:, :, None, :], (NFREQ, orders, 2, MODES)
    ).reshape(NFREQ, orders * 2 * MODES, 1)
    root_weight = jnp.sqrt(weight)

    mode_fields = None
    for k in range(fields):
        send = mix(coeffs[k], mixing, factor, root_weight, owners, orders)
        got = lax.all_to_all(send, owner_axes, split_axis=0, concat_axis=0, tiled=True)
        got = got.reshape(owners, own_freqs, orders, 2, MODES, part)
        mode_fields = unpack(got, k, fields, mode_fields)
    mode_fields = jnp.transpose(mode_fields, (0, 1, 2, 4, 3, 5))
    own_energy = lax.dynamic_slice_in_dim(energy, me * own_freqs, own_freqs)
    return (mode_fields, jnp.transpose(own_energy, (1, 0, 2)))


def solution(mesh):
    placed = (P("sector", "tm", None, "space"), P(), P("space"), P())
    return jax.shard_map(
        local,
        mesh=mesh,
        in_specs=placed,
        out_specs=(
            P(None, ("sector", "tm"), None, None, None, "space"),
            P(None, ("sector", "tm"), None),
        ),
        check_vma=False,
    )
```

```python
import functools
import math

import jax
import jax.numpy as jnp
from jax import lax
from jax.experimental import pallas as pl
from jax.experimental.pallas import tpu as pltpu
from jax.sharding import PartitionSpec as P

NFFT = 64
NFREQ = 32
MODES = 8
SUBIT = 4
LANES = 128
EPSILON = 1e-06
VMEM_LIMIT = 48 * 1024 * 1024


def time_table(length, freq_count):
    steps_t = jnp.arange(length, dtype=jnp.float32)
    freq_f = jnp.arange(freq_count, dtype=jnp.float32)
    window = 0.5 - 0.5 * jnp.cos(2.0 * math.pi * steps_t / length)
    angles = 2.0 * math.pi * freq_f[:, None] * steps_t[None, :] / length
    both = jnp.stack([window * jnp.cos(angles), -window * jnp.sin(angles)])
    return (both / math.sqrt(length)).astype(jnp.bfloat16)


def order_table(orders, sectors):
    order_m = jnp.arange(orders, dtype=jnp.float32)[:, None]
    sector_s = jnp.arange(sectors, dtype=jnp.float32)[None, :]
    angles = 2.0 * math.pi * order_m * sector_s / sectors
    cosine = jnp.cos(angles)
    sine_part = jnp.sin(angles)
    upper_row = jnp.stack([cosine, sine_part], -1)
    lower_row = jnp.stack([-sine_part, cosine], -1)
    return (jnp.stack([upper_row, lower_row], 1) / math.sqrt(sectors)).astype(jnp.bfloat16)


def half_span(blocks):
    half = blocks // 2
    return half, (half - 1) * (NFFT // 2) + NFFT // 8 + NFFT


def placed_time_basis(block_start, tm_count):
    blocks = block_start.shape[0] // tm_count
    half, span = half_span(blocks)
    basis = time_table(NFFT, NFREQ)
    first = jnp.arange(blocks, dtype=jnp.int32) // half * (half * (NFFT // 2))
    inside = block_start.reshape(tm_count, blocks) - first[None, :]
    place = (
        inside[:, :, None, None] + jnp.arange(NFFT, dtype=jnp.int32)[:, None]
        == jnp.arange(span, dtype=jnp.int32)[None, :]
    ).astype(jnp.bfloat16)
    table = jnp.einsum(
        "eft,jhbtu->jhfebu",
        basis,
        place.reshape(tm_count, 2, half, NFFT, span),
        preferred_element_type=jnp.float32,
    ).astype(jnp.bfloat16)
    return table.reshape(tm_count, 2, NFREQ * 2 * half, span)


def coeff_kernel(sec_count, freqs, orders, time_ref, azimuth_ref, weight_ref, before_ref, record_ref,
                 coeff_ref, gram_ref, spectra):
    step = pl.program_id(0)
    tm_count, halves, _, span = time_ref.shape
    sec_local, rec_len, columns = record_ref.shape[2:]
    sectors = spectra.shape[0]
    rows = spectra.shape[2] // NFREQ

    @pl.when(step < sec_count)
    def _():
        for s in range(sec_local):
            for h in range(halves):
                first = h * (rec_len - span) // (halves - 1)
                parts = [
                    jnp.dot(
                        time_ref[j, h],
                        record_ref[0, j, s, first:first + span],
                        preferred_element_type=jnp.float32,
                    ).reshape(NFREQ, rows // tm_count, columns)
                    for j in range(tm_count)
                ]
                joined = jnp.stack(parts, 1).reshape(NFREQ * rows, columns)
                spectra[step * sec_local + s, h] = joined.astype(jnp.bfloat16)

    @pl.when(step >= sec_count)
    def _():
        half_rows = azimuth_ref.shape[0]
        depth = half_rows // (2 * orders)
        blocks = depth * halves
        wide = orders * blocks
        row = lax.broadcasted_iota(jnp.int32, (wide, wide), 0) % blocks
        column = lax.broadcasted_iota(jnp.int32, (wide, wide), 1) % blocks
        owner = lax.broadcasted_iota(jnp.int32, (blocks, wide), 1) // blocks
        for n in range(freqs):
            at = pl.multiple_of(((step - sec_count) * freqs + n) * rows, rows)
            parts = [
                jnp.dot(
                    azimuth_ref[...],
                    spectra[:, h, pl.ds(at, rows), :].reshape(sectors * rows, columns),
                    preferred_element_type=jnp.float32,
                ).reshape(2 * orders, depth, columns)
                for h in range(halves)
            ]
            coeffs = jnp.stack(parts, 1).reshape(2 * wide, columns).astype(jnp.bfloat16)
            coeff_ref[n] = coeffs
            weighted = (coeffs.astype(jnp.float32) * weight_ref[...]).astype(jnp.bfloat16)
            swapped = jnp.concatenate([coeffs[wide:], coeffs[:wide]], 0)
            across = (((1,), (1,)), ((), ()))
            upper = lax.dot_general(
                weighted[:wide], coeffs, across, preferred_element_type=jnp.float32
            )
            lower = lax.dot_general(
                weighted[wide:], swapped, across, preferred_element_type=jnp.float32
            )
            real = upper[:, :wide] + lower[:, :wide]
            imag = upper[:, wide:] - lower[:, wide:]
            packed = jnp.where(row <= column, real, imag)
            own = packed[:blocks]
            for m in range(1, orders):
                own = jnp.where(owner == m, packed[m * blocks:(m + 1) * blocks], own)
            gram_ref[n] = before_ref[n] + own


def coeffs_and_gram(arrived, time_basis, azimuth, weight, before):
    sec_count, tm_count, sec_local, rec_len, columns = arrived.shape
    sectors = sec_count * sec_local
    halves = time_basis.shape[1]
    blocks, wide = before.shape[1:]
    rows = azimuth.shape[1] // sectors
    steps = 4
    freqs = NFREQ // steps
    later = lambda i: jnp.maximum(i - sec_count, 0)
    early = lambda i: jnp.minimum(i, sec_count - 1)
    flops = 2 * columns * (
        sectors * time_basis.size + NFREQ * halves * azimuth.size + NFREQ * 4 * wide * wide
    )
    return pl.pallas_call(
        functools.partial(coeff_kernel, sec_count, freqs, wide // blocks),
        grid=(sec_count + steps,),
        in_specs=[
            pl.BlockSpec(time_basis.shape, lambda i: (0, 0, 0, 0)),
            pl.BlockSpec(azimuth.shape, lambda i: (0, 0)),
            pl.BlockSpec(weight.shape, lambda i: (0, 0)),
            pl.BlockSpec((freqs, blocks, wide), lambda i: (later(i), 0, 0)),
            pl.BlockSpec(
                (1, tm_count, sec_local, rec_len, columns), lambda i: (early(i), 0, 0, 0, 0)
            ),
        ],
        out_specs=[
            pl.BlockSpec((freqs, 2 * wide, columns), lambda i: (later(i), 0, 0)),
            pl.BlockSpec((freqs, blocks, wide), lambda i: (later(i), 0, 0)),
        ],
        out_shape=[
            jax.ShapeDtypeStruct((NFREQ, 2 * wide, columns), jnp.bfloat16),
            jax.ShapeDtypeStruct(before.shape, jnp.float32),
        ],
        scratch_shapes=[pltpu.VMEM((sectors, halves, NFREQ * rows, columns), jnp.bfloat16)],
        compiler_params=pltpu.CompilerParams(vmem_limit_bytes=VMEM_LIMIT),
        cost_estimate=pl.CostEstimate(
            flops=flops,
            bytes_accessed=2 * (arrived.size + NFREQ * 2 * wide * columns),
            transcendentals=0,
        ),
        name="coeffs_and_gram",
    )(time_basis, azimuth, weight, before, arrived)


def subspace_kernel(cell_total, first, packed_ref, basis_ref, energy_ref):
    size, _, pairs = packed_ref.shape
    row = lax.broadcasted_iota(jnp.int32, (size, pairs), 0)
    column_re, column_im = [], []
    for q in range(size):
        down, along = packed_ref[q], packed_ref[:, q, :]
        column_re.append(jnp.where(row <= q, down, along))
        column_im.append(jnp.where(row > q, down, jnp.where(row == q, 0.0, -along)))

    def image_of(vec_re, vec_im):
        out_re, out_im = [], []
        for j in range(MODES):
            sum_re = jnp.zeros_like(column_re[0])
            sum_im = jnp.zeros_like(column_re[0])
            for q in range(size):
                at_re, at_im = vec_re[j][q:q + 1], vec_im[j][q:q + 1]
                sum_re += column_re[q] * at_re - column_im[q] * at_im
                sum_im += column_re[q] * at_im + column_im[q] * at_re
            out_re.append(sum_re)
            out_im.append(sum_im)
        return out_re, out_im

    total = lambda x: jnp.sum(x, 0, keepdims=True)
    vec_re = [column_re[q] for q in first]
    vec_im = [column_im[q] for q in first]
    for sweep in range(SUBIT):
        if sweep > 0:
            vec_re, vec_im = image_of(vec_re, vec_im)
        vec_re, vec_im = list(vec_re), list(vec_im)
        for i in range(MODES):
            scale = 1.0 / jnp.sqrt(total(vec_re[i] * vec_re[i] + vec_im[i] * vec_im[i]) + EPSILON)
            own_re, own_im = vec_re[i] * scale, vec_im[i] * scale
            vec_re[i], vec_im[i] = own_re, own_im
            for j in range(i + 1, MODES):
                proj_re = total(own_re * vec_re[j] + own_im * vec_im[j])
                proj_im = total(own_re * vec_im[j] - own_im * vec_re[j])
                vec_re[j] = vec_re[j] - (proj_re * own_re - proj_im * own_im)
                vec_im[j] = vec_im[j] - (proj_re * own_im + proj_im * own_re)
    image_re, image_im = image_of(vec_re, vec_im)
    for j in range(MODES):
        basis_ref[0, j] = vec_re[j]
        basis_ref[1, j] = vec_im[j]
        energy_ref[j:j + 1] = total(vec_re[j] * image_re[j] + vec_im[j] * image_im[j]) / cell_total


def subspace(packed, first, cell_total):
    size, _, pairs = packed.shape
    return pl.pallas_call(
        functools.partial(subspace_kernel, float(cell_total), first),
        out_shape=[
            jax.ShapeDtypeStruct((2, MODES, size, pairs), jnp.float32),
            jax.ShapeDtypeStruct((MODES, pairs), jnp.float32),
        ],
        name="subspace",
    )(packed)


def mix_kernel(orders, own_freqs, coeff_ref, mixing_ref, spread_ref, factor_ref, root_ref, *refs):
    out_ref = refs[-1]
    freqs, rows, _ = mixing_ref.shape
    total = spread_ref.shape[1]
    blocks = total // (2 * orders)
    row = lax.broadcasted_iota(jnp.int32, (rows, total), 0) // (rows // orders)
    column = lax.broadcasted_iota(jnp.int32, (rows, total), 1) // blocks % orders
    factor = jnp.transpose(factor_ref[...])
    for n in range(freqs):
        wide = jnp.dot(mixing_ref[n], spread_ref[...], preferred_element_type=jnp.float32)
        wide = jnp.where(row == column, wide, 0.0).astype(jnp.bfloat16)
        fields = jnp.dot(wide, coeff_ref[n], preferred_element_type=jnp.float32)
        scaled = fields * (factor[:, n:n + 1] * root_ref[...])
        out_ref[n // own_freqs, 0, n % own_freqs] = scaled.astype(jnp.bfloat16)


def mix(coeffs, mixing, spread, factor, root_weight, owners, orders, at, count, whole):
    _, rows, columns = coeffs.shape
    out_rows, depth = mixing.shape[1:]
    own_freqs = NFREQ // owners
    steps = 4
    freqs = NFREQ // steps
    inputs = [coeffs, mixing, spread, factor, root_weight] + ([] if whole is None else [whole])
    in_specs = [
        pl.BlockSpec((freqs, rows, columns), lambda i: (i, 0, 0)),
        pl.BlockSpec((freqs, out_rows, depth), lambda i: (i, 0, 0)),
        pl.BlockSpec(spread.shape, lambda i: (0, 0)),
        pl.BlockSpec((freqs, out_rows), lambda i: (i, 0)),
        pl.BlockSpec(root_weight.shape, lambda i: (0, 0)),
        pl.BlockSpec(memory_space=pl.ANY),
    ]
    return pl.pallas_call(
        functools.partial(mix_kernel, orders, own_freqs),
        grid=(steps,),
        in_specs=in_specs[:len(inputs)],
        out_specs=pl.BlockSpec(
            (owners // steps, 1, own_freqs, out_rows, columns), lambda i: (i, at, 0, 0, 0)
        ),
        out_shape=jax.ShapeDtypeStruct((owners, count, own_freqs, out_rows, columns), jnp.bfloat16),
        input_output_aliases={} if whole is None else {5: 0},
        compiler_params=pltpu.CompilerParams(vmem_limit_bytes=VMEM_LIMIT),
        cost_estimate=pl.CostEstimate(
            flops=2 * NFREQ * out_rows * rows * columns,
            bytes_accessed=2 * NFREQ * (rows + out_rows) * columns,
            transcendentals=0,
        ),
        name="mix",
    )(*inputs)


def pack_kernel(record_ref, out_ref):
    owners, _, _, part = out_ref.shape
    for d in range(owners):
        out_ref[d, 0] = record_ref[0, 0, :, d * part:(d + 1) * part]


def pack(by_field, k, owners):
    sec_local, _, rec_len, cells = by_field.shape
    part = cells // owners
    return pl.pallas_call(
        pack_kernel,
        grid=(sec_local,),
        in_specs=[pl.BlockSpec((1, 1, rec_len, cells), lambda i: (i, k, 0, 0))],
        out_specs=pl.BlockSpec((owners, 1, rec_len, part), lambda i: (0, i, 0, 0)),
        out_shape=jax.ShapeDtypeStruct((owners, sec_local, rec_len, part), by_field.dtype),
        compiler_params=pltpu.CompilerParams(vmem_limit_bytes=VMEM_LIMIT),
        cost_estimate=pl.CostEstimate(
            flops=0, bytes_accessed=4 * sec_local * rec_len * cells, transcendentals=0
        ),
        name="pack",
    )(by_field)


def unpack_kernel(piece_ref, *refs):
    out_ref = refs[-1]
    owners, count, part = piece_ref.shape[0], piece_ref.shape[1], piece_ref.shape[-1]
    for k in range(count):
        for d in range(owners):
            out_ref[:, 0, :, k, :, d * part:(d + 1) * part] = piece_ref[d, k, 0]


def unpack(pieces, first, fields, whole):
    owners, count, freqs, orders, two, modes, part = pieces.shape
    shape = (orders, freqs, two, fields, modes, owners * part)
    inputs = [pieces] if whole is None else [pieces, whole]
    in_specs = [
        pl.BlockSpec((owners, count, 1, orders, two, modes, part), lambda i: (0, 0, i, 0, 0, 0, 0)),
        pl.BlockSpec(memory_space=pl.ANY),
    ]
    return pl.pallas_call(
        unpack_kernel,
        grid=(freqs,),
        in_specs=in_specs[:len(inputs)],
        out_specs=pl.BlockSpec(
            (orders, 1, two, count, modes, owners * part),
            lambda i: (0, i, 0, first // count, 0, 0),
        ),
        out_shape=jax.ShapeDtypeStruct(shape, pieces.dtype),
        input_output_aliases={} if whole is None else {1: 0},
        compiler_params=pltpu.CompilerParams(vmem_limit_bytes=VMEM_LIMIT),
        cost_estimate=pl.CostEstimate(flops=0, bytes_accessed=4 * pieces.size, transcendentals=0),
        name="unpack",
    )(*inputs)


def local(records, block_start, slab_index, weight_table):
    sec_local, rec_len, fields, cell_local = records.shape
    sec_count = lax.axis_size("sector")
    tm_count = lax.axis_size("tm")
    space_count = lax.axis_size("space")
    owners = sec_count * tm_count
    owner_axes = ("sector", "tm")
    sectors = sec_local * sec_count
    orders = sectors // 2
    blocks = block_start.shape[0]
    depth = 2 * blocks
    part = cell_local // owners
    own_freqs = NFREQ // owners
    me = lax.axis_index("sector") * tm_count + lax.axis_index("tm")

    by_field = jnp.transpose(records, (0, 2, 1, 3))
    arrived = []
    for k in range(fields):
        send = pack(by_field, k, owners)
        got = lax.all_to_all(send, owner_axes, split_axis=0, concat_axis=0, tiled=True)
        arrived.append(got.reshape(sec_count, tm_count, sec_local, rec_len, part))

    time_basis = placed_time_basis(block_start, tm_count)
    half, _ = half_span(blocks // tm_count)
    halves = blocks // tm_count // half
    azimuth = jnp.einsum(
        "mcse,ij,bd->cmibsjed",
        order_table(orders, sectors),
        jnp.eye(tm_count, dtype=jnp.bfloat16),
        jnp.eye(half, dtype=jnp.bfloat16),
    ).reshape(2 * orders * tm_count * half, sectors * tm_count * 2 * half)
    place = [
        (b // half % halves * tm_count + b // (half * halves)) * half + b % half
        for b in range(blocks)
    ]
    own_slab = lax.dynamic_slice_in_dim(slab_index, me * part, part)
    weight = jnp.sum(
        jnp.where(
            own_slab[None, :] == jnp.arange(weight_table.shape[0], dtype=jnp.int32)[:, None],
            weight_table[:, None],
            0.0,
        ),
        0,
        keepdims=True,
    )

    gram = jnp.zeros((NFREQ, blocks, orders * blocks), jnp.float32)
    coeffs = []
    for k in range(fields):
        own, gram = coeffs_and_gram(arrived[k], time_basis, azimuth, weight, gram)
        coeffs.append(own)

    if own_freqs % space_count == 0:
        axes = owner_axes + ("space",)
    else:
        gram = lax.psum(gram, "space")
        axes = owner_axes
    solvers = math.prod(lax.axis_size(a) for a in axes)
    solved = NFREQ // solvers
    gram = gram.reshape((solvers, solved) + gram.shape[1:])
    gram = lax.all_to_all(gram, axes, split_axis=0, concat_axis=0, tiled=True)
    gram = jnp.sum(gram, 0).reshape(solved, blocks, orders, blocks)
    gram = jnp.transpose(gram, (3, 1, 0, 2)).reshape(blocks, blocks, solved * orders)
    basis, energy = subspace(gram, tuple(place[:MODES]), fields * cell_local * space_count)

    short = basis.astype(jnp.bfloat16).reshape(2, MODES, blocks, solved, orders)
    short = jnp.transpose(short, (3, 4, 0, 1, 2))
    short_re, short_im = short[:, :, 0], short[:, :, 1]
    mixing = jnp.stack(
        [jnp.concatenate([short_re, -short_im], -1), jnp.concatenate([short_im, short_re], -1)], 2
    ).reshape(solved, orders * 2 * MODES * depth)
    energy = jnp.transpose(energy.reshape(MODES, solved, orders), (1, 2, 0)).reshape(solved, -1)
    high = energy.astype(jnp.bfloat16)
    rest = energy - high.astype(jnp.float32)
    middle = rest.astype(jnp.bfloat16)
    low = (rest - middle.astype(jnp.float32)).astype(jnp.bfloat16)
    packet = jnp.concatenate([mixing, high, middle, low], 1)
    width = -(-packet.shape[1] // LANES) * LANES
    packet = jnp.pad(packet, ((0, 0), (0, width - packet.shape[1])))
    packet = packet.reshape(1, solved, width // LANES, LANES)
    packet = jnp.broadcast_to(packet, (solvers,) + packet.shape[1:])
    packet = lax.all_to_all(packet, axes, split_axis=0, concat_axis=0, tiled=True)
    packet = packet.reshape(NFREQ, width)
    count = orders * MODES
    mixing = packet[:, :orders * 2 * MODES * depth].reshape(NFREQ, orders * 2 * MODES, depth)
    tail = packet[:, orders * 2 * MODES * depth:].astype(jnp.float32)
    energy = (tail[:, :count] + tail[:, count:2 * count]) + tail[:, 2 * count:3 * count]
    energy = energy.reshape(NFREQ, orders, MODES)
    factor = jnp.broadcast_to(
        lax.rsqrt(energy)[:, :, None, :], (NFREQ, orders, 2, MODES)
    ).reshape(NFREQ, orders * 2 * MODES)
    root_weight = jnp.sqrt(weight)
    spread = jnp.broadcast_to(
        jnp.eye(depth, dtype=jnp.bfloat16).reshape(depth, 2, 1, blocks), (depth, 2, orders, blocks)
    ).reshape(depth, depth * orders)

    mode_fields = None
    for first, count in ((fields - 1, 1), (0, fields - 1)):
        send = None
        for n in range(count):
            send = mix(
                coeffs[first + n], mixing, spread, factor, root_weight, owners, orders, n, count, send
            )
        got = lax.all_to_all(send, owner_axes, split_axis=0, concat_axis=0, tiled=True)
        got = got.reshape(owners, count, own_freqs, orders, 2, MODES, part)
        mode_fields = unpack(got, first, fields, mode_fields)
    mode_fields = jnp.transpose(mode_fields, (0, 1, 2, 4, 3, 5))
    own_energy = lax.dynamic_slice_in_dim(energy, me * own_freqs, own_freqs)
    return (mode_fields, jnp.transpose(own_energy, (1, 0, 2)))


def solution(mesh):
    placed = (P("sector", "tm", None, "space"), P(), P("space"), P())
    return jax.shard_map(
        local,
        mesh=mesh,
        in_specs=placed,
        out_specs=(
            P(None, ("sector", "tm"), None, None, None, "space"),
            P(None, ("sector", "tm"), None),
        ),
        check_vma=False,
    )
```

```python
import functools
import math

import jax
import jax.numpy as jnp
from jax import lax
from jax.experimental import pallas as pl
from jax.experimental.pallas import tpu as pltpu
from jax.sharding import PartitionSpec as P

NFFT = 64
NFREQ = 32
MODES = 8
SUBIT = 4
LANES = 128
EPSILON = 1e-06
VMEM_LIMIT = 48 * 1024 * 1024


def time_table(length, freq_count):
    steps_t = jnp.arange(length, dtype=jnp.float32)
    freq_f = jnp.arange(freq_count, dtype=jnp.float32)
    window = 0.5 - 0.5 * jnp.cos(2.0 * math.pi * steps_t / length)
    angles = 2.0 * math.pi * freq_f[:, None] * steps_t[None, :] / length
    both = jnp.stack([window * jnp.cos(angles), -window * jnp.sin(angles)])
    return (both / math.sqrt(length)).astype(jnp.bfloat16)


def order_table(orders, sectors):
    order_m = jnp.arange(orders, dtype=jnp.float32)[:, None]
    sector_s = jnp.arange(sectors, dtype=jnp.float32)[None, :]
    angles = 2.0 * math.pi * order_m * sector_s / sectors
    cosine = jnp.cos(angles)
    sine_part = jnp.sin(angles)
    upper_row = jnp.stack([cosine, sine_part], -1)
    lower_row = jnp.stack([-sine_part, cosine], -1)
    return (jnp.stack([upper_row, lower_row], 1) / math.sqrt(sectors)).astype(jnp.bfloat16)


def half_span(blocks):
    half = blocks // 2
    return half, (half - 1) * (NFFT // 2) + NFFT // 8 + NFFT


def placed_time_basis(block_start, tm_count):
    blocks = block_start.shape[0] // tm_count
    half, span = half_span(blocks)
    basis = time_table(NFFT, NFREQ)
    first = jnp.arange(blocks, dtype=jnp.int32) // half * (half * (NFFT // 2))
    inside = block_start.reshape(tm_count, blocks) - first[None, :]
    place = (
        inside[:, :, None, None] + jnp.arange(NFFT, dtype=jnp.int32)[:, None]
        == jnp.arange(span, dtype=jnp.int32)[None, :]
    ).astype(jnp.bfloat16)
    table = jnp.einsum(
        "eft,jhbtu->jhfebu",
        basis,
        place.reshape(tm_count, 2, half, NFFT, span),
        preferred_element_type=jnp.float32,
    ).astype(jnp.bfloat16)
    return table.reshape(tm_count, 2, NFREQ * 2 * half, span)


def coeff_kernel(sec_count, sec_local, freqs, orders, place_ref, time_ref, azimuth_ref, weight_ref,
                 before_ref, *refs):
    record_refs, (coeff_ref, gram_ref, spectra) = refs[:-3], refs[-3:]
    step = pl.program_id(0)
    tm_count, halves, _, span = time_ref.shape
    rec_len, columns = record_refs[0].shape[1:]
    sectors = spectra.shape[0]
    rows = spectra.shape[2] // NFREQ

    @pl.when(step < sec_local)
    def _():
        for shift in range(sec_count):
            source = lax.rem(place_ref[0] + sec_count - shift, sec_count)
            own = record_refs[shift * tm_count:(shift + 1) * tm_count]
            for h in range(halves):
                first = h * (rec_len - span) // (halves - 1)
                pieces = [ref[0, first:first + span] for ref in own]
                parts = []
                for j in range(tm_count):
                    piece = pieces[0]
                    for n in range(1, tm_count):
                        here = lax.rem(place_ref[1] + tm_count - n, tm_count) == j
                        piece = jnp.where(here, pieces[n], piece)
                    part = jnp.dot(time_ref[j, h], piece, preferred_element_type=jnp.float32)
                    parts.append(part.reshape(NFREQ, rows // tm_count, columns))
                joined = jnp.stack(parts, 1).reshape(NFREQ * rows, columns)
                spectra[source * sec_local + step, h] = joined.astype(jnp.bfloat16)

    @pl.when(step >= sec_local)
    def _():
        half_rows = azimuth_ref.shape[0]
        depth = half_rows // (2 * orders)
        blocks = depth * halves
        wide = orders * blocks
        row = lax.broadcasted_iota(jnp.int32, (wide, wide), 0) % blocks
        column = lax.broadcasted_iota(jnp.int32, (wide, wide), 1) % blocks
        owner = lax.broadcasted_iota(jnp.int32, (blocks, wide), 1) // blocks
        for n in range(freqs):
            at = pl.multiple_of(((step - sec_local) * freqs + n) * rows, rows)
            parts = [
                jnp.dot(
                    azimuth_ref[...],
                    spectra[:, h, pl.ds(at, rows), :].reshape(sectors * rows, columns),
                    preferred_element_type=jnp.float32,
                ).reshape(2 * orders, depth, columns)
                for h in range(halves)
            ]
            coeffs = jnp.stack(parts, 1).reshape(2 * wide, columns).astype(jnp.bfloat16)
            coeff_ref[n] = coeffs
            weighted = (coeffs.astype(jnp.float32) * weight_ref[...]).astype(jnp.bfloat16)
            swapped = jnp.concatenate([coeffs[wide:], coeffs[:wide]], 0)
            across = (((1,), (1,)), ((), ()))
            upper = lax.dot_general(
                weighted[:wide], coeffs, across, preferred_element_type=jnp.float32
            )
            lower = lax.dot_general(
                weighted[wide:], swapped, across, preferred_element_type=jnp.float32
            )
            real = upper[:, :wide] + lower[:, :wide]
            imag = upper[:, wide:] - lower[:, wide:]
            packed = jnp.where(row <= column, real, imag)
            own = packed[:blocks]
            for m in range(1, orders):
                own = jnp.where(owner == m, packed[m * blocks:(m + 1) * blocks], own)
            gram_ref[n] = before_ref[n] + own


def coeffs_and_gram(place, arrived, sec_count, time_basis, azimuth, weight, before):
    sec_local, rec_len, columns = arrived[0].shape
    sectors = sec_count * sec_local
    halves = time_basis.shape[1]
    blocks, wide = before.shape[1:]
    rows = azimuth.shape[1] // sectors
    steps = 4
    freqs = NFREQ // steps
    later = lambda i: jnp.maximum(i - sec_local, 0)
    early = lambda i: jnp.minimum(i, sec_local - 1)
    flops = 2 * columns * (
        sectors * time_basis.size + NFREQ * halves * azimuth.size + NFREQ * 4 * wide * wide
    )
    piece = pl.BlockSpec((1, rec_len, columns), lambda i, _: (early(i), 0, 0))
    return pl.pallas_call(
        functools.partial(coeff_kernel, sec_count, sec_local, freqs, wide // blocks),
        grid_spec=pltpu.PrefetchScalarGridSpec(
            num_scalar_prefetch=1,
            grid=(sec_local + steps,),
            in_specs=[
                pl.BlockSpec(time_basis.shape, lambda i, _: (0, 0, 0, 0)),
                pl.BlockSpec(azimuth.shape, lambda i, _: (0, 0)),
                pl.BlockSpec(weight.shape, lambda i, _: (0, 0)),
                pl.BlockSpec((freqs, blocks, wide), lambda i, _: (later(i), 0, 0)),
            ] + [piece] * len(arrived),
            out_specs=[
                pl.BlockSpec((freqs, 2 * wide, columns), lambda i, _: (later(i), 0, 0)),
                pl.BlockSpec((freqs, blocks, wide), lambda i, _: (later(i), 0, 0)),
            ],
            scratch_shapes=[pltpu.VMEM((sectors, halves, NFREQ * rows, columns), jnp.bfloat16)],
        ),
        out_shape=[
            jax.ShapeDtypeStruct((NFREQ, 2 * wide, columns), jnp.bfloat16),
            jax.ShapeDtypeStruct(before.shape, jnp.float32),
        ],
        compiler_params=pltpu.CompilerParams(vmem_limit_bytes=VMEM_LIMIT),
        cost_estimate=pl.CostEstimate(
            flops=flops,
            bytes_accessed=2 * (len(arrived) * arrived[0].size + NFREQ * 2 * wide * columns),
            transcendentals=0,
        ),
        name="coeffs_and_gram",
    )(place, time_basis, azimuth, weight, before, *arrived)


def subspace_kernel(cell_total, first, packed_ref, basis_ref, energy_ref):
    size, _, pairs = packed_ref.shape
    row = lax.broadcasted_iota(jnp.int32, (size, pairs), 0)
    column_re, column_im = [], []
    for q in range(size):
        down, along = packed_ref[q], packed_ref[:, q, :]
        column_re.append(jnp.where(row <= q, down, along))
        column_im.append(jnp.where(row > q, down, jnp.where(row == q, 0.0, -along)))

    def image_of(vec_re, vec_im):
        out_re, out_im = [], []
        for j in range(MODES):
            sum_re = jnp.zeros_like(column_re[0])
            sum_im = jnp.zeros_like(column_re[0])
            for q in range(size):
                at_re, at_im = vec_re[j][q:q + 1], vec_im[j][q:q + 1]
                sum_re += column_re[q] * at_re - column_im[q] * at_im
                sum_im += column_re[q] * at_im + column_im[q] * at_re
            out_re.append(sum_re)
            out_im.append(sum_im)
        return out_re, out_im

    total = lambda x: jnp.sum(x, 0, keepdims=True)
    vec_re = [column_re[q] for q in first]
    vec_im = [column_im[q] for q in first]
    for sweep in range(SUBIT):
        if sweep > 0:
            vec_re, vec_im = image_of(vec_re, vec_im)
        vec_re, vec_im = list(vec_re), list(vec_im)
        for i in range(MODES):
            scale = 1.0 / jnp.sqrt(total(vec_re[i] * vec_re[i] + vec_im[i] * vec_im[i]) + EPSILON)
            own_re, own_im = vec_re[i] * scale, vec_im[i] * scale
            vec_re[i], vec_im[i] = own_re, own_im
            for j in range(i + 1, MODES):
                proj_re = total(own_re * vec_re[j] + own_im * vec_im[j])
                proj_im = total(own_re * vec_im[j] - own_im * vec_re[j])
                vec_re[j] = vec_re[j] - (proj_re * own_re - proj_im * own_im)
                vec_im[j] = vec_im[j] - (proj_re * own_im + proj_im * own_re)
    image_re, image_im = image_of(vec_re, vec_im)
    for j in range(MODES):
        basis_ref[0, j] = vec_re[j]
        basis_ref[1, j] = vec_im[j]
        energy_ref[j:j + 1] = total(vec_re[j] * image_re[j] + vec_im[j] * image_im[j]) / cell_total


def subspace(packed, first, cell_total):
    size, _, pairs = packed.shape
    return pl.pallas_call(
        functools.partial(subspace_kernel, float(cell_total), first),
        out_shape=[
            jax.ShapeDtypeStruct((2, MODES, size, pairs), jnp.float32),
            jax.ShapeDtypeStruct((MODES, pairs), jnp.float32),
        ],
        name="subspace",
    )(packed)


def mix_kernel(orders, own_freqs, coeff_ref, mixing_ref, spread_ref, factor_ref, root_ref, *refs):
    out_ref = refs[-1]
    freqs, rows, _ = mixing_ref.shape
    total = spread_ref.shape[1]
    blocks = total // (2 * orders)
    row = lax.broadcasted_iota(jnp.int32, (rows, total), 0) // (rows // orders)
    column = lax.broadcasted_iota(jnp.int32, (rows, total), 1) // blocks % orders
    factor = jnp.transpose(factor_ref[...])
    for n in range(freqs):
        wide = jnp.dot(mixing_ref[n], spread_ref[...], preferred_element_type=jnp.float32)
        wide = jnp.where(row == column, wide, 0.0).astype(jnp.bfloat16)
        fields = jnp.dot(wide, coeff_ref[n], preferred_element_type=jnp.float32)
        scaled = fields * (factor[:, n:n + 1] * root_ref[...])
        out_ref[n // own_freqs, 0, n % own_freqs] = scaled.astype(jnp.bfloat16)


def mix(coeffs, mixing, spread, factor, root_weight, owners, orders, at, count, whole):
    _, rows, columns = coeffs.shape
    out_rows, depth = mixing.shape[1:]
    own_freqs = NFREQ // owners
    steps = 4
    freqs = NFREQ // steps
    inputs = [coeffs, mixing, spread, factor, root_weight] + ([] if whole is None else [whole])
    in_specs = [
        pl.BlockSpec((freqs, rows, columns), lambda i: (i, 0, 0)),
        pl.BlockSpec((freqs, out_rows, depth), lambda i: (i, 0, 0)),
        pl.BlockSpec(spread.shape, lambda i: (0, 0)),
        pl.BlockSpec((freqs, out_rows), lambda i: (i, 0)),
        pl.BlockSpec(root_weight.shape, lambda i: (0, 0)),
        pl.BlockSpec(memory_space=pl.ANY),
    ]
    return pl.pallas_call(
        functools.partial(mix_kernel, orders, own_freqs),
        grid=(steps,),
        in_specs=in_specs[:len(inputs)],
        out_specs=pl.BlockSpec(
            (owners // steps, 1, own_freqs, out_rows, columns), lambda i: (i, at, 0, 0, 0)
        ),
        out_shape=jax.ShapeDtypeStruct((owners, count, own_freqs, out_rows, columns), jnp.bfloat16),
        input_output_aliases={} if whole is None else {5: 0},
        compiler_params=pltpu.CompilerParams(vmem_limit_bytes=VMEM_LIMIT),
        cost_estimate=pl.CostEstimate(
            flops=2 * NFREQ * out_rows * rows * columns,
            bytes_accessed=2 * NFREQ * (rows + out_rows) * columns,
            transcendentals=0,
        ),
        name="mix",
    )(*inputs)


def take_kernel(place_ref, record_ref, out_ref):
    out_ref[...] = record_ref[:, 0]


def take(by_field, k, owner, owners):
    sec_local, _, rec_len, cells = by_field.shape
    part = cells // owners
    if part % LANES:
        return lax.dynamic_slice_in_dim(by_field[:, k], owner * part, part, 2)
    return pl.pallas_call(
        take_kernel,
        grid_spec=pltpu.PrefetchScalarGridSpec(
            num_scalar_prefetch=1,
            grid=(1,),
            in_specs=[
                pl.BlockSpec((sec_local, 1, rec_len, part), lambda i, at: (0, k, 0, at[0]))
            ],
            out_specs=pl.BlockSpec((sec_local, rec_len, part), lambda i, at: (0, 0, 0)),
        ),
        out_shape=jax.ShapeDtypeStruct((sec_local, rec_len, part), by_field.dtype),
        compiler_params=pltpu.CompilerParams(vmem_limit_bytes=VMEM_LIMIT),
        cost_estimate=pl.CostEstimate(
            flops=0, bytes_accessed=4 * sec_local * rec_len * part, transcendentals=0
        ),
        name="take",
    )(jnp.reshape(owner, (1,)), by_field)


def unpack_kernel(piece_ref, *refs):
    out_ref = refs[-1]
    owners, count, part = piece_ref.shape[0], piece_ref.shape[1], piece_ref.shape[-1]
    for k in range(count):
        for d in range(owners):
            out_ref[:, 0, :, k, :, d * part:(d + 1) * part] = piece_ref[d, k, 0]


def unpack(pieces, first, fields, whole):
    owners, count, freqs, orders, two, modes, part = pieces.shape
    shape = (orders, freqs, two, fields, modes, owners * part)
    inputs = [pieces] if whole is None else [pieces, whole]
    in_specs = [
        pl.BlockSpec((owners, count, 1, orders, two, modes, part), lambda i: (0, 0, i, 0, 0, 0, 0)),
        pl.BlockSpec(memory_space=pl.ANY),
    ]
    return pl.pallas_call(
        unpack_kernel,
        grid=(freqs,),
        in_specs=in_specs[:len(inputs)],
        out_specs=pl.BlockSpec(
            (orders, 1, two, count, modes, owners * part),
            lambda i: (0, i, 0, first // count, 0, 0),
        ),
        out_shape=jax.ShapeDtypeStruct(shape, pieces.dtype),
        input_output_aliases={} if whole is None else {1: 0},
        compiler_params=pltpu.CompilerParams(vmem_limit_bytes=VMEM_LIMIT),
        cost_estimate=pl.CostEstimate(flops=0, bytes_accessed=4 * pieces.size, transcendentals=0),
        name="unpack",
    )(*inputs)


def local(records, block_start, slab_index, weight_table):
    sec_local, rec_len, fields, cell_local = records.shape
    sec_count = lax.axis_size("sector")
    tm_count = lax.axis_size("tm")
    space_count = lax.axis_size("space")
    owners = sec_count * tm_count
    owner_axes = ("sector", "tm")
    sectors = sec_local * sec_count
    orders = sectors // 2
    blocks = block_start.shape[0]
    depth = 2 * blocks
    part = cell_local // owners
    own_freqs = NFREQ // owners
    me = lax.axis_index("sector") * tm_count + lax.axis_index("tm")

    by_field = jnp.transpose(records, (0, 2, 1, 3))
    sec_at, tm_at = lax.axis_index("sector"), lax.axis_index("tm")
    shifts = [(z, x) for z in range(sec_count) for x in range(tm_count)]
    in_order = sorted(shifts, key=lambda r: (r[0] == 0, abs(2 * r[0] - sec_count), r))
    arrived = []
    for k in range(fields):
        got = {}
        for z, x in in_order:
            owner = (sec_at + z) % sec_count * tm_count + (tm_at + x) % tm_count
            piece = take(by_field, k, owner, owners)
            if (z, x) != (0, 0):
                hops = [
                    (a * tm_count + j, (a + z) % sec_count * tm_count + (j + x) % tm_count)
                    for a in range(sec_count)
                    for j in range(tm_count)
                ]
                piece = lax.ppermute(piece, owner_axes, hops)
            got[z, x] = piece
        arrived.append([got[r] for r in shifts])

    time_basis = placed_time_basis(block_start, tm_count)
    half, _ = half_span(blocks // tm_count)
    halves = blocks // tm_count // half
    azimuth = jnp.einsum(
        "mcse,ij,bd->cmibsjed",
        order_table(orders, sectors),
        jnp.eye(tm_count, dtype=jnp.bfloat16),
        jnp.eye(half, dtype=jnp.bfloat16),
    ).reshape(2 * orders * tm_count * half, sectors * tm_count * 2 * half)
    place = [
        (b // half % halves * tm_count + b // (half * halves)) * half + b % half
        for b in range(blocks)
    ]
    own_slab = lax.dynamic_slice_in_dim(slab_index, me * part, part)
    weight = jnp.sum(
        jnp.where(
            own_slab[None, :] == jnp.arange(weight_table.shape[0], dtype=jnp.int32)[:, None],
            weight_table[:, None],
            0.0,
        ),
        0,
        keepdims=True,
    )

    gram = jnp.zeros((NFREQ, blocks, orders * blocks), jnp.float32)
    coeffs = []
    for k in range(fields):
        own, gram = coeffs_and_gram(
            jnp.stack([sec_at, tm_at]), arrived[k], sec_count, time_basis, azimuth, weight, gram
        )
        coeffs.append(own)

    if own_freqs % space_count == 0:
        axes = owner_axes + ("space",)
    else:
        gram = lax.psum(gram, "space")
        axes = owner_axes
    solvers = math.prod(lax.axis_size(a) for a in axes)
    solved = NFREQ // solvers
    gram = gram.reshape((solvers, solved) + gram.shape[1:])
    gram = lax.all_to_all(gram, axes, split_axis=0, concat_axis=0, tiled=True)
    gram = jnp.sum(gram, 0).reshape(solved, blocks, orders, blocks)
    gram = jnp.transpose(gram, (3, 1, 0, 2)).reshape(blocks, blocks, solved * orders)
    basis, energy = subspace(gram, tuple(place[:MODES]), fields * cell_local * space_count)

    short = basis.astype(jnp.bfloat16).reshape(2, MODES, blocks, solved, orders)
    short = jnp.transpose(short, (3, 4, 0, 1, 2))
    short_re, short_im = short[:, :, 0], short[:, :, 1]
    mixing = jnp.stack(
        [jnp.concatenate([short_re, -short_im], -1), jnp.concatenate([short_im, short_re], -1)], 2
    ).reshape(solved, orders * 2 * MODES * depth)
    energy = jnp.transpose(energy.reshape(MODES, solved, orders), (1, 2, 0)).reshape(solved, -1)
    high = energy.astype(jnp.bfloat16)
    rest = energy - high.astype(jnp.float32)
    middle = rest.astype(jnp.bfloat16)
    low = (rest - middle.astype(jnp.float32)).astype(jnp.bfloat16)
    packet = jnp.concatenate([mixing, high, middle, low], 1)
    width = -(-packet.shape[1] // LANES) * LANES
    packet = jnp.pad(packet, ((0, 0), (0, width - packet.shape[1])))
    packet = packet.reshape(1, solved, width // LANES, LANES)
    packet = jnp.broadcast_to(packet, (solvers,) + packet.shape[1:])
    packet = lax.all_to_all(packet, axes, split_axis=0, concat_axis=0, tiled=True)
    packet = packet.reshape(NFREQ, width)
    count = orders * MODES
    mixing = packet[:, :orders * 2 * MODES * depth].reshape(NFREQ, orders * 2 * MODES, depth)
    tail = packet[:, orders * 2 * MODES * depth:].astype(jnp.float32)
    energy = (tail[:, :count] + tail[:, count:2 * count]) + tail[:, 2 * count:3 * count]
    energy = energy.reshape(NFREQ, orders, MODES)
    factor = jnp.broadcast_to(
        lax.rsqrt(energy)[:, :, None, :], (NFREQ, orders, 2, MODES)
    ).reshape(NFREQ, orders * 2 * MODES)
    root_weight = jnp.sqrt(weight)
    spread = jnp.broadcast_to(
        jnp.eye(depth, dtype=jnp.bfloat16).reshape(depth, 2, 1, blocks), (depth, 2, orders, blocks)
    ).reshape(depth, depth * orders)

    mode_fields = None
    for first, count in ((fields - 1, 1), (0, fields - 1)):
        send = None
        for n in range(count):
            send = mix(
                coeffs[first + n], mixing, spread, factor, root_weight, owners, orders, n, count, send
            )
        got = lax.all_to_all(send, owner_axes, split_axis=0, concat_axis=0, tiled=True)
        got = got.reshape(owners, count, own_freqs, orders, 2, MODES, part)
        mode_fields = unpack(got, first, fields, mode_fields)
    mode_fields = jnp.transpose(mode_fields, (0, 1, 2, 4, 3, 5))
    own_energy = lax.dynamic_slice_in_dim(energy, me * own_freqs, own_freqs)
    return (mode_fields, jnp.transpose(own_energy, (1, 0, 2)))


def solution(mesh):
    placed = (P("sector", "tm", None, "space"), P(), P("space"), P())
    return jax.shard_map(
        local,
        mesh=mesh,
        in_specs=placed,
        out_specs=(
            P(None, ("sector", "tm"), None, None, None, "space"),
            P(None, ("sector", "tm"), None),
        ),
        check_vma=False,
    )
```

```python
import functools
import math

import jax
import jax.numpy as jnp
from jax import lax
from jax.experimental import pallas as pl
from jax.experimental.pallas import tpu as pltpu
from jax.sharding import PartitionSpec as P

NFFT = 64
NFREQ = 32
MODES = 8
SUBIT = 4
LANES = 128
EPSILON = 1e-06
VMEM_LIMIT = 48 * 1024 * 1024


def time_table(length, freq_count):
    steps_t = jnp.arange(length, dtype=jnp.float32)
    freq_f = jnp.arange(freq_count, dtype=jnp.float32)
    window = 0.5 - 0.5 * jnp.cos(2.0 * math.pi * steps_t / length)
    angles = 2.0 * math.pi * freq_f[:, None] * steps_t[None, :] / length
    both = jnp.stack([window * jnp.cos(angles), -window * jnp.sin(angles)])
    return (both / math.sqrt(length)).astype(jnp.bfloat16)


def order_table(orders, sectors):
    order_m = jnp.arange(orders, dtype=jnp.float32)[:, None]
    sector_s = jnp.arange(sectors, dtype=jnp.float32)[None, :]
    angles = 2.0 * math.pi * order_m * sector_s / sectors
    cosine = jnp.cos(angles)
    sine_part = jnp.sin(angles)
    upper_row = jnp.stack([cosine, sine_part], -1)
    lower_row = jnp.stack([-sine_part, cosine], -1)
    return (jnp.stack([upper_row, lower_row], 1) / math.sqrt(sectors)).astype(jnp.bfloat16)


def half_span(blocks):
    half = blocks // 2
    return half, (half - 1) * (NFFT // 2) + NFFT // 8 + NFFT


def placed_time_basis(block_start, tm_count):
    blocks = block_start.shape[0] // tm_count
    half, span = half_span(blocks)
    basis = time_table(NFFT, NFREQ)
    first = jnp.arange(blocks, dtype=jnp.int32) // half * (half * (NFFT // 2))
    inside = block_start.reshape(tm_count, blocks) - first[None, :]
    place = (
        inside[:, :, None, None] + jnp.arange(NFFT, dtype=jnp.int32)[:, None]
        == jnp.arange(span, dtype=jnp.int32)[None, :]
    ).astype(jnp.bfloat16)
    table = jnp.einsum(
        "eft,jhbtu->jhfebu",
        basis,
        place.reshape(tm_count, 2, half, NFFT, span),
        preferred_element_type=jnp.float32,
    ).astype(jnp.bfloat16)
    return table.reshape(tm_count, 2, NFREQ * 2 * half, span)


def coeff_kernel(sec_count, sec_local, freqs, orders, place_ref, time_ref, azimuth_ref, weight_ref,
                 before_ref, *refs):
    record_refs, (coeff_ref, gram_ref, spectra) = refs[:-3], refs[-3:]
    step = pl.program_id(0)
    tm_count, halves, _, span = time_ref.shape
    rec_len, columns = record_refs[0].shape[1:]
    sectors = spectra.shape[0]
    rows = spectra.shape[2] // NFREQ

    @pl.when(step < sec_local)
    def _():
        for shift in range(sec_count):
            source = lax.rem(place_ref[0] + sec_count - shift, sec_count)
            own = record_refs[shift * tm_count:(shift + 1) * tm_count]
            for h in range(halves):
                first = h * (rec_len - span) // (halves - 1)
                pieces = [ref[0, first:first + span] for ref in own]
                parts = []
                for j in range(tm_count):
                    piece = pieces[0]
                    for n in range(1, tm_count):
                        here = lax.rem(place_ref[1] + tm_count - n, tm_count) == j
                        piece = jnp.where(here, pieces[n], piece)
                    part = jnp.dot(time_ref[j, h], piece, preferred_element_type=jnp.float32)
                    parts.append(part.reshape(NFREQ, rows // tm_count, columns))
                joined = jnp.stack(parts, 1).reshape(NFREQ * rows, columns)
                spectra[source * sec_local + step, h] = joined.astype(jnp.bfloat16)

    @pl.when(step >= sec_local)
    def _():
        half_rows = azimuth_ref.shape[0]
        depth = half_rows // (2 * orders)
        blocks = depth * halves
        wide = orders * blocks
        row = lax.broadcasted_iota(jnp.int32, (wide, wide), 0) % blocks
        column = lax.broadcasted_iota(jnp.int32, (wide, wide), 1) % blocks
        owner = lax.broadcasted_iota(jnp.int32, (blocks, wide), 1) // blocks
        for n in range(freqs):
            at = pl.multiple_of(((step - sec_local) * freqs + n) * rows, rows)
            parts = [
                jnp.dot(
                    azimuth_ref[...],
                    spectra[:, h, pl.ds(at, rows), :].reshape(sectors * rows, columns),
                    preferred_element_type=jnp.float32,
                ).reshape(2 * orders, depth, columns)
                for h in range(halves)
            ]
            coeffs = jnp.stack(parts, 1).reshape(2 * wide, columns).astype(jnp.bfloat16)
            coeff_ref[n] = coeffs
            weighted = (coeffs.astype(jnp.float32) * weight_ref[...]).astype(jnp.bfloat16)
            swapped = jnp.concatenate([coeffs[wide:], coeffs[:wide]], 0)
            across = (((1,), (1,)), ((), ()))
            upper = lax.dot_general(
                weighted[:wide], coeffs, across, preferred_element_type=jnp.float32
            )
            lower = lax.dot_general(
                weighted[wide:], swapped, across, preferred_element_type=jnp.float32
            )
            real = upper[:, :wide] + lower[:, :wide]
            imag = upper[:, wide:] - lower[:, wide:]
            packed = jnp.where(row <= column, real, imag)
            own = packed[:blocks]
            for m in range(1, orders):
                own = jnp.where(owner == m, packed[m * blocks:(m + 1) * blocks], own)
            gram_ref[n] = before_ref[n] + own


def coeffs_and_gram(place, arrived, sec_count, time_basis, azimuth, weight, before):
    sec_local, rec_len, columns = arrived[0].shape
    sectors = sec_count * sec_local
    halves = time_basis.shape[1]
    blocks, wide = before.shape[1:]
    rows = azimuth.shape[1] // sectors
    steps = 4
    freqs = NFREQ // steps
    later = lambda i: jnp.maximum(i - sec_local, 0)
    early = lambda i: jnp.minimum(i, sec_local - 1)
    flops = 2 * columns * (
        sectors * time_basis.size + NFREQ * halves * azimuth.size + NFREQ * 4 * wide * wide
    )
    piece = pl.BlockSpec((1, rec_len, columns), lambda i, _: (early(i), 0, 0))
    return pl.pallas_call(
        functools.partial(coeff_kernel, sec_count, sec_local, freqs, wide // blocks),
        grid_spec=pltpu.PrefetchScalarGridSpec(
            num_scalar_prefetch=1,
            grid=(sec_local + steps,),
            in_specs=[
                pl.BlockSpec(time_basis.shape, lambda i, _: (0, 0, 0, 0)),
                pl.BlockSpec(azimuth.shape, lambda i, _: (0, 0)),
                pl.BlockSpec(weight.shape, lambda i, _: (0, 0)),
                pl.BlockSpec((freqs, blocks, wide), lambda i, _: (later(i), 0, 0)),
            ] + [piece] * len(arrived),
            out_specs=[
                pl.BlockSpec((freqs, 2 * wide, columns), lambda i, _: (later(i), 0, 0)),
                pl.BlockSpec((freqs, blocks, wide), lambda i, _: (later(i), 0, 0)),
            ],
            scratch_shapes=[pltpu.VMEM((sectors, halves, NFREQ * rows, columns), jnp.bfloat16)],
        ),
        out_shape=[
            jax.ShapeDtypeStruct((NFREQ, 2 * wide, columns), jnp.bfloat16),
            jax.ShapeDtypeStruct(before.shape, jnp.float32),
        ],
        compiler_params=pltpu.CompilerParams(vmem_limit_bytes=VMEM_LIMIT),
        cost_estimate=pl.CostEstimate(
            flops=flops,
            bytes_accessed=2 * (len(arrived) * arrived[0].size + NFREQ * 2 * wide * columns),
            transcendentals=0,
        ),
        name="coeffs_and_gram",
    )(place, time_basis, azimuth, weight, before, *arrived)


def subspace_kernel(cell_total, first, packed_ref, basis_ref, energy_ref):
    size, _, pairs = packed_ref.shape
    row = lax.broadcasted_iota(jnp.int32, (size, pairs), 0)
    column_re, column_im = [], []
    for q in range(size):
        down, along = packed_ref[q], packed_ref[:, q, :]
        column_re.append(jnp.where(row <= q, down, along))
        column_im.append(jnp.where(row > q, down, jnp.where(row == q, 0.0, -along)))

    def image_of(vec_re, vec_im):
        out_re, out_im = [], []
        for j in range(MODES):
            sum_re = jnp.zeros_like(column_re[0])
            sum_im = jnp.zeros_like(column_re[0])
            for q in range(size):
                at_re, at_im = vec_re[j][q:q + 1], vec_im[j][q:q + 1]
                sum_re += column_re[q] * at_re - column_im[q] * at_im
                sum_im += column_re[q] * at_im + column_im[q] * at_re
            out_re.append(sum_re)
            out_im.append(sum_im)
        return out_re, out_im

    total = lambda x: jnp.sum(x, 0, keepdims=True)
    vec_re = [column_re[q] for q in first]
    vec_im = [column_im[q] for q in first]
    for sweep in range(SUBIT):
        if sweep > 0:
            vec_re, vec_im = image_of(vec_re, vec_im)
        vec_re, vec_im = list(vec_re), list(vec_im)
        for i in range(MODES):
            scale = 1.0 / jnp.sqrt(total(vec_re[i] * vec_re[i] + vec_im[i] * vec_im[i]) + EPSILON)
            own_re, own_im = vec_re[i] * scale, vec_im[i] * scale
            vec_re[i], vec_im[i] = own_re, own_im
            for j in range(i + 1, MODES):
                proj_re = total(own_re * vec_re[j] + own_im * vec_im[j])
                proj_im = total(own_re * vec_im[j] - own_im * vec_re[j])
                vec_re[j] = vec_re[j] - (proj_re * own_re - proj_im * own_im)
                vec_im[j] = vec_im[j] - (proj_re * own_im + proj_im * own_re)
    image_re, image_im = image_of(vec_re, vec_im)
    for j in range(MODES):
        basis_ref[0, j] = vec_re[j]
        basis_ref[1, j] = vec_im[j]
        energy_ref[j:j + 1] = total(vec_re[j] * image_re[j] + vec_im[j] * image_im[j]) / cell_total


def subspace(packed, first, cell_total):
    size, _, pairs = packed.shape
    return pl.pallas_call(
        functools.partial(subspace_kernel, float(cell_total), first),
        out_shape=[
            jax.ShapeDtypeStruct((2, MODES, size, pairs), jnp.float32),
            jax.ShapeDtypeStruct((MODES, pairs), jnp.float32),
        ],
        name="subspace",
    )(packed)


def mix_kernel(orders, parts, owner_ref, mixing_ref, spread_ref, factor_ref, root_ref, *refs):
    coeff_refs, out_ref = refs[:-1], refs[-1]
    freqs, rows, _ = mixing_ref.shape
    total = spread_ref.shape[1]
    blocks = total // (2 * orders)
    row = lax.broadcasted_iota(jnp.int32, (rows, total), 0) // (rows // orders)
    column = lax.broadcasted_iota(jnp.int32, (rows, total), 1) // blocks % orders
    factor = jnp.transpose(factor_ref[0])
    for n in range(freqs):
        wide = jnp.dot(mixing_ref[n], spread_ref[...], preferred_element_type=jnp.float32)
        wide = jnp.where(row == column, wide, 0.0).astype(jnp.bfloat16)
        for (k, low, high), coeff_ref in zip(parts, coeff_refs):
            fields = jnp.dot(wide, coeff_ref[n], preferred_element_type=jnp.float32)
            scaled = fields * (factor[:, n:n + 1] * root_ref[:, low:high])
            out_ref[k, n, :, low:high] = scaled.astype(jnp.bfloat16)


def mix(owner, coeffs, parts, mixing, spread, factor, root_weight, owners, orders, fields):
    rows = coeffs[0].shape[1]
    out_rows, depth = mixing.shape[1:]
    columns = root_weight.shape[1]
    freqs = NFREQ // owners
    return pl.pallas_call(
        functools.partial(mix_kernel, orders, parts),
        grid_spec=pltpu.PrefetchScalarGridSpec(
            num_scalar_prefetch=1,
            grid=(1,),
            in_specs=[
                pl.BlockSpec((freqs, out_rows, depth), lambda i, at: (at[0], 0, 0)),
                pl.BlockSpec(spread.shape, lambda i, at: (0, 0)),
                pl.BlockSpec((1, freqs, out_rows), lambda i, at: (at[0], 0, 0)),
                pl.BlockSpec(root_weight.shape, lambda i, at: (0, 0)),
            ] + [
                pl.BlockSpec((freqs, rows, x.shape[2]), lambda i, at: (at[0], 0, 0)) for x in coeffs
            ],
            out_specs=pl.BlockSpec((fields, freqs, out_rows, columns), lambda i, at: (0, 0, 0, 0)),
        ),
        out_shape=jax.ShapeDtypeStruct((fields, freqs, out_rows, columns), jnp.bfloat16),
        compiler_params=pltpu.CompilerParams(vmem_limit_bytes=VMEM_LIMIT),
        cost_estimate=pl.CostEstimate(
            flops=2 * freqs * out_rows * rows * fields * columns,
            bytes_accessed=2 * freqs * (rows + out_rows) * fields * columns,
            transcendentals=0,
        ),
        name="mix",
    )(jnp.reshape(owner, (1,)), mixing, spread, factor, root_weight, *coeffs)


def take_kernel(place_ref, record_ref, out_ref):
    out_ref[...] = record_ref[:, 0]


def take(by_field, owner, owners, part):
    sec_local, _, rec_len, cells = by_field.shape
    k, low, high = part
    count = high - low
    own = cells // owners
    if count % LANES:
        return lax.dynamic_slice_in_dim(by_field[:, k], owner * own + low, count, 2)
    return pl.pallas_call(
        take_kernel,
        grid_spec=pltpu.PrefetchScalarGridSpec(
            num_scalar_prefetch=1,
            grid=(1,),
            in_specs=[
                pl.BlockSpec((sec_local, 1, rec_len, count), lambda i, at: (0, k, 0, at[0]))
            ],
            out_specs=pl.BlockSpec((sec_local, rec_len, count), lambda i, at: (0, 0, 0)),
        ),
        out_shape=jax.ShapeDtypeStruct((sec_local, rec_len, count), by_field.dtype),
        compiler_params=pltpu.CompilerParams(vmem_limit_bytes=VMEM_LIMIT),
        cost_estimate=pl.CostEstimate(
            flops=0, bytes_accessed=4 * sec_local * rec_len * count, transcendentals=0
        ),
        name="take",
    )(jnp.reshape(owner * (own // count) + low // count, (1,)), by_field)


def unpack_kernel(owner_ref, piece_ref, *refs):
    out_ref = refs[-1]
    for k in range(piece_ref.shape[0]):
        for f in range(piece_ref.shape[1]):
            out_ref[:, f, :, k] = piece_ref[k, f]


def unpack(owner, piece, owners, whole):
    fields, freqs, orders, two, modes, part = piece.shape
    shape = (orders, freqs, two, fields, modes, owners * part)
    if part % LANES:
        whole = jnp.zeros(shape, piece.dtype) if whole is None else whole
        piece = jnp.transpose(piece, (2, 1, 3, 0, 4, 5))
        return lax.dynamic_update_slice_in_dim(whole, piece, owner * part, 5)
    inputs = [piece] if whole is None else [piece, whole]
    in_specs = [
        pl.BlockSpec(piece.shape, lambda i, at: (0, 0, 0, 0, 0, 0)),
        pl.BlockSpec(memory_space=pl.ANY),
    ]
    return pl.pallas_call(
        unpack_kernel,
        grid_spec=pltpu.PrefetchScalarGridSpec(
            num_scalar_prefetch=1,
            grid=(1,),
            in_specs=in_specs[:len(inputs)],
            out_specs=pl.BlockSpec(shape[:5] + (part,), lambda i, at: (0, 0, 0, 0, 0, at[0])),
        ),
        out_shape=jax.ShapeDtypeStruct(shape, piece.dtype),
        input_output_aliases={} if whole is None else {2: 0},
        compiler_params=pltpu.CompilerParams(vmem_limit_bytes=VMEM_LIMIT),
        cost_estimate=pl.CostEstimate(flops=0, bytes_accessed=4 * piece.size, transcendentals=0),
        name="unpack",
    )(jnp.reshape(owner, (1,)), *inputs)


def local(records, block_start, slab_index, weight_table):
    sec_local, rec_len, fields, cell_local = records.shape
    sec_count = lax.axis_size("sector")
    tm_count = lax.axis_size("tm")
    space_count = lax.axis_size("space")
    owners = sec_count * tm_count
    owner_axes = ("sector", "tm")
    sectors = sec_local * sec_count
    orders = sectors // 2
    blocks = block_start.shape[0]
    depth = 2 * blocks
    part = cell_local // owners
    own_freqs = NFREQ // owners
    me = lax.axis_index("sector") * tm_count + lax.axis_index("tm")

    by_field = jnp.transpose(records, (0, 2, 1, 3))
    sec_at, tm_at = lax.axis_index("sector"), lax.axis_index("tm")
    shifts = [(z, x) for z in range(sec_count) for x in range(tm_count)]
    in_order = sorted(shifts, key=lambda r: (r[0] == 0, abs(2 * r[0] - sec_count), r))

    def owner_after(z, x):
        return (sec_at + z) % sec_count * tm_count + (tm_at + x) % tm_count

    def send(piece, z, x):
        if (z, x) == (0, 0):
            return piece
        hops = [
            (a * tm_count + j, (a + z) % sec_count * tm_count + (j + x) % tm_count)
            for a in range(sec_count)
            for j in range(tm_count)
        ]
        return lax.ppermute(piece, owner_axes, hops)

    parts = [(k, 0, part) for k in range(fields)]
    if part % (2 * LANES) == 0:
        parts[-1:] = [(fields - 1, 0, part // 2), (fields - 1, part // 2, part)]
    arrived = []
    for own_part in parts:
        got = {r: send(take(by_field, owner_after(*r), owners, own_part), *r) for r in in_order}
        arrived.append([got[r] for r in shifts])

    time_basis = placed_time_basis(block_start, tm_count)
    half, _ = half_span(blocks // tm_count)
    halves = blocks // tm_count // half
    azimuth = jnp.einsum(
        "mcse,ij,bd->cmibsjed",
        order_table(orders, sectors),
        jnp.eye(tm_count, dtype=jnp.bfloat16),
        jnp.eye(half, dtype=jnp.bfloat16),
    ).reshape(2 * orders * tm_count * half, sectors * tm_count * 2 * half)
    place = [
        (b // half % halves * tm_count + b // (half * halves)) * half + b % half
        for b in range(blocks)
    ]
    own_slab = lax.dynamic_slice_in_dim(slab_index, me * part, part)
    weight = jnp.sum(
        jnp.where(
            own_slab[None, :] == jnp.arange(weight_table.shape[0], dtype=jnp.int32)[:, None],
            weight_table[:, None],
            0.0,
        ),
        0,
        keepdims=True,
    )

    gram = jnp.zeros((NFREQ, blocks, orders * blocks), jnp.float32)
    coeffs = []
    for pieces, (_, low, high) in zip(arrived, parts):
        own, gram = coeffs_and_gram(
            jnp.stack([sec_at, tm_at]), pieces, sec_count, time_basis, azimuth, weight[:, low:high], gram
        )
        coeffs.append(own)

    if own_freqs % space_count == 0:
        axes = owner_axes + ("space",)
    else:
        gram = lax.psum(gram, "space")
        axes = owner_axes
    solvers = math.prod(lax.axis_size(a) for a in axes)
    solved = NFREQ // solvers
    gram = gram.reshape((solvers, solved) + gram.shape[1:])
    gram = lax.all_to_all(gram, axes, split_axis=0, concat_axis=0, tiled=True)
    gram = jnp.sum(gram, 0).reshape(solved, blocks, orders, blocks)
    gram = jnp.transpose(gram, (3, 1, 0, 2)).reshape(blocks, blocks, solved * orders)
    basis, energy = subspace(gram, tuple(place[:MODES]), fields * cell_local * space_count)

    short = basis.astype(jnp.bfloat16).reshape(2, MODES, blocks, solved, orders)
    short = jnp.transpose(short, (3, 4, 0, 1, 2))
    short_re, short_im = short[:, :, 0], short[:, :, 1]
    mixing = jnp.stack(
        [jnp.concatenate([short_re, -short_im], -1), jnp.concatenate([short_im, short_re], -1)], 2
    ).reshape(solved, orders * 2 * MODES * depth)
    energy = jnp.transpose(energy.reshape(MODES, solved, orders), (1, 2, 0)).reshape(solved, -1)
    high = energy.astype(jnp.bfloat16)
    rest = energy - high.astype(jnp.float32)
    middle = rest.astype(jnp.bfloat16)
    low = (rest - middle.astype(jnp.float32)).astype(jnp.bfloat16)
    packet = jnp.concatenate([mixing, high, middle, low], 1)
    width = -(-packet.shape[1] // LANES) * LANES
    packet = jnp.pad(packet, ((0, 0), (0, width - packet.shape[1])))
    packet = packet.reshape(1, solved, width // LANES, LANES)
    packet = jnp.broadcast_to(packet, (solvers,) + packet.shape[1:])
    packet = lax.all_to_all(packet, axes, split_axis=0, concat_axis=0, tiled=True)
    packet = packet.reshape(NFREQ, width)
    count = orders * MODES
    mixing = packet[:, :orders * 2 * MODES * depth].reshape(NFREQ, orders * 2 * MODES, depth)
    tail = packet[:, orders * 2 * MODES * depth:].astype(jnp.float32)
    energy = (tail[:, :count] + tail[:, count:2 * count]) + tail[:, 2 * count:3 * count]
    energy = energy.reshape(NFREQ, orders, MODES)
    factor = jnp.broadcast_to(
        lax.rsqrt(energy)[:, :, None, :], (NFREQ, orders, 2, MODES)
    ).reshape(owners, own_freqs, orders * 2 * MODES)
    root_weight = jnp.sqrt(weight)
    spread = jnp.broadcast_to(
        jnp.eye(depth, dtype=jnp.bfloat16).reshape(depth, 2, 1, blocks), (depth, 2, orders, blocks)
    ).reshape(depth, depth * orders)

    mode_fields = None
    arrived = []
    for z, x in in_order:
        piece = mix(
            owner_after(z, x), coeffs, parts, mixing, spread, factor, root_weight, owners, orders, fields
        )
        arrived.append((owner_after(-z, -x), send(piece, z, x)))
    for owner, piece in arrived:
        piece = piece.reshape(fields, own_freqs, orders, 2, MODES, part)
        mode_fields = unpack(owner, piece, owners, mode_fields)
    mode_fields = jnp.transpose(mode_fields, (0, 1, 2, 4, 3, 5))
    own_energy = lax.dynamic_slice_in_dim(energy, me * own_freqs, own_freqs)
    return (mode_fields, jnp.transpose(own_energy, (1, 0, 2)))


def solution(mesh):
    placed = (P("sector", "tm", None, "space"), P(), P("space"), P())
    return jax.shard_map(
        local,
        mesh=mesh,
        in_specs=placed,
        out_specs=(
            P(None, ("sector", "tm"), None, None, None, "space"),
            P(None, ("sector", "tm"), None),
        ),
        check_vma=False,
    )
```

```python
import functools
import math

import jax
import jax.numpy as jnp
from jax import lax
from jax.experimental import pallas as pl
from jax.experimental.pallas import tpu as pltpu
from jax.sharding import PartitionSpec as P

NFFT = 64
NFREQ = 32
MODES = 8
SUBIT = 4
LANES = 128
EPSILON = 1e-06
VMEM_LIMIT = 48 * 1024 * 1024


def time_table(length, freq_count):
    steps_t = jnp.arange(length, dtype=jnp.float32)
    freq_f = jnp.arange(freq_count, dtype=jnp.float32)
    window = 0.5 - 0.5 * jnp.cos(2.0 * math.pi * steps_t / length)
    angles = 2.0 * math.pi * freq_f[:, None] * steps_t[None, :] / length
    both = jnp.stack([window * jnp.cos(angles), -window * jnp.sin(angles)])
    return (both / math.sqrt(length)).astype(jnp.bfloat16)


def order_table(orders, sectors):
    order_m = jnp.arange(orders, dtype=jnp.float32)[:, None]
    sector_s = jnp.arange(sectors, dtype=jnp.float32)[None, :]
    angles = 2.0 * math.pi * order_m * sector_s / sectors
    cosine = jnp.cos(angles)
    sine_part = jnp.sin(angles)
    upper_row = jnp.stack([cosine, sine_part], -1)
    lower_row = jnp.stack([-sine_part, cosine], -1)
    return (jnp.stack([upper_row, lower_row], 1) / math.sqrt(sectors)).astype(jnp.bfloat16)


def half_span(blocks):
    half = blocks // 2
    return half, (half - 1) * (NFFT // 2) + NFFT // 8 + NFFT


def placed_time_basis(block_start, tm_count):
    blocks = block_start.shape[0] // tm_count
    half, span = half_span(blocks)
    basis = time_table(NFFT, NFREQ)
    first = jnp.arange(blocks, dtype=jnp.int32) // half * (half * (NFFT // 2))
    inside = block_start.reshape(tm_count, blocks) - first[None, :]
    place = (
        inside[:, :, None, None] + jnp.arange(NFFT, dtype=jnp.int32)[:, None]
        == jnp.arange(span, dtype=jnp.int32)[None, :]
    ).astype(jnp.bfloat16)
    table = jnp.einsum(
        "eft,jhbtu->jhfebu",
        basis,
        place.reshape(tm_count, 2, half, NFFT, span),
        preferred_element_type=jnp.float32,
    ).astype(jnp.bfloat16)
    return table.reshape(tm_count, 2, NFREQ * 2 * half, span)


def coeff_kernel(sec_count, sec_local, freqs, orders, place_ref, time_ref, azimuth_ref, weight_ref,
                 before_ref, *refs):
    record_refs, (coeff_ref, gram_ref, spectra) = refs[:-3], refs[-3:]
    step = pl.program_id(0)
    tm_count, halves, _, span = time_ref.shape
    rec_len, columns = record_refs[0].shape[1:]
    sectors = spectra.shape[0]
    rows = spectra.shape[2] // NFREQ

    beside = 2 if columns == LANES and sec_count % 2 == 0 else 1

    @pl.when(step < sec_local)
    def _():
        for shift in range(0, sec_count, beside):
            for h in range(halves):
                first = h * (rec_len - span) // (halves - 1)
                parts = []
                for j in range(tm_count):
                    row = []
                    for n in range(beside):
                        own = record_refs[(shift + n) * tm_count:(shift + n + 1) * tm_count]
                        piece = own[0][0, first:first + span]
                        for x in range(1, tm_count):
                            here = lax.rem(place_ref[1] + tm_count - x, tm_count) == j
                            piece = jnp.where(here, own[x][0, first:first + span], piece)
                        row.append(piece)
                    wide_piece = row[0] if beside == 1 else jnp.concatenate(row, 1)
                    part = jnp.dot(time_ref[j, h], wide_piece, preferred_element_type=jnp.float32)
                    parts.append(part.reshape(NFREQ, rows // tm_count, beside * columns))
                joined = jnp.stack(parts, 1).reshape(NFREQ * rows, beside * columns)
                joined = joined.astype(jnp.bfloat16)
                for n in range(beside):
                    source = lax.rem(place_ref[0] + sec_count - shift - n, sec_count)
                    spectra[source * sec_local + step, h] = joined[:, n * columns:(n + 1) * columns]

    @pl.when(step >= sec_local)
    def _():
        half_rows = azimuth_ref.shape[0]
        depth = half_rows // (2 * orders)
        blocks = depth * halves
        wide = orders * blocks
        row = lax.broadcasted_iota(jnp.int32, (wide, wide), 0) % blocks
        column = lax.broadcasted_iota(jnp.int32, (wide, wide), 1) % blocks
        owner = lax.broadcasted_iota(jnp.int32, (blocks, wide), 1) // blocks
        for n in range(freqs):
            at = pl.multiple_of(((step - sec_local) * freqs + n) * rows, rows)
            own = [
                spectra[:, h, pl.ds(at, rows), :].reshape(sectors * rows, columns)
                for h in range(halves)
            ]
            if beside == halves:
                both = jnp.dot(
                    azimuth_ref[...], jnp.concatenate(own, 1), preferred_element_type=jnp.float32
                )
                parts = [both[:, h * columns:(h + 1) * columns] for h in range(halves)]
            else:
                parts = [
                    jnp.dot(azimuth_ref[...], x, preferred_element_type=jnp.float32) for x in own
                ]
            parts = [x.reshape(2 * orders, depth, columns) for x in parts]
            coeffs = jnp.stack(parts, 1).reshape(2 * wide, columns).astype(jnp.bfloat16)
            coeff_ref[n] = coeffs
            weighted = (coeffs.astype(jnp.float32) * weight_ref[...]).astype(jnp.bfloat16)
            products = lax.dot_general(
                weighted, coeffs, (((1,), (1,)), ((), ())), preferred_element_type=jnp.float32
            )
            real = products[:wide, :wide] + products[wide:, wide:]
            imag = products[:wide, wide:] - products[wide:, :wide]
            packed = jnp.where(row <= column, real, imag)
            own = packed[:blocks]
            for m in range(1, orders):
                own = jnp.where(owner == m, packed[m * blocks:(m + 1) * blocks], own)
            gram_ref[n] = before_ref[n] + own


def coeffs_and_gram(place, arrived, sec_count, time_basis, azimuth, weight, before):
    sec_local, rec_len, columns = arrived[0].shape
    sectors = sec_count * sec_local
    halves = time_basis.shape[1]
    blocks, wide = before.shape[1:]
    rows = azimuth.shape[1] // sectors
    steps = 4
    freqs = NFREQ // steps
    later = lambda i: jnp.maximum(i - sec_local, 0)
    early = lambda i: jnp.minimum(i, sec_local - 1)
    flops = 2 * columns * (
        sectors * time_basis.size + NFREQ * halves * azimuth.size + NFREQ * 4 * wide * wide
    )
    piece = pl.BlockSpec((1, rec_len, columns), lambda i, _: (early(i), 0, 0))
    return pl.pallas_call(
        functools.partial(coeff_kernel, sec_count, sec_local, freqs, wide // blocks),
        grid_spec=pltpu.PrefetchScalarGridSpec(
            num_scalar_prefetch=1,
            grid=(sec_local + steps,),
            in_specs=[
                pl.BlockSpec(time_basis.shape, lambda i, _: (0, 0, 0, 0)),
                pl.BlockSpec(azimuth.shape, lambda i, _: (0, 0)),
                pl.BlockSpec(weight.shape, lambda i, _: (0, 0)),
                pl.BlockSpec((freqs, blocks, wide), lambda i, _: (later(i), 0, 0)),
            ] + [piece] * len(arrived),
            out_specs=[
                pl.BlockSpec((freqs, 2 * wide, columns), lambda i, _: (later(i), 0, 0)),
                pl.BlockSpec((freqs, blocks, wide), lambda i, _: (later(i), 0, 0)),
            ],
            scratch_shapes=[pltpu.VMEM((sectors, halves, NFREQ * rows, columns), jnp.bfloat16)],
        ),
        out_shape=[
            jax.ShapeDtypeStruct((NFREQ, 2 * wide, columns), jnp.bfloat16),
            jax.ShapeDtypeStruct(before.shape, jnp.float32),
        ],
        compiler_params=pltpu.CompilerParams(vmem_limit_bytes=VMEM_LIMIT),
        cost_estimate=pl.CostEstimate(
            flops=flops,
            bytes_accessed=2 * (len(arrived) * arrived[0].size + NFREQ * 2 * wide * columns),
            transcendentals=0,
        ),
        name="coeffs_and_gram",
    )(place, time_basis, azimuth, weight, before, *arrived)


def subspace_kernel(cell_total, first, packed_ref, basis_ref, energy_ref):
    size, _, pairs = packed_ref.shape
    row = lax.broadcasted_iota(jnp.int32, (size, pairs), 0)
    column_re, column_im = [], []
    for q in range(size):
        down, along = packed_ref[q], packed_ref[:, q, :]
        column_re.append(jnp.where(row <= q, down, along))
        column_im.append(jnp.where(row > q, down, jnp.where(row == q, 0.0, -along)))

    def image_of(vec_re, vec_im):
        out_re, out_im = [], []
        for j in range(MODES):
            sum_re = jnp.zeros_like(column_re[0])
            sum_im = jnp.zeros_like(column_re[0])
            for q in range(size):
                at_re, at_im = vec_re[j][q:q + 1], vec_im[j][q:q + 1]
                sum_re += column_re[q] * at_re - column_im[q] * at_im
                sum_im += column_re[q] * at_im + column_im[q] * at_re
            out_re.append(sum_re)
            out_im.append(sum_im)
        return out_re, out_im

    total = lambda x: jnp.sum(x, 0, keepdims=True)
    vec_re = [column_re[q] for q in first]
    vec_im = [column_im[q] for q in first]
    for sweep in range(SUBIT):
        if sweep > 0:
            vec_re, vec_im = image_of(vec_re, vec_im)
        vec_re, vec_im = list(vec_re), list(vec_im)
        for i in range(MODES):
            scale = 1.0 / jnp.sqrt(total(vec_re[i] * vec_re[i] + vec_im[i] * vec_im[i]) + EPSILON)
            own_re, own_im = vec_re[i] * scale, vec_im[i] * scale
            vec_re[i], vec_im[i] = own_re, own_im
            for j in range(i + 1, MODES):
                proj_re = total(own_re * vec_re[j] + own_im * vec_im[j])
                proj_im = total(own_re * vec_im[j] - own_im * vec_re[j])
                vec_re[j] = vec_re[j] - (proj_re * own_re - proj_im * own_im)
                vec_im[j] = vec_im[j] - (proj_re * own_im + proj_im * own_re)
    image_re, image_im = image_of(vec_re, vec_im)
    for j in range(MODES):
        basis_ref[0, j] = vec_re[j]
        basis_ref[1, j] = vec_im[j]
        energy_ref[j:j + 1] = total(vec_re[j] * image_re[j] + vec_im[j] * image_im[j]) / cell_total


def subspace(packed, first, cell_total):
    size, _, pairs = packed.shape
    return pl.pallas_call(
        functools.partial(subspace_kernel, float(cell_total), first),
        out_shape=[
            jax.ShapeDtypeStruct((2, MODES, size, pairs), jnp.float32),
            jax.ShapeDtypeStruct((MODES, pairs), jnp.float32),
        ],
        name="subspace",
    )(packed)


def mix_kernel(orders, parts, owner_ref, mixing_ref, spread_ref, factor_ref, root_ref, *refs):
    coeff_refs, out_ref = refs[:len(parts)], refs[-1]
    freqs, own_rows, _ = mixing_ref.shape
    rows = 2 * own_rows
    total = spread_ref.shape[2]
    blocks = total // (2 * orders)
    row = lax.broadcasted_iota(jnp.int32, (rows, total), 0) % own_rows // (own_rows // orders)
    column = lax.broadcasted_iota(jnp.int32, (rows, total), 1) // blocks % orders
    factor = jnp.transpose(factor_ref[0])
    for n in range(freqs):
        wide = jnp.concatenate(
            [
                jnp.dot(mixing_ref[n], spread_ref[d], preferred_element_type=jnp.float32)
                for d in range(2)
            ],
            0,
        )
        wide = jnp.where(row == column, wide, 0.0).astype(jnp.bfloat16)
        for (k, low, high), coeff_ref in zip(parts, coeff_refs):
            fields = jnp.dot(wide, coeff_ref[n], preferred_element_type=jnp.float32)
            scaled = fields * (factor[:, n:n + 1] * root_ref[:, low:high])
            out_ref[k, n, :, low:high] = scaled.astype(jnp.bfloat16)


def mix(owner, coeffs, parts, mixing, spread, factor, root_weight, owners, orders, fields, after):
    rows = coeffs[0].shape[1]
    own_rows, depth = mixing.shape[1:]
    out_rows = 2 * own_rows
    columns = root_weight.shape[1]
    freqs = NFREQ // owners
    return pl.pallas_call(
        functools.partial(mix_kernel, orders, parts),
        grid_spec=pltpu.PrefetchScalarGridSpec(
            num_scalar_prefetch=1,
            grid=(1,),
            in_specs=[
                pl.BlockSpec((freqs, own_rows, depth), lambda i, at: (at[0], 0, 0)),
                pl.BlockSpec(spread.shape, lambda i, at: (0, 0, 0)),
                pl.BlockSpec((1, freqs, out_rows), lambda i, at: (at[0], 0, 0)),
                pl.BlockSpec(root_weight.shape, lambda i, at: (0, 0)),
            ] + [
                pl.BlockSpec((freqs, rows, x.shape[2]), lambda i, at: (at[0], 0, 0)) for x in coeffs
            ] + [pl.BlockSpec(memory_space=pl.ANY)] * len(after),
            out_specs=pl.BlockSpec((fields, freqs, out_rows, columns), lambda i, at: (0, 0, 0, 0)),
        ),
        out_shape=jax.ShapeDtypeStruct((fields, freqs, out_rows, columns), jnp.bfloat16),
        compiler_params=pltpu.CompilerParams(vmem_limit_bytes=VMEM_LIMIT),
        cost_estimate=pl.CostEstimate(
            flops=2 * freqs * out_rows * rows * fields * columns,
            bytes_accessed=2 * freqs * (rows + out_rows) * fields * columns,
            transcendentals=0,
        ),
        name="mix",
    )(jnp.reshape(owner, (1,)), mixing, spread, factor, root_weight, *coeffs, *after)


def take_kernel(place_ref, record_ref, *refs):
    out_ref = refs[-1]
    out_ref[...] = record_ref[:, 0]


def take(by_field, owner, owners, part, after):
    sec_local, _, rec_len, cells = by_field.shape
    k, low, high = part
    count = high - low
    own = cells // owners
    if count % LANES:
        return lax.dynamic_slice_in_dim(by_field[:, k], owner * own + low, count, 2)
    return pl.pallas_call(
        take_kernel,
        grid_spec=pltpu.PrefetchScalarGridSpec(
            num_scalar_prefetch=1,
            grid=(1,),
            in_specs=[
                pl.BlockSpec((sec_local, 1, rec_len, count), lambda i, at: (0, k, 0, at[0]))
            ] + [pl.BlockSpec(memory_space=pl.ANY)] * len(after),
            out_specs=pl.BlockSpec((sec_local, rec_len, count), lambda i, at: (0, 0, 0)),
        ),
        out_shape=jax.ShapeDtypeStruct((sec_local, rec_len, count), by_field.dtype),
        compiler_params=pltpu.CompilerParams(vmem_limit_bytes=VMEM_LIMIT),
        cost_estimate=pl.CostEstimate(
            flops=0, bytes_accessed=4 * sec_local * rec_len * count, transcendentals=0
        ),
        name="take",
    )(jnp.reshape(owner * (own // count) + low // count, (1,)), by_field, *after)


def unpack_kernel(owner_ref, piece_ref, *refs):
    out_ref = refs[-1]
    for k in range(piece_ref.shape[0]):
        for f in range(piece_ref.shape[1]):
            for d in range(piece_ref.shape[2]):
                out_ref[:, f, d, k] = piece_ref[k, f, d]


def unpack(owner, piece, owners, whole):
    fields, freqs, two, orders, modes, part = piece.shape
    shape = (orders, freqs, two, fields, modes, owners * part)
    if part % LANES:
        whole = jnp.zeros(shape, piece.dtype) if whole is None else whole
        piece = jnp.transpose(piece, (3, 1, 2, 0, 4, 5))
        return lax.dynamic_update_slice_in_dim(whole, piece, owner * part, 5)
    inputs = [piece] if whole is None else [piece, whole]
    in_specs = [
        pl.BlockSpec(piece.shape, lambda i, at: (0, 0, 0, 0, 0, 0)),
        pl.BlockSpec(memory_space=pl.ANY),
    ]
    return pl.pallas_call(
        unpack_kernel,
        grid_spec=pltpu.PrefetchScalarGridSpec(
            num_scalar_prefetch=1,
            grid=(1,),
            in_specs=in_specs[:len(inputs)],
            out_specs=pl.BlockSpec(shape[:5] + (part,), lambda i, at: (0, 0, 0, 0, 0, at[0])),
        ),
        out_shape=jax.ShapeDtypeStruct(shape, piece.dtype),
        input_output_aliases={} if whole is None else {2: 0},
        compiler_params=pltpu.CompilerParams(vmem_limit_bytes=VMEM_LIMIT),
        cost_estimate=pl.CostEstimate(flops=0, bytes_accessed=4 * piece.size, transcendentals=0),
        name="unpack",
    )(jnp.reshape(owner, (1,)), *inputs)


def local(records, block_start, slab_index, weight_table):
    sec_local, rec_len, fields, cell_local = records.shape
    sec_count = lax.axis_size("sector")
    tm_count = lax.axis_size("tm")
    space_count = lax.axis_size("space")
    owners = sec_count * tm_count
    owner_axes = ("sector", "tm")
    sectors = sec_local * sec_count
    orders = sectors // 2
    blocks = block_start.shape[0]
    depth = 2 * blocks
    part = cell_local // owners
    own_freqs = NFREQ // owners
    me = lax.axis_index("sector") * tm_count + lax.axis_index("tm")

    by_field = jnp.transpose(records, (0, 2, 1, 3))
    sec_at, tm_at = lax.axis_index("sector"), lax.axis_index("tm")
    shifts = [(z, x) for z in range(sec_count) for x in range(tm_count)]
    in_order = sorted(
        [r for r in shifts if r[0] > 0], key=lambda r: (abs(2 * r[0] - sec_count), r)
    )
    in_order[2:2] = [r for r in shifts if r[0] == 0 and r[1] > 0] + [(0, 0)]

    def owner_after(z, x):
        return (sec_at + z) % sec_count * tm_count + (tm_at + x) % tm_count

    def send(piece, z, x):
        if (z, x) == (0, 0):
            return piece
        hops = [
            (a * tm_count + j, (a + z) % sec_count * tm_count + (j + x) % tm_count)
            for a in range(sec_count)
            for j in range(tm_count)
        ]
        return lax.ppermute(piece, owner_axes, hops)

    parts = [(k, 0, part) for k in range(fields)]
    if part % (2 * LANES) == 0:
        parts[-1:] = [(fields - 1, 0, part // 2), (fields - 1, part // 2, part)]
    time_basis = placed_time_basis(block_start, tm_count)
    half, _ = half_span(blocks // tm_count)
    halves = blocks // tm_count // half
    azimuth = jnp.einsum(
        "mcse,ij,bd->cmibsjed",
        order_table(orders, sectors),
        jnp.eye(tm_count, dtype=jnp.bfloat16),
        jnp.eye(half, dtype=jnp.bfloat16),
    ).reshape(2 * orders * tm_count * half, sectors * tm_count * 2 * half)
    place = [
        (b // half % halves * tm_count + b // (half * halves)) * half + b % half
        for b in range(blocks)
    ]
    own_slab = lax.dynamic_slice_in_dim(slab_index, me * part, part)
    weight = jnp.sum(
        jnp.where(
            own_slab[None, :] == jnp.arange(weight_table.shape[0], dtype=jnp.int32)[:, None],
            weight_table[:, None],
            0.0,
        ),
        0,
        keepdims=True,
    )

    gram = jnp.zeros((NFREQ, blocks, orders * blocks), jnp.float32)

    def coeffs_of(n, pieces, gram):
        _, low, high = parts[n]
        return coeffs_and_gram(
            jnp.stack([sec_at, tm_at]), pieces, sec_count, time_basis, azimuth, weight[:, low:high], gram
        )

    coeffs = []
    arrived = []
    for own_part in parts:
        if len(arrived) > 1:
            own, gram = coeffs_of(len(coeffs), arrived[len(coeffs)], gram)
            coeffs.append(own)
            after = (gram,)
        else:
            after = ()
        got = {r: send(take(by_field, owner_after(*r), owners, own_part, after), *r) for r in in_order}
        arrived.append([got[r] for r in shifts])
    while len(coeffs) < len(parts):
        own, gram = coeffs_of(len(coeffs), arrived[len(coeffs)], gram)
        coeffs.append(own)

    if own_freqs % space_count == 0:
        axes = owner_axes + ("space",)
    else:
        gram = lax.psum(gram, "space")
        axes = owner_axes
    solvers = math.prod(lax.axis_size(a) for a in axes)
    solved = NFREQ // solvers
    gram = gram.reshape((solvers, solved) + gram.shape[1:])
    gram = lax.all_to_all(gram, axes, split_axis=0, concat_axis=0, tiled=True)
    gram = jnp.sum(gram, 0).reshape(solved, blocks, orders, blocks)
    gram = jnp.transpose(gram, (3, 1, 0, 2)).reshape(blocks, blocks, solved * orders)
    basis, energy = subspace(gram, tuple(place[:MODES]), fields * cell_local * space_count)

    short = basis.astype(jnp.bfloat16).reshape(2, MODES, blocks, solved, orders)
    mixing = jnp.transpose(short, (3, 4, 1, 0, 2)).reshape(solved, orders * MODES * depth)
    energy = jnp.transpose(energy.reshape(MODES, solved, orders), (1, 2, 0)).reshape(solved, -1)
    high = energy.astype(jnp.bfloat16)
    rest = energy - high.astype(jnp.float32)
    middle = rest.astype(jnp.bfloat16)
    low = (rest - middle.astype(jnp.float32)).astype(jnp.bfloat16)
    packet = jnp.concatenate([mixing, high, middle, low], 1)
    width = -(-packet.shape[1] // LANES) * LANES
    packet = jnp.pad(packet, ((0, 0), (0, width - packet.shape[1])))
    packet = packet.reshape(1, solved, width // LANES, LANES)
    packet = jnp.broadcast_to(packet, (solvers,) + packet.shape[1:])
    packet = lax.all_to_all(packet, axes, split_axis=0, concat_axis=0, tiled=True)
    packet = packet.reshape(NFREQ, width)
    count = orders * MODES
    mixing = packet[:, :orders * MODES * depth].reshape(NFREQ, orders * MODES, depth)
    tail = packet[:, orders * MODES * depth:].astype(jnp.float32)
    energy = (tail[:, :count] + tail[:, count:2 * count]) + tail[:, 2 * count:3 * count]
    factor = lax.rsqrt(energy)
    factor = jnp.concatenate([factor, factor], 1).reshape(owners, own_freqs, orders * 2 * MODES)
    energy = energy.reshape(NFREQ, orders, MODES)
    root_weight = jnp.sqrt(weight)
    signs = jnp.array([[[1, 0], [0, -1]], [[0, 1], [1, 0]]], jnp.bfloat16)
    spread = jnp.broadcast_to(
        signs[:, :, None, :, None, None]
        * jnp.eye(blocks, dtype=jnp.bfloat16)[None, None, :, None, None, :],
        (2, 2, blocks, 2, orders, blocks),
    ).reshape(2, depth, depth * orders)

    mode_fields = None
    sent = []
    unpacked = 0
    in_flight = 5

    def unpack_next(mode_fields):
        owner, piece = sent[unpacked]
        piece = piece.reshape(fields, own_freqs, 2, orders, MODES, part)
        return unpack(owner, piece, owners, mode_fields)

    before = ()
    for z, x in in_order:
        if len(sent) > in_flight and part % LANES == 0:
            mode_fields = unpack_next(mode_fields)
            unpacked += 1
            before = before + (mode_fields,)
        piece = mix(
            owner_after(z, x), coeffs, parts, mixing, spread, factor, root_weight, owners, orders,
            fields, before,
        )
        before = (piece,)
        sent.append((owner_after(-z, -x), send(piece, z, x)))
    while unpacked < len(sent):
        mode_fields = unpack_next(mode_fields)
        unpacked += 1
    mode_fields = jnp.transpose(mode_fields, (0, 1, 2, 4, 3, 5))
    own_energy = lax.dynamic_slice_in_dim(energy, me * own_freqs, own_freqs)
    return (mode_fields, jnp.transpose(own_energy, (1, 0, 2)))


def solution(mesh):
    placed = (P("sector", "tm", None, "space"), P(), P("space"), P())
    return jax.shard_map(
        local,
        mesh=mesh,
        in_specs=placed,
        out_specs=(
            P(None, ("sector", "tm"), None, None, None, "space"),
            P(None, ("sector", "tm"), None),
        ),
        check_vma=False,
    )
```

```python
import functools
import math

import jax
import jax.numpy as jnp
from jax import lax
from jax.experimental import pallas as pl
from jax.experimental.pallas import tpu as pltpu
from jax.sharding import PartitionSpec as P

NFFT = 64
NFREQ = 32
MODES = 8
SUBIT = 4
LANES = 128
EPSILON = 1e-06
VMEM_LIMIT = 48 * 1024 * 1024


def time_table(length, freq_count):
    steps_t = jnp.arange(length, dtype=jnp.float32)
    freq_f = jnp.arange(freq_count, dtype=jnp.float32)
    window = 0.5 - 0.5 * jnp.cos(2.0 * math.pi * steps_t / length)
    angles = 2.0 * math.pi * freq_f[:, None] * steps_t[None, :] / length
    both = jnp.stack([window * jnp.cos(angles), -window * jnp.sin(angles)])
    return (both / math.sqrt(length)).astype(jnp.bfloat16)


def order_table(orders, sectors):
    order_m = jnp.arange(orders, dtype=jnp.float32)[:, None]
    sector_s = jnp.arange(sectors, dtype=jnp.float32)[None, :]
    angles = 2.0 * math.pi * order_m * sector_s / sectors
    cosine = jnp.cos(angles)
    sine_part = jnp.sin(angles)
    upper_row = jnp.stack([cosine, sine_part], -1)
    lower_row = jnp.stack([-sine_part, cosine], -1)
    return (jnp.stack([upper_row, lower_row], 1) / math.sqrt(sectors)).astype(jnp.bfloat16)


def half_span(blocks):
    half = blocks // 2
    return half, (half - 1) * (NFFT // 2) + NFFT // 8 + NFFT


def placed_time_basis(block_start, tm_count):
    blocks = block_start.shape[0] // tm_count
    half, span = half_span(blocks)
    basis = time_table(NFFT, NFREQ)
    first = jnp.arange(blocks, dtype=jnp.int32) // half * (half * (NFFT // 2))
    inside = block_start.reshape(tm_count, blocks) - first[None, :]
    place = (
        inside[:, :, None, None] + jnp.arange(NFFT, dtype=jnp.int32)[:, None]
        == jnp.arange(span, dtype=jnp.int32)[None, :]
    ).astype(jnp.bfloat16)
    table = jnp.einsum(
        "eft,jhbtu->jhfebu",
        basis,
        place.reshape(tm_count, 2, half, NFFT, span),
        preferred_element_type=jnp.float32,
    ).astype(jnp.bfloat16)
    return table.reshape(tm_count, 2, NFREQ * 2 * half, span)


def coeff_kernel(sec_count, sec_local, freqs, orders, place_ref, time_ref, azimuth_ref, weight_ref,
                 before_ref, *refs):
    record_refs, (coeff_ref, gram_ref, spectra) = refs[:-3], refs[-3:]
    step = pl.program_id(0)
    tm_count, halves, _, span = time_ref.shape
    rec_len, columns = record_refs[0].shape[1:]
    sectors = spectra.shape[0]
    rows = spectra.shape[2] // NFREQ

    @pl.when(step < sec_local)
    def _():
        for shift in range(sec_count):
            source = lax.rem(place_ref[0] + sec_count - shift, sec_count)
            own = record_refs[shift * tm_count:(shift + 1) * tm_count]
            for h in range(halves):
                first = h * (rec_len - span) // (halves - 1)
                parts = []
                for j in range(tm_count):
                    piece = own[0][0, first:first + span]
                    for x in range(1, tm_count):
                        here = lax.rem(place_ref[1] + tm_count - x, tm_count) == j
                        piece = jnp.where(here, own[x][0, first:first + span], piece)
                    part = jnp.dot(time_ref[j, h], piece, preferred_element_type=jnp.float32)
                    parts.append(part.reshape(NFREQ, rows // tm_count, columns))
                joined = jnp.stack(parts, 1).reshape(NFREQ * rows, columns)
                spectra[source * sec_local + step, h] = joined.astype(jnp.bfloat16)

    @pl.when(step >= sec_local)
    def _():
        half_rows = azimuth_ref.shape[0]
        depth = half_rows // (2 * orders)
        blocks = depth * halves
        wide = orders * blocks
        row = lax.broadcasted_iota(jnp.int32, (wide, wide), 0) % blocks
        column = lax.broadcasted_iota(jnp.int32, (wide, wide), 1) % blocks
        owner = lax.broadcasted_iota(jnp.int32, (blocks, wide), 1) // blocks
        for n in range(freqs):
            at = pl.multiple_of(((step - sec_local) * freqs + n) * rows, rows)
            own = [
                spectra[:, h, pl.ds(at, rows), :].reshape(sectors * rows, columns)
                for h in range(halves)
            ]
            parts = [
                jnp.dot(azimuth_ref[...], x, preferred_element_type=jnp.float32) for x in own
            ]
            parts = [x.reshape(2 * orders, depth, columns) for x in parts]
            coeffs = jnp.stack(parts, 1).reshape(2 * wide, columns).astype(jnp.bfloat16)
            coeff_ref[n] = coeffs
            weighted = (coeffs.astype(jnp.float32) * weight_ref[...]).astype(jnp.bfloat16)
            products = lax.dot_general(
                weighted, coeffs, (((1,), (1,)), ((), ())), preferred_element_type=jnp.float32
            )
            real = products[:wide, :wide] + products[wide:, wide:]
            imag = products[:wide, wide:] - products[wide:, :wide]
            packed = jnp.where(row <= column, real, imag)
            own = packed[:blocks]
            for m in range(1, orders):
                own = jnp.where(owner == m, packed[m * blocks:(m + 1) * blocks], own)
            gram_ref[n] = before_ref[n] + own


def coeffs_and_gram(place, arrived, sec_count, time_basis, azimuth, weight, before):
    sec_local, rec_len, columns = arrived[0].shape
    sectors = sec_count * sec_local
    halves = time_basis.shape[1]
    blocks, wide = before.shape[1:]
    rows = azimuth.shape[1] // sectors
    steps = 4
    freqs = NFREQ // steps
    later = lambda i: jnp.maximum(i - sec_local, 0)
    early = lambda i: jnp.minimum(i, sec_local - 1)
    flops = 2 * columns * (
        sectors * time_basis.size + NFREQ * halves * azimuth.size + NFREQ * 4 * wide * wide
    )
    piece = pl.BlockSpec((1, rec_len, columns), lambda i, _: (early(i), 0, 0))
    return pl.pallas_call(
        functools.partial(coeff_kernel, sec_count, sec_local, freqs, wide // blocks),
        grid_spec=pltpu.PrefetchScalarGridSpec(
            num_scalar_prefetch=1,
            grid=(sec_local + steps,),
            in_specs=[
                pl.BlockSpec(time_basis.shape, lambda i, _: (0, 0, 0, 0)),
                pl.BlockSpec(azimuth.shape, lambda i, _: (0, 0)),
                pl.BlockSpec(weight.shape, lambda i, _: (0, 0)),
                pl.BlockSpec((freqs, blocks, wide), lambda i, _: (later(i), 0, 0)),
            ] + [piece] * len(arrived),
            out_specs=[
                pl.BlockSpec((freqs, 2 * wide, columns), lambda i, _: (later(i), 0, 0)),
                pl.BlockSpec((freqs, blocks, wide), lambda i, _: (later(i), 0, 0)),
            ],
            scratch_shapes=[pltpu.VMEM((sectors, halves, NFREQ * rows, columns), jnp.bfloat16)],
        ),
        out_shape=[
            jax.ShapeDtypeStruct((NFREQ, 2 * wide, columns), jnp.bfloat16),
            jax.ShapeDtypeStruct(before.shape, jnp.float32),
        ],
        compiler_params=pltpu.CompilerParams(vmem_limit_bytes=VMEM_LIMIT),
        cost_estimate=pl.CostEstimate(
            flops=flops,
            bytes_accessed=2 * (len(arrived) * arrived[0].size + NFREQ * 2 * wide * columns),
            transcendentals=0,
        ),
        name="coeffs_and_gram",
    )(place, time_basis, azimuth, weight, before, *arrived)


def subspace_kernel(cell_total, first, packed_ref, basis_ref, energy_ref):
    size, _, pairs = packed_ref.shape
    row = lax.broadcasted_iota(jnp.int32, (size, pairs), 0)
    column_re, column_im = [], []
    for q in range(size):
        down, along = packed_ref[q], packed_ref[:, q, :]
        column_re.append(jnp.where(row <= q, down, along))
        column_im.append(jnp.where(row > q, down, jnp.where(row == q, 0.0, -along)))

    def image_of(vec_re, vec_im):
        out_re, out_im = [], []
        for j in range(MODES):
            sum_re = jnp.zeros_like(column_re[0])
            sum_im = jnp.zeros_like(column_re[0])
            for q in range(size):
                at_re, at_im = vec_re[j][q:q + 1], vec_im[j][q:q + 1]
                sum_re += column_re[q] * at_re - column_im[q] * at_im
                sum_im += column_re[q] * at_im + column_im[q] * at_re
            out_re.append(sum_re)
            out_im.append(sum_im)
        return out_re, out_im

    total = lambda x: jnp.sum(x, 0, keepdims=True)
    vec_re = [column_re[q] for q in first]
    vec_im = [column_im[q] for q in first]
    for sweep in range(SUBIT):
        if sweep > 0:
            vec_re, vec_im = image_of(vec_re, vec_im)
        vec_re, vec_im = list(vec_re), list(vec_im)
        for i in range(MODES):
            scale = 1.0 / jnp.sqrt(total(vec_re[i] * vec_re[i] + vec_im[i] * vec_im[i]) + EPSILON)
            own_re, own_im = vec_re[i] * scale, vec_im[i] * scale
            vec_re[i], vec_im[i] = own_re, own_im
            for j in range(i + 1, MODES):
                proj_re = total(own_re * vec_re[j] + own_im * vec_im[j])
                proj_im = total(own_re * vec_im[j] - own_im * vec_re[j])
                vec_re[j] = vec_re[j] - (proj_re * own_re - proj_im * own_im)
                vec_im[j] = vec_im[j] - (proj_re * own_im + proj_im * own_re)
    image_re, image_im = image_of(vec_re, vec_im)
    for j in range(MODES):
        basis_ref[0, j] = vec_re[j]
        basis_ref[1, j] = vec_im[j]
        energy_ref[j:j + 1] = total(vec_re[j] * image_re[j] + vec_im[j] * image_im[j]) / cell_total


def subspace(packed, first, cell_total):
    size, _, pairs = packed.shape
    return pl.pallas_call(
        functools.partial(subspace_kernel, float(cell_total), first),
        out_shape=[
            jax.ShapeDtypeStruct((2, MODES, size, pairs), jnp.float32),
            jax.ShapeDtypeStruct((MODES, pairs), jnp.float32),
        ],
        name="subspace",
    )(packed)


def mix_kernel(orders, fields, owner_ref, mixing_ref, spread_ref, factor_ref, root_ref, *refs):
    out_ref = refs[-1]
    freqs, own_rows, _ = mixing_ref.shape
    rows = 2 * own_rows
    total = spread_ref.shape[2]
    blocks = total // (2 * orders)
    row = lax.broadcasted_iota(jnp.int32, (rows, total), 0) % own_rows // (own_rows // orders)
    column = lax.broadcasted_iota(jnp.int32, (rows, total), 1) // blocks % orders
    factor = jnp.transpose(factor_ref[0])
    for n in range(freqs):
        wide = jnp.concatenate(
            [
                jnp.dot(mixing_ref[n], spread_ref[d], preferred_element_type=jnp.float32)
                for d in range(2)
            ],
            0,
        )
        wide = jnp.where(row == column, wide, 0.0).astype(jnp.bfloat16)
        scale = factor[:, n:n + 1] * root_ref[...]
        for k in range(fields):
            mixed = jnp.dot(wide, refs[k][n], preferred_element_type=jnp.float32)
            out_ref[k, n] = (mixed * scale).astype(jnp.bfloat16)


def mix(owner, coeffs, mixing, spread, factor, root_weight, owners, orders, after):
    rows = coeffs[0].shape[1]
    own_rows, depth = mixing.shape[1:]
    out_rows = 2 * own_rows
    columns = root_weight.shape[1]
    freqs, fields = NFREQ // owners, len(coeffs)
    return pl.pallas_call(
        functools.partial(mix_kernel, orders, fields),
        grid_spec=pltpu.PrefetchScalarGridSpec(
            num_scalar_prefetch=1,
            grid=(1,),
            in_specs=[
                pl.BlockSpec((freqs, own_rows, depth), lambda i, at: (at[0], 0, 0)),
                pl.BlockSpec(spread.shape, lambda i, at: (0, 0, 0)),
                pl.BlockSpec((1, freqs, out_rows), lambda i, at: (at[0], 0, 0)),
                pl.BlockSpec(root_weight.shape, lambda i, at: (0, 0)),
            ] + [
                pl.BlockSpec((freqs, rows, x.shape[2]), lambda i, at: (at[0], 0, 0)) for x in coeffs
            ] + [pl.BlockSpec(memory_space=pl.ANY)] * len(after),
            out_specs=pl.BlockSpec((fields, freqs, out_rows, columns), lambda i, at: (0, 0, 0, 0)),
        ),
        out_shape=jax.ShapeDtypeStruct((fields, freqs, out_rows, columns), jnp.bfloat16),
        compiler_params=pltpu.CompilerParams(vmem_limit_bytes=VMEM_LIMIT),
        cost_estimate=pl.CostEstimate(
            flops=2 * freqs * out_rows * rows * fields * columns,
            bytes_accessed=2 * freqs * (rows + out_rows) * fields * columns,
            transcendentals=0,
        ),
        name="mix",
    )(jnp.reshape(owner, (1,)), mixing, spread, factor, root_weight, *coeffs, *after)


def take_kernel(place_ref, record_ref, out_ref):
    out_ref[...] = record_ref[:, 0]


def take(by_field, k, owner, owners):
    sec_local, _, rec_len, cells = by_field.shape
    count = cells // owners
    if count % LANES:
        return lax.dynamic_slice_in_dim(by_field[:, k], owner * count, count, 2)
    return pl.pallas_call(
        take_kernel,
        grid_spec=pltpu.PrefetchScalarGridSpec(
            num_scalar_prefetch=1,
            grid=(1,),
            in_specs=[
                pl.BlockSpec((sec_local, 1, rec_len, count), lambda i, at: (0, k, 0, at[0]))
            ],
            out_specs=pl.BlockSpec((sec_local, rec_len, count), lambda i, at: (0, 0, 0)),
        ),
        out_shape=jax.ShapeDtypeStruct((sec_local, rec_len, count), by_field.dtype),
        compiler_params=pltpu.CompilerParams(vmem_limit_bytes=VMEM_LIMIT),
        cost_estimate=pl.CostEstimate(
            flops=0, bytes_accessed=4 * sec_local * rec_len * count, transcendentals=0
        ),
        name="take",
    )(jnp.reshape(owner, (1,)), by_field)


def unpack_kernel(owner_ref, piece_ref, *refs):
    out_ref = refs[-1]
    for k in range(piece_ref.shape[0]):
        for f in range(piece_ref.shape[1]):
            for d in range(piece_ref.shape[2]):
                out_ref[:, f, d, k] = piece_ref[k, f, d]


def unpack(owner, piece, owners, whole):
    fields, freqs, two, orders, modes, part = piece.shape
    shape = (orders, freqs, two, fields, modes, owners * part)
    if part % LANES:
        whole = jnp.zeros(shape, piece.dtype) if whole is None else whole
        piece = jnp.transpose(piece, (3, 1, 2, 0, 4, 5))
        return lax.dynamic_update_slice_in_dim(whole, piece, owner * part, 5)
    inputs = [piece] if whole is None else [piece, whole]
    in_specs = [
        pl.BlockSpec(piece.shape, lambda i, at: (0, 0, 0, 0, 0, 0)),
        pl.BlockSpec(memory_space=pl.ANY),
    ]
    return pl.pallas_call(
        unpack_kernel,
        grid_spec=pltpu.PrefetchScalarGridSpec(
            num_scalar_prefetch=1,
            grid=(1,),
            in_specs=in_specs[:len(inputs)],
            out_specs=pl.BlockSpec(shape[:5] + (part,), lambda i, at: (0, 0, 0, 0, 0, at[0])),
        ),
        out_shape=jax.ShapeDtypeStruct(shape, piece.dtype),
        input_output_aliases={} if whole is None else {2: 0},
        compiler_params=pltpu.CompilerParams(vmem_limit_bytes=VMEM_LIMIT),
        cost_estimate=pl.CostEstimate(flops=0, bytes_accessed=4 * piece.size, transcendentals=0),
        name="unpack",
    )(jnp.reshape(owner, (1,)), *inputs)


def local(records, block_start, slab_index, weight_table):
    sec_local, rec_len, fields, cell_local = records.shape
    sec_count = lax.axis_size("sector")
    tm_count = lax.axis_size("tm")
    space_count = lax.axis_size("space")
    owners = sec_count * tm_count
    owner_axes = ("sector", "tm")
    sectors = sec_local * sec_count
    orders = sectors // 2
    blocks = block_start.shape[0]
    depth = 2 * blocks
    part = cell_local // owners
    own_freqs = NFREQ // owners
    me = lax.axis_index("sector") * tm_count + lax.axis_index("tm")

    by_field = jnp.transpose(records, (0, 2, 1, 3))
    sec_at, tm_at = lax.axis_index("sector"), lax.axis_index("tm")
    shifts = [(z, x) for z in range(sec_count) for x in range(tm_count)]
    in_order = sorted(
        [r for r in shifts if r != (0, 0)], key=lambda r: (r[0] == 0, abs(2 * r[0] - sec_count), r)
    )

    def owner_after(z, x):
        return (sec_at + z) % sec_count * tm_count + (tm_at + x) % tm_count

    def send(piece, z, x):
        if (z, x) == (0, 0):
            return piece
        hops = [
            (a * tm_count + j, (a + z) % sec_count * tm_count + (j + x) % tm_count)
            for a in range(sec_count)
            for j in range(tm_count)
        ]
        return lax.ppermute(piece, owner_axes, hops)

    arrived = []
    for k in range(fields):
        got = {r: send(take(by_field, k, owner_after(*r), owners), *r) for r in in_order + [(0, 0)]}
        arrived.append([got[r] for r in shifts])

    time_basis = placed_time_basis(block_start, tm_count)
    half, _ = half_span(blocks // tm_count)
    halves = blocks // tm_count // half
    azimuth = jnp.einsum(
        "mcse,ij,bd->cmibsjed",
        order_table(orders, sectors),
        jnp.eye(tm_count, dtype=jnp.bfloat16),
        jnp.eye(half, dtype=jnp.bfloat16),
    ).reshape(2 * orders * tm_count * half, sectors * tm_count * 2 * half)
    place = [
        (b // half % halves * tm_count + b // (half * halves)) * half + b % half
        for b in range(blocks)
    ]
    own_slab = lax.dynamic_slice_in_dim(slab_index, me * part, part)
    weight = jnp.sum(
        jnp.where(
            own_slab[None, :] == jnp.arange(weight_table.shape[0], dtype=jnp.int32)[:, None],
            weight_table[:, None],
            0.0,
        ),
        0,
        keepdims=True,
    )

    gram = jnp.zeros((NFREQ, blocks, orders * blocks), jnp.float32)

    coeffs = []
    for k in range(fields):
        own, gram = coeffs_and_gram(
            jnp.stack([sec_at, tm_at]), arrived[k], sec_count, time_basis, azimuth, weight, gram
        )
        coeffs.append(own)

    if own_freqs % space_count == 0:
        axes = owner_axes + ("space",)
    else:
        gram = lax.psum(gram, "space")
        axes = owner_axes
    solvers = math.prod(lax.axis_size(a) for a in axes)
    solved = NFREQ // solvers
    gram = gram.reshape((solvers, solved) + gram.shape[1:])
    gram = lax.all_to_all(gram, axes, split_axis=0, concat_axis=0, tiled=True)
    gram = jnp.sum(gram, 0).reshape(solved, blocks, orders, blocks)
    gram = jnp.transpose(gram, (3, 1, 0, 2)).reshape(blocks, blocks, solved * orders)
    basis, energy = subspace(gram, tuple(place[:MODES]), fields * cell_local * space_count)

    short = basis.astype(jnp.bfloat16).reshape(2, MODES, blocks, solved, orders)
    mixing = jnp.transpose(short, (3, 4, 1, 0, 2)).reshape(solved, orders * MODES * depth)
    energy = jnp.transpose(energy.reshape(MODES, solved, orders), (1, 2, 0)).reshape(solved, -1)
    high = energy.astype(jnp.bfloat16)
    rest = energy - high.astype(jnp.float32)
    middle = rest.astype(jnp.bfloat16)
    low = (rest - middle.astype(jnp.float32)).astype(jnp.bfloat16)
    packet = jnp.concatenate([mixing, high, middle, low], 1)
    width = -(-packet.shape[1] // LANES) * LANES
    packet = jnp.pad(packet, ((0, 0), (0, width - packet.shape[1])))
    packet = packet.reshape(1, solved, width // LANES, LANES)
    packet = jnp.broadcast_to(packet, (solvers,) + packet.shape[1:])
    packet = lax.all_to_all(packet, axes, split_axis=0, concat_axis=0, tiled=True)
    packet = packet.reshape(NFREQ, width)
    count = orders * MODES
    mixing = packet[:, :orders * MODES * depth].reshape(NFREQ, orders * MODES, depth)
    tail = packet[:, orders * MODES * depth:].astype(jnp.float32)
    energy = (tail[:, :count] + tail[:, count:2 * count]) + tail[:, 2 * count:3 * count]
    factor = lax.rsqrt(energy)
    factor = jnp.concatenate([factor, factor], 1).reshape(owners, own_freqs, orders * 2 * MODES)
    energy = energy.reshape(NFREQ, orders, MODES)
    root_weight = jnp.sqrt(weight)
    signs = jnp.array([[[1, 0], [0, -1]], [[0, 1], [1, 0]]], jnp.bfloat16)
    spread = jnp.broadcast_to(
        signs[:, :, None, :, None, None]
        * jnp.eye(blocks, dtype=jnp.bfloat16)[None, None, :, None, None, :],
        (2, 2, blocks, 2, orders, blocks),
    ).reshape(2, depth, depth * orders)

    sent = []
    before = ()
    for z, x in in_order + [(0, 0)]:
        piece = mix(
            owner_after(z, x), coeffs, mixing, spread, factor, root_weight, owners, orders, before
        )
        before = (piece,)
        sent.append((owner_after(-z, -x), send(piece, z, x)))
    mode_fields = None
    for owner, piece in sent[-1:] + sent[:-1]:
        piece = piece.reshape(fields, own_freqs, 2, orders, MODES, part)
        mode_fields = unpack(owner, piece, owners, mode_fields)
    mode_fields = jnp.transpose(mode_fields, (0, 1, 2, 4, 3, 5))
    own_energy = lax.dynamic_slice_in_dim(energy, me * own_freqs, own_freqs)
    return (mode_fields, jnp.transpose(own_energy, (1, 0, 2)))


def solution(mesh):
    placed = (P("sector", "tm", None, "space"), P(), P("space"), P())
    return jax.shard_map(
        local,
        mesh=mesh,
        in_specs=placed,
        out_specs=(
            P(None, ("sector", "tm"), None, None, None, "space"),
            P(None, ("sector", "tm"), None),
        ),
        check_vma=False,
    )
```

```python
import functools
import math

import jax
import jax.numpy as jnp
from jax import lax
from jax.experimental import pallas as pl
from jax.experimental.pallas import tpu as pltpu
from jax.sharding import PartitionSpec as P

NFFT = 64
NFREQ = 32
MODES = 8
SUBIT = 4
LANES = 128
EPSILON = 1e-06
VMEM_LIMIT = 48 * 1024 * 1024


def time_table(length, freq_count):
    steps_t = jnp.arange(length, dtype=jnp.float32)
    freq_f = jnp.arange(freq_count, dtype=jnp.float32)
    window = 0.5 - 0.5 * jnp.cos(2.0 * math.pi * steps_t / length)
    angles = 2.0 * math.pi * freq_f[:, None] * steps_t[None, :] / length
    both = jnp.stack([window * jnp.cos(angles), -window * jnp.sin(angles)])
    return (both / math.sqrt(length)).astype(jnp.bfloat16)


def order_table(orders, sectors):
    order_m = jnp.arange(orders, dtype=jnp.float32)[:, None]
    sector_s = jnp.arange(sectors, dtype=jnp.float32)[None, :]
    angles = 2.0 * math.pi * order_m * sector_s / sectors
    cosine = jnp.cos(angles)
    sine_part = jnp.sin(angles)
    upper_row = jnp.stack([cosine, sine_part], -1)
    lower_row = jnp.stack([-sine_part, cosine], -1)
    return (jnp.stack([upper_row, lower_row], 1) / math.sqrt(sectors)).astype(jnp.bfloat16)


def half_span(blocks):
    half = blocks // 2
    return half, (half - 1) * (NFFT // 2) + NFFT // 8 + NFFT


def placed_time_basis(block_start, tm_count):
    blocks = block_start.shape[0] // tm_count
    half, span = half_span(blocks)
    basis = time_table(NFFT, NFREQ)
    first = jnp.arange(blocks, dtype=jnp.int32) // half * (half * (NFFT // 2))
    inside = block_start.reshape(tm_count, blocks) - first[None, :]
    place = (
        inside[:, :, None, None] + jnp.arange(NFFT, dtype=jnp.int32)[:, None]
        == jnp.arange(span, dtype=jnp.int32)[None, :]
    ).astype(jnp.bfloat16)
    table = jnp.einsum(
        "eft,jhbtu->jhfebu",
        basis,
        place.reshape(tm_count, 2, half, NFFT, span),
        preferred_element_type=jnp.float32,
    ).astype(jnp.bfloat16)
    return table.reshape(tm_count, 2, NFREQ * 2 * half, span)


def coeff_kernel(sec_count, sec_local, freqs, orders, place_ref, time_ref, azimuth_ref, weight_ref,
                 before_ref, *refs):
    record_refs, (coeff_ref, gram_ref, spectra) = refs[:-3], refs[-3:]
    step = pl.program_id(0)
    tm_count, halves, _, span = time_ref.shape
    rec_len, columns = record_refs[0].shape[2:]
    sectors = spectra.shape[0]
    rows = spectra.shape[2] // NFREQ

    @pl.when(step < sec_local)
    def _():
        for shift in range(sec_count):
            source = lax.rem(place_ref[0] + sec_count - shift, sec_count)
            own = record_refs[shift * tm_count:(shift + 1) * tm_count]
            for h in range(halves):
                first = h * (rec_len - span) // (halves - 1)
                parts = []
                for j in range(tm_count):
                    piece = own[0][0, 0, first:first + span]
                    for x in range(1, tm_count):
                        here = lax.rem(place_ref[1] + tm_count - x, tm_count) == j
                        piece = jnp.where(here, own[x][0, 0, first:first + span], piece)
                    part = jnp.dot(time_ref[j, h], piece, preferred_element_type=jnp.float32)
                    parts.append(part.reshape(NFREQ, rows // tm_count, columns))
                joined = jnp.stack(parts, 1).reshape(NFREQ * rows, columns)
                spectra[source * sec_local + step, h] = joined.astype(jnp.bfloat16)

    @pl.when(step >= sec_local)
    def _():
        half_rows = azimuth_ref.shape[0]
        depth = half_rows // (2 * orders)
        blocks = depth * halves
        wide = orders * blocks
        row = lax.broadcasted_iota(jnp.int32, (wide, wide), 0) % blocks
        column = lax.broadcasted_iota(jnp.int32, (wide, wide), 1) % blocks
        owner = lax.broadcasted_iota(jnp.int32, (blocks, wide), 1) // blocks
        for n in range(freqs):
            at = pl.multiple_of(((step - sec_local) * freqs + n) * rows, rows)
            own = [
                spectra[:, h, pl.ds(at, rows), :].reshape(sectors * rows, columns)
                for h in range(halves)
            ]
            parts = [
                jnp.dot(azimuth_ref[...], x, preferred_element_type=jnp.float32) for x in own
            ]
            parts = [x.reshape(2 * orders, depth, columns) for x in parts]
            coeffs = jnp.stack(parts, 1).reshape(2 * wide, columns).astype(jnp.bfloat16)
            coeff_ref[n] = coeffs
            weighted = (coeffs.astype(jnp.float32) * weight_ref[...]).astype(jnp.bfloat16)
            products = lax.dot_general(
                weighted, coeffs, (((1,), (1,)), ((), ())), preferred_element_type=jnp.float32
            )
            real = products[:wide, :wide] + products[wide:, wide:]
            imag = products[:wide, wide:] - products[wide:, :wide]
            packed = jnp.where(row <= column, real, imag)
            own = packed[:blocks]
            for m in range(1, orders):
                own = jnp.where(owner == m, packed[m * blocks:(m + 1) * blocks], own)
            gram_ref[n] = before_ref[n] + own


def coeffs_and_gram(place, arrived, k, sec_count, time_basis, azimuth, weight, before):
    sec_local, _, rec_len, columns = arrived[0].shape
    sectors = sec_count * sec_local
    tm_count, halves = time_basis.shape[:2]
    blocks, wide = before.shape[1:]
    rows = azimuth.shape[1] // sectors
    steps = 4
    freqs = NFREQ // steps
    later = lambda i: jnp.maximum(i - sec_local, 0)
    early = lambda i: jnp.minimum(i, sec_local - 1)
    flops = 2 * columns * (
        sectors * time_basis.size + NFREQ * halves * azimuth.size + NFREQ * 4 * wide * wide
    )
    piece = pl.BlockSpec((1, 1, rec_len, columns), lambda i, _: (early(i), k, 0, 0))
    return pl.pallas_call(
        functools.partial(coeff_kernel, sec_count, sec_local, freqs, wide // blocks),
        grid_spec=pltpu.PrefetchScalarGridSpec(
            num_scalar_prefetch=1,
            grid=(sec_local + steps,),
            in_specs=[
                pl.BlockSpec(time_basis.shape, lambda i, _: (0, 0, 0, 0)),
                pl.BlockSpec(azimuth.shape, lambda i, _: (0, 0)),
                pl.BlockSpec(weight.shape, lambda i, _: (0, 0)),
                pl.BlockSpec((freqs, blocks, wide), lambda i, _: (later(i), 0, 0)),
            ] + [piece] * len(arrived),
            out_specs=[
                pl.BlockSpec((freqs, 2 * wide, columns), lambda i, _: (later(i), 0, 0)),
                pl.BlockSpec((freqs, blocks, wide), lambda i, _: (later(i), 0, 0)),
            ],
            scratch_shapes=[pltpu.VMEM((sectors, halves, NFREQ * rows, columns), jnp.bfloat16)],
        ),
        out_shape=[
            pltpu.HBM((NFREQ, 2 * wide, columns), jnp.bfloat16),
            jax.ShapeDtypeStruct(before.shape, jnp.float32),
        ],
        compiler_params=pltpu.CompilerParams(vmem_limit_bytes=VMEM_LIMIT),
        cost_estimate=pl.CostEstimate(
            flops=flops,
            bytes_accessed=2 * columns * (sectors * tm_count * rec_len + NFREQ * 2 * wide),
            transcendentals=0,
        ),
        name="coeffs_and_gram",
    )(place, time_basis, azimuth, weight, before, *arrived)


def subspace_kernel(cell_total, first, packed_ref, basis_ref, energy_ref):
    size, _, pairs = packed_ref.shape
    row = lax.broadcasted_iota(jnp.int32, (size, pairs), 0)
    column_re, column_im = [], []
    for q in range(size):
        down, along = packed_ref[q], packed_ref[:, q, :]
        column_re.append(jnp.where(row <= q, down, along))
        column_im.append(jnp.where(row > q, down, jnp.where(row == q, 0.0, -along)))

    def image_of(vec_re, vec_im):
        out_re, out_im = [], []
        for j in range(MODES):
            sum_re = jnp.zeros_like(column_re[0])
            sum_im = jnp.zeros_like(column_re[0])
            for q in range(size):
                at_re, at_im = vec_re[j][q:q + 1], vec_im[j][q:q + 1]
                sum_re += column_re[q] * at_re - column_im[q] * at_im
                sum_im += column_re[q] * at_im + column_im[q] * at_re
            out_re.append(sum_re)
            out_im.append(sum_im)
        return out_re, out_im

    total = lambda x: jnp.sum(x, 0, keepdims=True)
    vec_re = [column_re[q] for q in first]
    vec_im = [column_im[q] for q in first]
    for sweep in range(SUBIT):
        if sweep > 0:
            vec_re, vec_im = image_of(vec_re, vec_im)
        vec_re, vec_im = list(vec_re), list(vec_im)
        for i in range(MODES):
            scale = 1.0 / jnp.sqrt(total(vec_re[i] * vec_re[i] + vec_im[i] * vec_im[i]) + EPSILON)
            own_re, own_im = vec_re[i] * scale, vec_im[i] * scale
            vec_re[i], vec_im[i] = own_re, own_im
            for j in range(i + 1, MODES):
                proj_re = total(own_re * vec_re[j] + own_im * vec_im[j])
                proj_im = total(own_re * vec_im[j] - own_im * vec_re[j])
                vec_re[j] = vec_re[j] - (proj_re * own_re - proj_im * own_im)
                vec_im[j] = vec_im[j] - (proj_re * own_im + proj_im * own_re)
    image_re, image_im = image_of(vec_re, vec_im)
    for j in range(MODES):
        basis_ref[0, j] = vec_re[j]
        basis_ref[1, j] = vec_im[j]
        energy_ref[j:j + 1] = total(vec_re[j] * image_re[j] + vec_im[j] * image_im[j]) / cell_total


def subspace(packed, first, cell_total):
    size, _, pairs = packed.shape
    return pl.pallas_call(
        functools.partial(subspace_kernel, float(cell_total), first),
        out_shape=[
            jax.ShapeDtypeStruct((2, MODES, size, pairs), jnp.float32),
            jax.ShapeDtypeStruct((MODES, pairs), jnp.float32),
        ],
        name="subspace",
    )(packed)


def mix_kernel(orders, fields, owner_ref, mixing_ref, spread_ref, factor_ref, root_ref, *refs):
    out_ref = refs[-1]
    freqs, own_rows, _ = mixing_ref.shape
    rows = 2 * own_rows
    total = spread_ref.shape[2]
    blocks = total // (2 * orders)
    row = lax.broadcasted_iota(jnp.int32, (rows, total), 0) % own_rows // (own_rows // orders)
    column = lax.broadcasted_iota(jnp.int32, (rows, total), 1) // blocks % orders
    factor = jnp.transpose(factor_ref[0])
    for n in range(freqs):
        wide = jnp.concatenate(
            [
                jnp.dot(mixing_ref[n], spread_ref[d], preferred_element_type=jnp.float32)
                for d in range(2)
            ],
            0,
        )
        wide = jnp.where(row == column, wide, 0.0).astype(jnp.bfloat16)
        scale = factor[:, n:n + 1] * root_ref[...]
        for k in range(fields):
            mixed = jnp.dot(wide, refs[k][n], preferred_element_type=jnp.float32)
            out_ref[k, n] = (mixed * scale).astype(jnp.bfloat16)


def mix(owner, coeffs, mixing, spread, factor, root_weight, owners, orders, after):
    rows = coeffs[0].shape[1]
    own_rows, depth = mixing.shape[1:]
    out_rows = 2 * own_rows
    columns = root_weight.shape[1]
    freqs, fields = NFREQ // owners, len(coeffs)
    return pl.pallas_call(
        functools.partial(mix_kernel, orders, fields),
        grid_spec=pltpu.PrefetchScalarGridSpec(
            num_scalar_prefetch=1,
            grid=(1,),
            in_specs=[
                pl.BlockSpec((freqs, own_rows, depth), lambda i, at: (at[0], 0, 0)),
                pl.BlockSpec(spread.shape, lambda i, at: (0, 0, 0)),
                pl.BlockSpec((1, freqs, out_rows), lambda i, at: (at[0], 0, 0)),
                pl.BlockSpec(root_weight.shape, lambda i, at: (0, 0)),
            ] + [
                pl.BlockSpec((freqs, rows, x.shape[2]), lambda i, at: (at[0], 0, 0)) for x in coeffs
            ] + [pl.BlockSpec(memory_space=pl.ANY)] * len(after),
            out_specs=pl.BlockSpec((fields, freqs, out_rows, columns), lambda i, at: (0, 0, 0, 0)),
        ),
        out_shape=jax.ShapeDtypeStruct((fields, freqs, out_rows, columns), jnp.bfloat16),
        compiler_params=pltpu.CompilerParams(vmem_limit_bytes=VMEM_LIMIT),
        cost_estimate=pl.CostEstimate(
            flops=2 * freqs * out_rows * rows * fields * columns,
            bytes_accessed=2 * freqs * (rows + out_rows) * fields * columns,
            transcendentals=0,
        ),
        name="mix",
    )(jnp.reshape(owner, (1,)), mixing, spread, factor, root_weight, *coeffs, *after)


def take_kernel(place_ref, record_ref, out_ref):
    out_ref[...] = record_ref[...]


def take(by_field, first, fields, owner, owners):
    sec_local, _, rec_len, cells = by_field.shape
    count = cells // owners
    if count % LANES:
        return lax.dynamic_slice_in_dim(by_field[:, first:first + fields], owner * count, count, 3)
    shape = (sec_local, fields, rec_len, count)
    return pl.pallas_call(
        take_kernel,
        grid_spec=pltpu.PrefetchScalarGridSpec(
            num_scalar_prefetch=1,
            grid=(1,),
            in_specs=[pl.BlockSpec(shape, lambda i, at: (0, first // fields, 0, at[0]))],
            out_specs=pl.BlockSpec(shape, lambda i, at: (0, 0, 0, 0)),
        ),
        out_shape=jax.ShapeDtypeStruct(shape, by_field.dtype),
        compiler_params=pltpu.CompilerParams(vmem_limit_bytes=VMEM_LIMIT),
        cost_estimate=pl.CostEstimate(
            flops=0, bytes_accessed=4 * math.prod(shape), transcendentals=0
        ),
        name="take",
    )(jnp.reshape(owner, (1,)), by_field)


def unpack_kernel(owner_ref, piece_ref, *refs):
    out_ref = refs[-1]
    for k in range(piece_ref.shape[0]):
        for f in range(piece_ref.shape[1]):
            for d in range(piece_ref.shape[2]):
                out_ref[:, f, d, k] = piece_ref[k, f, d]


def unpack(owner, piece, owners, whole):
    fields, freqs, two, orders, modes, part = piece.shape
    shape = (orders, freqs, two, fields, modes, owners * part)
    if part % LANES:
        whole = jnp.zeros(shape, piece.dtype) if whole is None else whole
        piece = jnp.transpose(piece, (3, 1, 2, 0, 4, 5))
        return lax.dynamic_update_slice_in_dim(whole, piece, owner * part, 5)
    inputs = [piece] if whole is None else [piece, whole]
    in_specs = [
        pl.BlockSpec(piece.shape, lambda i, at: (0, 0, 0, 0, 0, 0)),
        pl.BlockSpec(memory_space=pl.ANY),
    ]
    return pl.pallas_call(
        unpack_kernel,
        grid_spec=pltpu.PrefetchScalarGridSpec(
            num_scalar_prefetch=1,
            grid=(1,),
            in_specs=in_specs[:len(inputs)],
            out_specs=pl.BlockSpec(shape[:5] + (part,), lambda i, at: (0, 0, 0, 0, 0, at[0])),
        ),
        out_shape=jax.ShapeDtypeStruct(shape, piece.dtype),
        input_output_aliases={} if whole is None else {2: 0},
        compiler_params=pltpu.CompilerParams(vmem_limit_bytes=VMEM_LIMIT),
        cost_estimate=pl.CostEstimate(flops=0, bytes_accessed=4 * piece.size, transcendentals=0),
        name="unpack",
    )(jnp.reshape(owner, (1,)), *inputs)


def local(records, block_start, slab_index, weight_table):
    sec_local, rec_len, fields, cell_local = records.shape
    sec_count = lax.axis_size("sector")
    tm_count = lax.axis_size("tm")
    space_count = lax.axis_size("space")
    owners = sec_count * tm_count
    owner_axes = ("sector", "tm")
    sectors = sec_local * sec_count
    orders = sectors // 2
    blocks = block_start.shape[0]
    depth = 2 * blocks
    part = cell_local // owners
    own_freqs = NFREQ // owners
    me = lax.axis_index("sector") * tm_count + lax.axis_index("tm")

    by_field = jnp.transpose(records, (0, 2, 1, 3))
    sec_at, tm_at = lax.axis_index("sector"), lax.axis_index("tm")
    shifts = [(z, x) for z in range(sec_count) for x in range(tm_count)]
    in_order = sorted(
        [r for r in shifts if r != (0, 0)], key=lambda r: (r[0] == 0, abs(2 * r[0] - sec_count), r)
    )

    def owner_after(z, x):
        return (sec_at + z) % sec_count * tm_count + (tm_at + x) % tm_count

    def send(piece, z, x):
        if (z, x) == (0, 0):
            return piece
        hops = [
            (a * tm_count + j, (a + z) % sec_count * tm_count + (j + x) % tm_count)
            for a in range(sec_count)
            for j in range(tm_count)
        ]
        return lax.ppermute(piece, owner_axes, hops)

    arrived = []
    for first, count in ((0, fields - 1), (fields - 1, 1)):
        got = {}
        for z, x in in_order + [(0, 0)]:
            got[z, x] = send(take(by_field, first, count, owner_after(z, x), owners), z, x)
        arrived += [([got[r] for r in shifts], k) for k in range(count)]

    time_basis = placed_time_basis(block_start, tm_count)
    half, _ = half_span(blocks // tm_count)
    halves = blocks // tm_count // half
    azimuth = jnp.einsum(
        "mcse,ij,bd->cmibsjed",
        order_table(orders, sectors),
        jnp.eye(tm_count, dtype=jnp.bfloat16),
        jnp.eye(half, dtype=jnp.bfloat16),
    ).reshape(2 * orders * tm_count * half, sectors * tm_count * 2 * half)
    place = [
        (b // half % halves * tm_count + b // (half * halves)) * half + b % half
        for b in range(blocks)
    ]
    own_slab = lax.dynamic_slice_in_dim(slab_index, me * part, part)
    weight = jnp.sum(
        jnp.where(
            own_slab[None, :] == jnp.arange(weight_table.shape[0], dtype=jnp.int32)[:, None],
            weight_table[:, None],
            0.0,
        ),
        0,
        keepdims=True,
    )

    gram = jnp.zeros((NFREQ, blocks, orders * blocks), jnp.float32)

    coeffs = []
    for k in range(fields):
        own, gram = coeffs_and_gram(
            jnp.stack([sec_at, tm_at]), *arrived[k], sec_count, time_basis, azimuth, weight, gram
        )
        coeffs.append(own)

    if own_freqs % space_count == 0:
        axes = owner_axes + ("space",)
    else:
        gram = lax.psum(gram, "space")
        axes = owner_axes
    solvers = math.prod(lax.axis_size(a) for a in axes)
    solved = NFREQ // solvers
    gram = gram.reshape((solvers, solved) + gram.shape[1:])
    gram = lax.all_to_all(gram, axes, split_axis=0, concat_axis=0, tiled=True)
    gram = jnp.sum(gram, 0).reshape(solved, blocks, orders, blocks)
    gram = jnp.transpose(gram, (3, 1, 0, 2)).reshape(blocks, blocks, solved * orders)
    basis, energy = subspace(gram, tuple(place[:MODES]), fields * cell_local * space_count)

    short = basis.astype(jnp.bfloat16).reshape(2, MODES, blocks, solved, orders)
    mixing = jnp.transpose(short, (3, 4, 1, 0, 2)).reshape(solved, orders * MODES * depth)
    energy = jnp.transpose(energy.reshape(MODES, solved, orders), (1, 2, 0)).reshape(solved, -1)
    high = energy.astype(jnp.bfloat16)
    rest = energy - high.astype(jnp.float32)
    middle = rest.astype(jnp.bfloat16)
    low = (rest - middle.astype(jnp.float32)).astype(jnp.bfloat16)
    packet = jnp.concatenate([mixing, high, middle, low], 1)
    width = -(-packet.shape[1] // LANES) * LANES
    packet = jnp.pad(packet, ((0, 0), (0, width - packet.shape[1])))
    packet = packet.reshape(1, solved, width // LANES, LANES)
    packet = jnp.broadcast_to(packet, (solvers,) + packet.shape[1:])
    packet = lax.all_to_all(packet, axes, split_axis=0, concat_axis=0, tiled=True)
    packet = packet.reshape(NFREQ, width)
    count = orders * MODES
    mixing = packet[:, :orders * MODES * depth].reshape(NFREQ, orders * MODES, depth)
    tail = packet[:, orders * MODES * depth:].astype(jnp.float32)
    energy = (tail[:, :count] + tail[:, count:2 * count]) + tail[:, 2 * count:3 * count]
    factor = lax.rsqrt(energy)
    factor = jnp.concatenate([factor, factor], 1).reshape(owners, own_freqs, orders * 2 * MODES)
    energy = energy.reshape(NFREQ, orders, MODES)
    root_weight = jnp.sqrt(weight)
    signs = jnp.array([[[1, 0], [0, -1]], [[0, 1], [1, 0]]], jnp.bfloat16)
    spread = jnp.broadcast_to(
        signs[:, :, None, :, None, None]
        * jnp.eye(blocks, dtype=jnp.bfloat16)[None, None, :, None, None, :],
        (2, 2, blocks, 2, orders, blocks),
    ).reshape(2, depth, depth * orders)

    sent = []
    before = ()
    for z, x in in_order + [(0, 0)]:
        piece = mix(
            owner_after(z, x), coeffs, mixing, spread, factor, root_weight, owners, orders, before
        )
        before = (piece,)
        sent.append((owner_after(-z, -x), send(piece, z, x)))
    mode_fields = None
    for owner, piece in sent[-1:] + sent[:-1]:
        piece = piece.reshape(fields, own_freqs, 2, orders, MODES, part)
        mode_fields = unpack(owner, piece, owners, mode_fields)
    mode_fields = jnp.transpose(mode_fields, (0, 1, 2, 4, 3, 5))
    own_energy = lax.dynamic_slice_in_dim(energy, me * own_freqs, own_freqs)
    return (mode_fields, jnp.transpose(own_energy, (1, 0, 2)))


def solution(mesh):
    placed = (P("sector", "tm", None, "space"), P(), P("space"), P())
    return jax.shard_map(
        local,
        mesh=mesh,
        in_specs=placed,
        out_specs=(
            P(None, ("sector", "tm"), None, None, None, "space"),
            P(None, ("sector", "tm"), None),
        ),
        check_vma=False,
    )
```

```python
import functools
import math

import jax
import jax.numpy as jnp
from jax import lax
from jax.experimental import pallas as pl
from jax.experimental.pallas import tpu as pltpu
from jax.sharding import PartitionSpec as P

NFFT = 64
NFREQ = 32
MODES = 8
SUBIT = 4
LANES = 128
EPSILON = 1e-06
VMEM_LIMIT = 48 * 1024 * 1024


def time_table(length, freq_count):
    steps_t = jnp.arange(length, dtype=jnp.float32)
    freq_f = jnp.arange(freq_count, dtype=jnp.float32)
    window = 0.5 - 0.5 * jnp.cos(2.0 * math.pi * steps_t / length)
    angles = 2.0 * math.pi * freq_f[:, None] * steps_t[None, :] / length
    both = jnp.stack([window * jnp.cos(angles), -window * jnp.sin(angles)])
    return (both / math.sqrt(length)).astype(jnp.bfloat16)


def order_table(orders, sectors):
    order_m = jnp.arange(orders, dtype=jnp.float32)[:, None]
    sector_s = jnp.arange(sectors, dtype=jnp.float32)[None, :]
    angles = 2.0 * math.pi * order_m * sector_s / sectors
    cosine = jnp.cos(angles)
    sine_part = jnp.sin(angles)
    upper_row = jnp.stack([cosine, sine_part], -1)
    lower_row = jnp.stack([-sine_part, cosine], -1)
    return (jnp.stack([upper_row, lower_row], 1) / math.sqrt(sectors)).astype(jnp.bfloat16)


def half_span(blocks):
    half = blocks // 2
    return half, (half - 1) * (NFFT // 2) + NFFT // 8 + NFFT


def placed_time_basis(block_start, tm_count):
    blocks = block_start.shape[0] // tm_count
    half, span = half_span(blocks)
    basis = time_table(NFFT, NFREQ)
    first = jnp.arange(blocks, dtype=jnp.int32) // half * (half * (NFFT // 2))
    inside = block_start.reshape(tm_count, blocks) - first[None, :]
    place = (
        inside[:, :, None, None] + jnp.arange(NFFT, dtype=jnp.int32)[:, None]
        == jnp.arange(span, dtype=jnp.int32)[None, :]
    ).astype(jnp.bfloat16)
    table = jnp.einsum(
        "eft,jhbtu->jhfebu",
        basis,
        place.reshape(tm_count, 2, half, NFFT, span),
        preferred_element_type=jnp.float32,
    ).astype(jnp.bfloat16)
    return table.reshape(tm_count, 2, NFREQ * 2 * half, span)


def coeff_kernel(sec_count, sec_local, freqs, orders, place_ref, time_ref, azimuth_ref, weight_ref,
                 before_ref, *refs):
    record_refs, (coeff_ref, gram_ref, spectra) = refs[:-3], refs[-3:]
    step = pl.program_id(0)
    tm_count, halves, _, span = time_ref.shape
    rec_len, columns = record_refs[0].shape[1:]
    sectors = spectra.shape[0]
    rows = spectra.shape[2] // NFREQ

    @pl.when(step < sec_local)
    def _():
        for shift in range(sec_count):
            source = lax.rem(place_ref[0] + sec_count - shift, sec_count)
            own = record_refs[shift * tm_count:(shift + 1) * tm_count]
            for h in range(halves):
                first = h * (rec_len - span) // (halves - 1)
                parts = []
                for j in range(tm_count):
                    piece = own[0][0, first:first + span]
                    for x in range(1, tm_count):
                        here = lax.rem(place_ref[1] + tm_count - x, tm_count) == j
                        piece = jnp.where(here, own[x][0, first:first + span], piece)
                    part = jnp.dot(time_ref[j, h], piece, preferred_element_type=jnp.float32)
                    parts.append(part.reshape(NFREQ, rows // tm_count, columns))
                joined = jnp.stack(parts, 1).reshape(NFREQ * rows, columns)
                spectra[source * sec_local + step, h] = joined.astype(jnp.bfloat16)

    @pl.when(step >= sec_local)
    def _():
        half_rows = azimuth_ref.shape[0]
        depth = half_rows // (2 * orders)
        blocks = depth * halves
        wide = orders * blocks
        row = lax.broadcasted_iota(jnp.int32, (wide, wide), 0) % blocks
        column = lax.broadcasted_iota(jnp.int32, (wide, wide), 1) % blocks
        owner = lax.broadcasted_iota(jnp.int32, (blocks, wide), 1) // blocks
        for n in range(freqs):
            at = pl.multiple_of(((step - sec_local) * freqs + n) * rows, rows)
            own = [
                spectra[:, h, pl.ds(at, rows), :].reshape(sectors * rows, columns)
                for h in range(halves)
            ]
            parts = [
                jnp.dot(azimuth_ref[...], x, preferred_element_type=jnp.float32) for x in own
            ]
            parts = [x.reshape(2 * orders, depth, columns) for x in parts]
            coeffs = jnp.stack(parts, 1).reshape(2 * wide, columns).astype(jnp.bfloat16)
            coeff_ref[n] = coeffs
            weighted = (coeffs.astype(jnp.float32) * weight_ref[...]).astype(jnp.bfloat16)
            products = lax.dot_general(
                weighted, coeffs, (((1,), (1,)), ((), ())), preferred_element_type=jnp.float32
            )
            real = products[:wide, :wide] + products[wide:, wide:]
            imag = products[:wide, wide:] - products[wide:, :wide]
            packed = jnp.where(row <= column, real, imag)
            own = packed[:blocks]
            for m in range(1, orders):
                own = jnp.where(owner == m, packed[m * blocks:(m + 1) * blocks], own)
            gram_ref[n] = before_ref[n] + own


def coeffs_and_gram(place, arrived, sec_count, time_basis, azimuth, weight, before):
    sec_local, rec_len, columns = arrived[0].shape
    sectors = sec_count * sec_local
    halves = time_basis.shape[1]
    blocks, wide = before.shape[1:]
    rows = azimuth.shape[1] // sectors
    steps = 4
    freqs = NFREQ // steps
    later = lambda i: jnp.maximum(i - sec_local, 0)
    early = lambda i: jnp.minimum(i, sec_local - 1)
    flops = 2 * columns * (
        sectors * time_basis.size + NFREQ * halves * azimuth.size + NFREQ * 4 * wide * wide
    )
    piece = pl.BlockSpec((1, rec_len, columns), lambda i, _: (early(i), 0, 0))
    return pl.pallas_call(
        functools.partial(coeff_kernel, sec_count, sec_local, freqs, wide // blocks),
        grid_spec=pltpu.PrefetchScalarGridSpec(
            num_scalar_prefetch=1,
            grid=(sec_local + steps,),
            in_specs=[
                pl.BlockSpec(time_basis.shape, lambda i, _: (0, 0, 0, 0)),
                pl.BlockSpec(azimuth.shape, lambda i, _: (0, 0)),
                pl.BlockSpec(weight.shape, lambda i, _: (0, 0)),
                pl.BlockSpec((freqs, blocks, wide), lambda i, _: (later(i), 0, 0)),
            ] + [piece] * len(arrived),
            out_specs=[
                pl.BlockSpec((freqs, 2 * wide, columns), lambda i, _: (later(i), 0, 0)),
                pl.BlockSpec((freqs, blocks, wide), lambda i, _: (later(i), 0, 0)),
            ],
            scratch_shapes=[pltpu.VMEM((sectors, halves, NFREQ * rows, columns), jnp.bfloat16)],
        ),
        out_shape=[
            jax.ShapeDtypeStruct((NFREQ, 2 * wide, columns), jnp.bfloat16),
            jax.ShapeDtypeStruct(before.shape, jnp.float32),
        ],
        compiler_params=pltpu.CompilerParams(vmem_limit_bytes=VMEM_LIMIT),
        cost_estimate=pl.CostEstimate(
            flops=flops,
            bytes_accessed=2 * (len(arrived) * arrived[0].size + NFREQ * 2 * wide * columns),
            transcendentals=0,
        ),
        name="coeffs_and_gram",
    )(place, time_basis, azimuth, weight, before, *arrived)


def subspace_kernel(cell_total, first, packed_ref, basis_ref, energy_ref):
    size, _, pairs = packed_ref.shape
    row = lax.broadcasted_iota(jnp.int32, (size, pairs), 0)
    column_re, column_im = [], []
    for q in range(size):
        down, along = packed_ref[q], packed_ref[:, q, :]
        column_re.append(jnp.where(row <= q, down, along))
        column_im.append(jnp.where(row > q, down, jnp.where(row == q, 0.0, -along)))

    def image_of(vec_re, vec_im):
        out_re, out_im = [], []
        for j in range(MODES):
            sum_re = jnp.zeros_like(column_re[0])
            sum_im = jnp.zeros_like(column_re[0])
            for q in range(size):
                at_re, at_im = vec_re[j][q:q + 1], vec_im[j][q:q + 1]
                sum_re += column_re[q] * at_re - column_im[q] * at_im
                sum_im += column_re[q] * at_im + column_im[q] * at_re
            out_re.append(sum_re)
            out_im.append(sum_im)
        return out_re, out_im

    total = lambda x: jnp.sum(x, 0, keepdims=True)
    vec_re = [column_re[q] for q in first]
    vec_im = [column_im[q] for q in first]
    for sweep in range(SUBIT):
        if sweep > 0:
            vec_re, vec_im = image_of(vec_re, vec_im)
        vec_re, vec_im = list(vec_re), list(vec_im)
        for i in range(MODES):
            scale = 1.0 / jnp.sqrt(total(vec_re[i] * vec_re[i] + vec_im[i] * vec_im[i]) + EPSILON)
            own_re, own_im = vec_re[i] * scale, vec_im[i] * scale
            vec_re[i], vec_im[i] = own_re, own_im
            for j in range(i + 1, MODES):
                proj_re = total(own_re * vec_re[j] + own_im * vec_im[j])
                proj_im = total(own_re * vec_im[j] - own_im * vec_re[j])
                vec_re[j] = vec_re[j] - (proj_re * own_re - proj_im * own_im)
                vec_im[j] = vec_im[j] - (proj_re * own_im + proj_im * own_re)
    image_re, image_im = image_of(vec_re, vec_im)
    for j in range(MODES):
        basis_ref[0, j] = vec_re[j]
        basis_ref[1, j] = vec_im[j]
        energy_ref[j:j + 1] = total(vec_re[j] * image_re[j] + vec_im[j] * image_im[j]) / cell_total


def subspace(packed, first, cell_total):
    size, _, pairs = packed.shape
    return pl.pallas_call(
        functools.partial(subspace_kernel, float(cell_total), first),
        out_shape=[
            jax.ShapeDtypeStruct((2, MODES, size, pairs), jnp.float32),
            jax.ShapeDtypeStruct((MODES, pairs), jnp.float32),
        ],
        name="subspace",
    )(packed)


def mix_kernel(orders, fields, owner_ref, mixing_ref, spread_ref, factor_ref, root_ref, *refs):
    out_ref = refs[-1]
    freqs, own_rows, _ = mixing_ref.shape
    rows = 2 * own_rows
    total = spread_ref.shape[2]
    blocks = total // (2 * orders)
    row = lax.broadcasted_iota(jnp.int32, (rows, total), 0) % own_rows // (own_rows // orders)
    column = lax.broadcasted_iota(jnp.int32, (rows, total), 1) // blocks % orders
    factor = jnp.transpose(factor_ref[0])
    for n in range(freqs):
        wide = jnp.concatenate(
            [
                jnp.dot(mixing_ref[n], spread_ref[d], preferred_element_type=jnp.float32)
                for d in range(2)
            ],
            0,
        )
        wide = jnp.where(row == column, wide, 0.0).astype(jnp.bfloat16)
        scale = factor[:, n:n + 1] * root_ref[...]
        for k in range(fields):
            mixed = jnp.dot(wide, refs[k][n], preferred_element_type=jnp.float32)
            out_ref[k, n] = (mixed * scale).astype(jnp.bfloat16)


def mix(owner, coeffs, mixing, spread, factor, root_weight, owners, orders, after):
    rows = coeffs[0].shape[1]
    own_rows, depth = mixing.shape[1:]
    out_rows = 2 * own_rows
    columns = root_weight.shape[1]
    freqs, fields = NFREQ // owners, len(coeffs)
    return pl.pallas_call(
        functools.partial(mix_kernel, orders, fields),
        grid_spec=pltpu.PrefetchScalarGridSpec(
            num_scalar_prefetch=1,
            grid=(1,),
            in_specs=[
                pl.BlockSpec((freqs, own_rows, depth), lambda i, at: (at[0], 0, 0)),
                pl.BlockSpec(spread.shape, lambda i, at: (0, 0, 0)),
                pl.BlockSpec((1, freqs, out_rows), lambda i, at: (at[0], 0, 0)),
                pl.BlockSpec(root_weight.shape, lambda i, at: (0, 0)),
            ] + [
                pl.BlockSpec((freqs, rows, x.shape[2]), lambda i, at: (at[0], 0, 0)) for x in coeffs
            ] + [pl.BlockSpec(memory_space=pl.ANY)] * len(after),
            out_specs=pl.BlockSpec((fields, freqs, out_rows, columns), lambda i, at: (0, 0, 0, 0)),
        ),
        out_shape=jax.ShapeDtypeStruct((fields, freqs, out_rows, columns), jnp.bfloat16),
        compiler_params=pltpu.CompilerParams(vmem_limit_bytes=VMEM_LIMIT),
        cost_estimate=pl.CostEstimate(
            flops=2 * freqs * out_rows * rows * fields * columns,
            bytes_accessed=2 * freqs * (rows + out_rows) * fields * columns,
            transcendentals=0,
        ),
        name="mix",
    )(jnp.reshape(owner, (1,)), mixing, spread, factor, root_weight, *coeffs, *after)


def take_kernel(place_ref, record_ref, out_ref):
    out_ref[...] = record_ref[:, 0]


def take(by_field, k, owner, owners):
    sec_local, _, rec_len, cells = by_field.shape
    count = cells // owners
    if count % LANES:
        return lax.dynamic_slice_in_dim(by_field[:, k], owner * count, count, 2)
    return pl.pallas_call(
        take_kernel,
        grid_spec=pltpu.PrefetchScalarGridSpec(
            num_scalar_prefetch=1,
            grid=(1,),
            in_specs=[
                pl.BlockSpec((sec_local, 1, rec_len, count), lambda i, at: (0, k, 0, at[0]))
            ],
            out_specs=pl.BlockSpec((sec_local, rec_len, count), lambda i, at: (0, 0, 0)),
        ),
        out_shape=jax.ShapeDtypeStruct((sec_local, rec_len, count), by_field.dtype),
        compiler_params=pltpu.CompilerParams(vmem_limit_bytes=VMEM_LIMIT),
        cost_estimate=pl.CostEstimate(
            flops=0, bytes_accessed=4 * sec_local * rec_len * count, transcendentals=0
        ),
        name="take",
    )(jnp.reshape(owner, (1,)), by_field)


def unpack_kernel(owner_ref, piece_ref, *refs):
    out_ref = refs[-1]
    for k in range(piece_ref.shape[0]):
        for d in range(piece_ref.shape[2]):
            out_ref[:, 0, d, k] = piece_ref[k, 0, d]


def unpack(owner, piece, owners, whole):
    fields, freqs, two, orders, modes, part = piece.shape
    shape = (orders, freqs, two, fields, modes, owners * part)
    if part % LANES:
        whole = jnp.zeros(shape, piece.dtype) if whole is None else whole
        piece = jnp.transpose(piece, (3, 1, 2, 0, 4, 5))
        return lax.dynamic_update_slice_in_dim(whole, piece, owner * part, 5)
    inputs = [piece] if whole is None else [piece, whole]
    in_specs = [
        pl.BlockSpec((fields, 1) + piece.shape[2:], lambda i, at: (0, i, 0, 0, 0, 0)),
        pl.BlockSpec(memory_space=pl.ANY),
    ]
    return pl.pallas_call(
        unpack_kernel,
        grid_spec=pltpu.PrefetchScalarGridSpec(
            num_scalar_prefetch=1,
            grid=(freqs,),
            in_specs=in_specs[:len(inputs)],
            out_specs=pl.BlockSpec(
                (orders, 1) + shape[2:5] + (part,), lambda i, at: (0, i, 0, 0, 0, at[0])
            ),
        ),
        out_shape=jax.ShapeDtypeStruct(shape, piece.dtype),
        input_output_aliases={} if whole is None else {2: 0},
        compiler_params=pltpu.CompilerParams(vmem_limit_bytes=VMEM_LIMIT),
        cost_estimate=pl.CostEstimate(flops=0, bytes_accessed=4 * piece.size, transcendentals=0),
        name="unpack",
    )(jnp.reshape(owner, (1,)), *inputs)


def local(records, block_start, slab_index, weight_table):
    sec_local, rec_len, fields, cell_local = records.shape
    sec_count = lax.axis_size("sector")
    tm_count = lax.axis_size("tm")
    space_count = lax.axis_size("space")
    owners = sec_count * tm_count
    owner_axes = ("sector", "tm")
    sectors = sec_local * sec_count
    orders = sectors // 2
    blocks = block_start.shape[0]
    depth = 2 * blocks
    part = cell_local // owners
    own_freqs = NFREQ // owners
    me = lax.axis_index("sector") * tm_count + lax.axis_index("tm")

    by_field = jnp.transpose(records, (0, 2, 1, 3))
    sec_at, tm_at = lax.axis_index("sector"), lax.axis_index("tm")
    shifts = [(z, x) for z in range(sec_count) for x in range(tm_count)]
    in_order = sorted(
        [r for r in shifts if r != (0, 0)], key=lambda r: (r[0] == 0, abs(2 * r[0] - sec_count), r)
    )

    def owner_after(z, x):
        return (sec_at + z) % sec_count * tm_count + (tm_at + x) % tm_count

    def send(piece, z, x):
        if (z, x) == (0, 0):
            return piece
        hops = [
            (a * tm_count + j, (a + z) % sec_count * tm_count + (j + x) % tm_count)
            for a in range(sec_count)
            for j in range(tm_count)
        ]
        return lax.ppermute(piece, owner_axes, hops)

    arrived = []
    for k in range(fields):
        got = {r: send(take(by_field, k, owner_after(*r), owners), *r) for r in in_order + [(0, 0)]}
        arrived.append([got[r] for r in shifts])

    time_basis = placed_time_basis(block_start, tm_count)
    half, _ = half_span(blocks // tm_count)
    halves = blocks // tm_count // half
    azimuth = jnp.einsum(
        "mcse,ij,bd->cmibsjed",
        order_table(orders, sectors),
        jnp.eye(tm_count, dtype=jnp.bfloat16),
        jnp.eye(half, dtype=jnp.bfloat16),
    ).reshape(2 * orders * tm_count * half, sectors * tm_count * 2 * half)
    place = [
        (b // half % halves * tm_count + b // (half * halves)) * half + b % half
        for b in range(blocks)
    ]
    own_slab = lax.dynamic_slice_in_dim(slab_index, me * part, part)
    weight = jnp.sum(
        jnp.where(
            own_slab[None, :] == jnp.arange(weight_table.shape[0], dtype=jnp.int32)[:, None],
            weight_table[:, None],
            0.0,
        ),
        0,
        keepdims=True,
    )

    gram = jnp.zeros((NFREQ, blocks, orders * blocks), jnp.float32)

    coeffs = []
    for k in range(fields):
        own, gram = coeffs_and_gram(
            jnp.stack([sec_at, tm_at]), arrived[k], sec_count, time_basis, azimuth, weight, gram
        )
        coeffs.append(own)

    if own_freqs % space_count == 0:
        axes = owner_axes + ("space",)
    else:
        gram = lax.psum(gram, "space")
        axes = owner_axes
    solvers = math.prod(lax.axis_size(a) for a in axes)
    solved = NFREQ // solvers
    gram = gram.reshape((solvers, solved) + gram.shape[1:])
    gram = lax.all_to_all(gram, axes, split_axis=0, concat_axis=0, tiled=True)
    gram = jnp.sum(gram, 0).reshape(solved, blocks, orders, blocks)
    gram = jnp.transpose(gram, (3, 1, 0, 2)).reshape(blocks, blocks, solved * orders)
    basis, energy = subspace(gram, tuple(place[:MODES]), fields * cell_local * space_count)

    short = basis.astype(jnp.bfloat16).reshape(2, MODES, blocks, solved, orders)
    mixing = jnp.transpose(short, (3, 4, 1, 0, 2)).reshape(solved, orders * MODES * depth)
    energy = jnp.transpose(energy.reshape(MODES, solved, orders), (1, 2, 0)).reshape(solved, -1)
    high = energy.astype(jnp.bfloat16)
    rest = energy - high.astype(jnp.float32)
    middle = rest.astype(jnp.bfloat16)
    low = (rest - middle.astype(jnp.float32)).astype(jnp.bfloat16)
    packet = jnp.concatenate([mixing, high, middle, low], 1)
    width = -(-packet.shape[1] // LANES) * LANES
    packet = jnp.pad(packet, ((0, 0), (0, width - packet.shape[1])))
    packet = packet.reshape(1, solved, width // LANES, LANES)
    packet = jnp.broadcast_to(packet, (solvers,) + packet.shape[1:])
    packet = lax.all_to_all(packet, axes, split_axis=0, concat_axis=0, tiled=True)
    packet = packet.reshape(NFREQ, width)
    count = orders * MODES
    mixing = packet[:, :orders * MODES * depth].reshape(NFREQ, orders * MODES, depth)
    tail = packet[:, orders * MODES * depth:].astype(jnp.float32)
    energy = (tail[:, :count] + tail[:, count:2 * count]) + tail[:, 2 * count:3 * count]
    factor = lax.rsqrt(energy)
    factor = jnp.concatenate([factor, factor], 1).reshape(owners, own_freqs, orders * 2 * MODES)
    energy = energy.reshape(NFREQ, orders, MODES)
    root_weight = jnp.sqrt(weight)
    signs = jnp.array([[[1, 0], [0, -1]], [[0, 1], [1, 0]]], jnp.bfloat16)
    spread = jnp.broadcast_to(
        signs[:, :, None, :, None, None]
        * jnp.eye(blocks, dtype=jnp.bfloat16)[None, None, :, None, None, :],
        (2, 2, blocks, 2, orders, blocks),
    ).reshape(2, depth, depth * orders)

    coeffs = [pltpu.with_memory_space_constraint(x, pltpu.HBM) for x in coeffs]
    sent = {}
    before = ()
    for z, x in in_order + [(0, 0)]:
        piece = mix(
            owner_after(z, x), coeffs, mixing, spread, factor, root_weight, owners, orders, before
        )
        before = (piece,)
        sent[z, x] = owner_after(-z, -x), send(piece, z, x)
    mode_fields = None
    for r in sorted(sent, key=lambda r: (r != (0, 0), r[0] == 0, r[0] == 1, in_order.index(r) if r in in_order else 0)):
        owner, piece = sent[r]
        piece = piece.reshape(fields, own_freqs, 2, orders, MODES, part)
        mode_fields = unpack(owner, piece, owners, mode_fields)
    mode_fields = jnp.transpose(mode_fields, (0, 1, 2, 4, 3, 5))
    own_energy = lax.dynamic_slice_in_dim(energy, me * own_freqs, own_freqs)
    return (mode_fields, jnp.transpose(own_energy, (1, 0, 2)))


def solution(mesh):
    placed = (P("sector", "tm", None, "space"), P(), P("space"), P())
    return jax.shard_map(
        local,
        mesh=mesh,
        in_specs=placed,
        out_specs=(
            P(None, ("sector", "tm"), None, None, None, "space"),
            P(None, ("sector", "tm"), None),
        ),
        check_vma=False,
    )
```

```python
import functools
import math

import jax
import jax.numpy as jnp
from jax import lax
from jax.experimental import pallas as pl
from jax.experimental.pallas import tpu as pltpu
from jax.sharding import PartitionSpec as P

NFFT = 64
NFREQ = 32
MODES = 8
SUBIT = 4
LANES = 128
EPSILON = 1e-06
VMEM_LIMIT = 48 * 1024 * 1024


def time_table(length, freq_count):
    steps_t = jnp.arange(length, dtype=jnp.float32)
    freq_f = jnp.arange(freq_count, dtype=jnp.float32)
    window = 0.5 - 0.5 * jnp.cos(2.0 * math.pi * steps_t / length)
    angles = 2.0 * math.pi * freq_f[:, None] * steps_t[None, :] / length
    both = jnp.stack([window * jnp.cos(angles), -window * jnp.sin(angles)])
    return (both / math.sqrt(length)).astype(jnp.bfloat16)


def order_table(orders, sectors):
    order_m = jnp.arange(orders, dtype=jnp.float32)[:, None]
    sector_s = jnp.arange(sectors, dtype=jnp.float32)[None, :]
    angles = 2.0 * math.pi * order_m * sector_s / sectors
    cosine = jnp.cos(angles)
    sine_part = jnp.sin(angles)
    upper_row = jnp.stack([cosine, sine_part], -1)
    lower_row = jnp.stack([-sine_part, cosine], -1)
    return (jnp.stack([upper_row, lower_row], 1) / math.sqrt(sectors)).astype(jnp.bfloat16)


def half_span(blocks):
    half = blocks // 2
    return half, (half - 1) * (NFFT // 2) + NFFT // 8 + NFFT


def placed_time_basis(block_start, tm_count):
    blocks = block_start.shape[0] // tm_count
    half, span = half_span(blocks)
    basis = time_table(NFFT, NFREQ)
    first = jnp.arange(blocks, dtype=jnp.int32) // half * (half * (NFFT // 2))
    inside = block_start.reshape(tm_count, blocks) - first[None, :]
    place = (
        inside[:, :, None, None] + jnp.arange(NFFT, dtype=jnp.int32)[:, None]
        == jnp.arange(span, dtype=jnp.int32)[None, :]
    ).astype(jnp.bfloat16)
    table = jnp.einsum(
        "eft,jhbtu->jhfebu",
        basis,
        place.reshape(tm_count, 2, half, NFFT, span),
        preferred_element_type=jnp.float32,
    ).astype(jnp.bfloat16)
    return table.reshape(tm_count, 2, NFREQ * 2 * half, span)


def coeff_kernel(sec_count, sec_local, freqs, orders, place_ref, time_ref, azimuth_ref, weight_ref,
                 before_ref, *refs):
    record_refs, (coeff_ref, gram_ref, spectra) = refs[:-3], refs[-3:]
    step = pl.program_id(0)
    tm_count, halves, _, span = time_ref.shape
    rec_len, columns = record_refs[0].shape[2:]
    sectors = spectra.shape[0]
    rows = spectra.shape[2] // NFREQ

    @pl.when(step < sec_local)
    def _():
        for shift in range(sec_count):
            source = lax.rem(place_ref[0] + sec_count - shift, sec_count)
            own = record_refs[shift * tm_count:(shift + 1) * tm_count]
            for h in range(halves):
                first = h * (rec_len - span) // (halves - 1)
                parts = []
                for j in range(tm_count):
                    piece = own[0][0, 0, first:first + span]
                    for x in range(1, tm_count):
                        here = lax.rem(place_ref[1] + tm_count - x, tm_count) == j
                        piece = jnp.where(here, own[x][0, 0, first:first + span], piece)
                    part = jnp.dot(time_ref[j, h], piece, preferred_element_type=jnp.float32)
                    parts.append(part.reshape(NFREQ, rows // tm_count, columns))
                joined = jnp.stack(parts, 1).reshape(NFREQ * rows, columns)
                spectra[source * sec_local + step, h] = joined.astype(jnp.bfloat16)

    @pl.when(step >= sec_local)
    def _():
        half_rows = azimuth_ref.shape[0]
        depth = half_rows // (2 * orders)
        blocks = depth * halves
        wide = orders * blocks
        row = lax.broadcasted_iota(jnp.int32, (wide, wide), 0) % blocks
        column = lax.broadcasted_iota(jnp.int32, (wide, wide), 1) % blocks
        owner = lax.broadcasted_iota(jnp.int32, (blocks, wide), 1) // blocks
        for n in range(freqs):
            at = pl.multiple_of(((step - sec_local) * freqs + n) * rows, rows)
            own = [
                spectra[:, h, pl.ds(at, rows), :].reshape(sectors * rows, columns)
                for h in range(halves)
            ]
            parts = [
                jnp.dot(azimuth_ref[...], x, preferred_element_type=jnp.float32) for x in own
            ]
            parts = [x.reshape(2 * orders, depth, columns) for x in parts]
            coeffs = jnp.stack(parts, 1).reshape(2 * wide, columns).astype(jnp.bfloat16)
            coeff_ref[n] = coeffs
            weighted = (coeffs.astype(jnp.float32) * weight_ref[...]).astype(jnp.bfloat16)
            products = lax.dot_general(
                weighted, coeffs, (((1,), (1,)), ((), ())), preferred_element_type=jnp.float32
            )
            real = products[:wide, :wide] + products[wide:, wide:]
            imag = products[:wide, wide:] - products[wide:, :wide]
            packed = jnp.where(row <= column, real, imag)
            own = packed[:blocks]
            for m in range(1, orders):
                own = jnp.where(owner == m, packed[m * blocks:(m + 1) * blocks], own)
            gram_ref[n] = before_ref[n] + own


def coeffs_and_gram(place, arrived, sec_count, time_basis, azimuth, weight, before):
    senders, sec_local, rec_len, columns = arrived[0].shape
    sectors = sec_count * sec_local
    tm_count, halves = time_basis.shape[:2]
    blocks, wide = before.shape[1:]
    rows = azimuth.shape[1] // sectors
    steps = 4
    freqs = NFREQ // steps
    later = lambda i: jnp.maximum(i - sec_local, 0)
    early = lambda i: jnp.minimum(i, sec_local - 1)
    flops = 2 * columns * (
        sectors * time_basis.size + NFREQ * halves * azimuth.size + NFREQ * 4 * wide * wide
    )

    def piece(z, x):
        def index(i, place):
            sender = lax.rem(place[0] + sec_count - z, sec_count) * tm_count
            sender += lax.rem(place[1] + tm_count - x, tm_count)
            return (sender if senders > 1 else 0, early(i), 0, 0)

        return pl.BlockSpec((1, 1, rec_len, columns), index)

    pieces = [piece(z, x) for z in range(sec_count) for x in range(tm_count)]
    if senders > 1:
        arrived = arrived * len(pieces)
    return pl.pallas_call(
        functools.partial(coeff_kernel, sec_count, sec_local, freqs, wide // blocks),
        grid_spec=pltpu.PrefetchScalarGridSpec(
            num_scalar_prefetch=1,
            grid=(sec_local + steps,),
            in_specs=[
                pl.BlockSpec(time_basis.shape, lambda i, _: (0, 0, 0, 0)),
                pl.BlockSpec(azimuth.shape, lambda i, _: (0, 0)),
                pl.BlockSpec(weight.shape, lambda i, _: (0, 0)),
                pl.BlockSpec((freqs, blocks, wide), lambda i, _: (later(i), 0, 0)),
            ] + pieces,
            out_specs=[
                pl.BlockSpec((freqs, 2 * wide, columns), lambda i, _: (later(i), 0, 0)),
                pl.BlockSpec((freqs, blocks, wide), lambda i, _: (later(i), 0, 0)),
            ],
            scratch_shapes=[pltpu.VMEM((sectors, halves, NFREQ * rows, columns), jnp.bfloat16)],
        ),
        out_shape=[
            jax.ShapeDtypeStruct((NFREQ, 2 * wide, columns), jnp.bfloat16),
            jax.ShapeDtypeStruct(before.shape, jnp.float32),
        ],
        compiler_params=pltpu.CompilerParams(vmem_limit_bytes=VMEM_LIMIT),
        cost_estimate=pl.CostEstimate(
            flops=flops,
            bytes_accessed=2 * columns * (sectors * tm_count * rec_len + NFREQ * 2 * wide),
            transcendentals=0,
        ),
        name="coeffs_and_gram",
    )(place, time_basis, azimuth, weight, before, *arrived)


def subspace_kernel(cell_total, first, packed_ref, basis_ref, energy_ref):
    size, _, pairs = packed_ref.shape
    row = lax.broadcasted_iota(jnp.int32, (size, pairs), 0)
    column_re, column_im = [], []
    for q in range(size):
        down, along = packed_ref[q], packed_ref[:, q, :]
        column_re.append(jnp.where(row <= q, down, along))
        column_im.append(jnp.where(row > q, down, jnp.where(row == q, 0.0, -along)))

    def image_of(vec_re, vec_im):
        out_re, out_im = [], []
        for j in range(MODES):
            sum_re = jnp.zeros_like(column_re[0])
            sum_im = jnp.zeros_like(column_re[0])
            for q in range(size):
                at_re, at_im = vec_re[j][q:q + 1], vec_im[j][q:q + 1]
                sum_re += column_re[q] * at_re - column_im[q] * at_im
                sum_im += column_re[q] * at_im + column_im[q] * at_re
            out_re.append(sum_re)
            out_im.append(sum_im)
        return out_re, out_im

    total = lambda x: jnp.sum(x, 0, keepdims=True)
    vec_re = [column_re[q] for q in first]
    vec_im = [column_im[q] for q in first]
    for sweep in range(SUBIT):
        if sweep > 0:
            vec_re, vec_im = image_of(vec_re, vec_im)
        vec_re, vec_im = list(vec_re), list(vec_im)
        for i in range(MODES):
            scale = 1.0 / jnp.sqrt(total(vec_re[i] * vec_re[i] + vec_im[i] * vec_im[i]) + EPSILON)
            own_re, own_im = vec_re[i] * scale, vec_im[i] * scale
            vec_re[i], vec_im[i] = own_re, own_im
            for j in range(i + 1, MODES):
                proj_re = total(own_re * vec_re[j] + own_im * vec_im[j])
                proj_im = total(own_re * vec_im[j] - own_im * vec_re[j])
                vec_re[j] = vec_re[j] - (proj_re * own_re - proj_im * own_im)
                vec_im[j] = vec_im[j] - (proj_re * own_im + proj_im * own_re)
    image_re, image_im = image_of(vec_re, vec_im)
    for j in range(MODES):
        basis_ref[0, j] = vec_re[j]
        basis_ref[1, j] = vec_im[j]
        energy_ref[j:j + 1] = total(vec_re[j] * image_re[j] + vec_im[j] * image_im[j]) / cell_total


def subspace(packed, first, cell_total):
    size, _, pairs = packed.shape
    return pl.pallas_call(
        functools.partial(subspace_kernel, float(cell_total), first),
        out_shape=[
            jax.ShapeDtypeStruct((2, MODES, size, pairs), jnp.float32),
            jax.ShapeDtypeStruct((MODES, pairs), jnp.float32),
        ],
        name="subspace",
    )(packed)


def mix_kernel(orders, fields, owner_ref, mixing_ref, spread_ref, factor_ref, root_ref, *refs):
    out_ref = refs[-1]
    freqs, own_rows, _ = mixing_ref.shape
    rows = 2 * own_rows
    total = spread_ref.shape[2]
    blocks = total // (2 * orders)
    row = lax.broadcasted_iota(jnp.int32, (rows, total), 0) % own_rows // (own_rows // orders)
    column = lax.broadcasted_iota(jnp.int32, (rows, total), 1) // blocks % orders
    factor = jnp.transpose(factor_ref[0])
    for n in range(freqs):
        wide = jnp.concatenate(
            [
                jnp.dot(mixing_ref[n], spread_ref[d], preferred_element_type=jnp.float32)
                for d in range(2)
            ],
            0,
        )
        wide = jnp.where(row == column, wide, 0.0).astype(jnp.bfloat16)
        scale = factor[:, n:n + 1] * root_ref[...]
        for k in range(fields):
            mixed = jnp.dot(wide, refs[k][n], preferred_element_type=jnp.float32)
            out_ref[k, n] = (mixed * scale).astype(jnp.bfloat16)


def mix(owner, coeffs, mixing, spread, factor, root_weight, owners, orders, after):
    rows = coeffs[0].shape[1]
    own_rows, depth = mixing.shape[1:]
    out_rows = 2 * own_rows
    columns = root_weight.shape[1]
    freqs, fields = NFREQ // owners, len(coeffs)
    return pl.pallas_call(
        functools.partial(mix_kernel, orders, fields),
        grid_spec=pltpu.PrefetchScalarGridSpec(
            num_scalar_prefetch=1,
            grid=(1,),
            in_specs=[
                pl.BlockSpec((freqs, own_rows, depth), lambda i, at: (at[0], 0, 0)),
                pl.BlockSpec(spread.shape, lambda i, at: (0, 0, 0)),
                pl.BlockSpec((1, freqs, out_rows), lambda i, at: (at[0], 0, 0)),
                pl.BlockSpec(root_weight.shape, lambda i, at: (0, 0)),
            ] + [
                pl.BlockSpec((freqs, rows, x.shape[2]), lambda i, at: (at[0], 0, 0)) for x in coeffs
            ] + [pl.BlockSpec(memory_space=pl.ANY)] * len(after),
            out_specs=pl.BlockSpec((fields, freqs, out_rows, columns), lambda i, at: (0, 0, 0, 0)),
        ),
        out_shape=jax.ShapeDtypeStruct((fields, freqs, out_rows, columns), jnp.bfloat16),
        compiler_params=pltpu.CompilerParams(vmem_limit_bytes=VMEM_LIMIT),
        cost_estimate=pl.CostEstimate(
            flops=2 * freqs * out_rows * rows * fields * columns,
            bytes_accessed=2 * freqs * (rows + out_rows) * fields * columns,
            transcendentals=0,
        ),
        name="mix",
    )(jnp.reshape(owner, (1,)), mixing, spread, factor, root_weight, *coeffs, *after)


def pack_kernel(record_ref, out_ref):
    owners, _, _, part = out_ref.shape
    for d in range(owners):
        out_ref[d, 0] = record_ref[0, 0, :, d * part:(d + 1) * part]


def pack(by_field, k, owners):
    sec_local, _, rec_len, cells = by_field.shape
    part = cells // owners
    return pl.pallas_call(
        pack_kernel,
        grid=(sec_local,),
        in_specs=[pl.BlockSpec((1, 1, rec_len, cells), lambda i: (i, k, 0, 0))],
        out_specs=pl.BlockSpec((owners, 1, rec_len, part), lambda i: (0, i, 0, 0)),
        out_shape=jax.ShapeDtypeStruct((owners, sec_local, rec_len, part), by_field.dtype),
        compiler_params=pltpu.CompilerParams(vmem_limit_bytes=VMEM_LIMIT),
        cost_estimate=pl.CostEstimate(
            flops=0, bytes_accessed=4 * sec_local * rec_len * cells, transcendentals=0
        ),
        name="pack",
    )(by_field)


def take_kernel(place_ref, record_ref, out_ref):
    out_ref[...] = record_ref[:, 0]


def take(by_field, k, owner, owners):
    sec_local, _, rec_len, cells = by_field.shape
    count = cells // owners
    if count % LANES:
        return lax.dynamic_slice_in_dim(by_field[:, k], owner * count, count, 2)
    return pl.pallas_call(
        take_kernel,
        grid_spec=pltpu.PrefetchScalarGridSpec(
            num_scalar_prefetch=1,
            grid=(1,),
            in_specs=[
                pl.BlockSpec((sec_local, 1, rec_len, count), lambda i, at: (0, k, 0, at[0]))
            ],
            out_specs=pl.BlockSpec((sec_local, rec_len, count), lambda i, at: (0, 0, 0)),
        ),
        out_shape=jax.ShapeDtypeStruct((sec_local, rec_len, count), by_field.dtype),
        compiler_params=pltpu.CompilerParams(vmem_limit_bytes=VMEM_LIMIT),
        cost_estimate=pl.CostEstimate(
            flops=0, bytes_accessed=4 * sec_local * rec_len * count, transcendentals=0
        ),
        name="take",
    )(jnp.reshape(owner, (1,)), by_field)


def unpack_kernel(count, owner_ref, *refs):
    out_ref = refs[-1]
    step = pl.program_id(0)
    for n in range(count):

        @pl.when(step == n)
        def _():
            for k in range(refs[n].shape[0]):
                for f in range(refs[n].shape[1]):
                    for d in range(refs[n].shape[2]):
                        out_ref[:, f, d, k] = refs[n][k, f, d]


def unpack(sources, pieces, owners, whole):
    fields, freqs, two, orders, modes, part = pieces[0].shape
    shape = (orders, freqs, two, fields, modes, owners * part)
    if part % LANES:
        whole = jnp.zeros(shape, pieces[0].dtype) if whole is None else whole
        for owner, piece in zip(sources, pieces):
            piece = jnp.transpose(piece, (3, 1, 2, 0, 4, 5))
            whole = lax.dynamic_update_slice_in_dim(whole, piece, owner * part, 5)
        return whole
    count = len(pieces)
    inputs = list(pieces) if whole is None else list(pieces) + [whole]
    in_specs = [
        pl.BlockSpec(pieces[0].shape, lambda i, at: (0, 0, 0, 0, 0, 0)) for _ in pieces
    ] + [pl.BlockSpec(memory_space=pl.ANY)]
    return pl.pallas_call(
        functools.partial(unpack_kernel, count),
        grid_spec=pltpu.PrefetchScalarGridSpec(
            num_scalar_prefetch=1,
            grid=(count,),
            in_specs=in_specs[:len(inputs)],
            out_specs=pl.BlockSpec(shape[:5] + (part,), lambda i, at: (0, 0, 0, 0, 0, at[i])),
        ),
        out_shape=jax.ShapeDtypeStruct(shape, pieces[0].dtype),
        input_output_aliases={} if whole is None else {1 + count: 0},
        compiler_params=pltpu.CompilerParams(vmem_limit_bytes=VMEM_LIMIT),
        cost_estimate=pl.CostEstimate(
            flops=0, bytes_accessed=4 * count * pieces[0].size, transcendentals=0
        ),
        name="unpack",
    )(jnp.stack(sources), *inputs)


def local(records, block_start, slab_index, weight_table):
    sec_local, rec_len, fields, cell_local = records.shape
    sec_count = lax.axis_size("sector")
    tm_count = lax.axis_size("tm")
    space_count = lax.axis_size("space")
    owners = sec_count * tm_count
    owner_axes = ("sector", "tm")
    sectors = sec_local * sec_count
    orders = sectors // 2
    blocks = block_start.shape[0]
    depth = 2 * blocks
    part = cell_local // owners
    own_freqs = NFREQ // owners
    me = lax.axis_index("sector") * tm_count + lax.axis_index("tm")

    by_field = jnp.transpose(records, (0, 2, 1, 3))
    sec_at, tm_at = lax.axis_index("sector"), lax.axis_index("tm")
    shifts = [(z, x) for z in range(sec_count) for x in range(tm_count)]
    in_order = sorted(
        [r for r in shifts if r != (0, 0)], key=lambda r: (r[0] == 0, abs(2 * r[0] - sec_count), r)
    )

    def owner_after(z, x):
        return (sec_at + z) % sec_count * tm_count + (tm_at + x) % tm_count

    def send(piece, z, x):
        if (z, x) == (0, 0):
            return piece
        hops = [
            (a * tm_count + j, (a + z) % sec_count * tm_count + (j + x) % tm_count)
            for a in range(sec_count)
            for j in range(tm_count)
        ]
        return lax.ppermute(piece, owner_axes, hops)

    arrived = []
    for k in range(fields):
        if k % 2:
            got = {r: send(take(by_field, k, owner_after(*r), owners), *r) for r in in_order + [(0, 0)]}
            arrived.append([got[r][None] for r in shifts])
        else:
            got = pack(by_field, k, owners)
            arrived.append(
                [lax.all_to_all(got, owner_axes, split_axis=0, concat_axis=0, tiled=True)]
            )

    time_basis = placed_time_basis(block_start, tm_count)
    half, _ = half_span(blocks // tm_count)
    halves = blocks // tm_count // half
    azimuth = jnp.einsum(
        "mcse,ij,bd->cmibsjed",
        order_table(orders, sectors),
        jnp.eye(tm_count, dtype=jnp.bfloat16),
        jnp.eye(half, dtype=jnp.bfloat16),
    ).reshape(2 * orders * tm_count * half, sectors * tm_count * 2 * half)
    place = [
        (b // half % halves * tm_count + b // (half * halves)) * half + b % half
        for b in range(blocks)
    ]
    own_slab = lax.dynamic_slice_in_dim(slab_index, me * part, part)
    weight = jnp.sum(
        jnp.where(
            own_slab[None, :] == jnp.arange(weight_table.shape[0], dtype=jnp.int32)[:, None],
            weight_table[:, None],
            0.0,
        ),
        0,
        keepdims=True,
    )

    gram = jnp.zeros((NFREQ, blocks, orders * blocks), jnp.float32)

    coeffs = []
    for k in range(fields):
        own, gram = coeffs_and_gram(
            jnp.stack([sec_at, tm_at]), arrived[k], sec_count, time_basis, azimuth, weight, gram
        )
        coeffs.append(own)

    if own_freqs % space_count == 0:
        axes = owner_axes + ("space",)
    else:
        gram = lax.psum(gram, "space")
        axes = owner_axes
    solvers = math.prod(lax.axis_size(a) for a in axes)
    solved = NFREQ // solvers
    gram = gram.reshape((solvers, solved) + gram.shape[1:])
    gram = lax.all_to_all(gram, axes, split_axis=0, concat_axis=0, tiled=True)
    gram = jnp.sum(gram, 0).reshape(solved, blocks, orders, blocks)
    gram = jnp.transpose(gram, (3, 1, 0, 2)).reshape(blocks, blocks, solved * orders)
    basis, energy = subspace(gram, tuple(place[:MODES]), fields * cell_local * space_count)

    short = basis.astype(jnp.bfloat16).reshape(2, MODES, blocks, solved, orders)
    mixing = jnp.transpose(short, (3, 4, 1, 0, 2)).reshape(solved, orders * MODES * depth)
    energy = jnp.transpose(energy.reshape(MODES, solved, orders), (1, 2, 0)).reshape(solved, -1)
    high = energy.astype(jnp.bfloat16)
    rest = energy - high.astype(jnp.float32)
    middle = rest.astype(jnp.bfloat16)
    low = (rest - middle.astype(jnp.float32)).astype(jnp.bfloat16)
    packet = jnp.concatenate([mixing, high, middle, low], 1)
    width = -(-packet.shape[1] // LANES) * LANES
    packet = jnp.pad(packet, ((0, 0), (0, width - packet.shape[1])))
    packet = packet.reshape(1, solved, width // LANES, LANES)
    packet = jnp.broadcast_to(packet, (solvers,) + packet.shape[1:])
    packet = lax.all_to_all(packet, axes, split_axis=0, concat_axis=0, tiled=True)
    packet = packet.reshape(NFREQ, width)
    count = orders * MODES
    mixing = packet[:, :orders * MODES * depth].reshape(NFREQ, orders * MODES, depth)
    tail = packet[:, orders * MODES * depth:].astype(jnp.float32)
    energy = (tail[:, :count] + tail[:, count:2 * count]) + tail[:, 2 * count:3 * count]
    factor = lax.rsqrt(energy)
    factor = jnp.concatenate([factor, factor], 1).reshape(owners, own_freqs, orders * 2 * MODES)
    energy = energy.reshape(NFREQ, orders, MODES)
    root_weight = jnp.sqrt(weight)
    signs = jnp.array([[[1, 0], [0, -1]], [[0, 1], [1, 0]]], jnp.bfloat16)
    spread = jnp.broadcast_to(
        signs[:, :, None, :, None, None]
        * jnp.eye(blocks, dtype=jnp.bfloat16)[None, None, :, None, None, :],
        (2, 2, blocks, 2, orders, blocks),
    ).reshape(2, depth, depth * orders)

    coeffs = [pltpu.with_memory_space_constraint(x, pltpu.HBM) for x in coeffs]
    sent = {}
    before = ()
    for z, x in in_order + [(0, 0)]:
        piece = mix(
            owner_after(z, x), coeffs, mixing, spread, factor, root_weight, owners, orders, before
        )
        before = (piece,)
        sent[z, x] = owner_after(-z, -x), send(piece, z, x)
    late = [r for r in in_order if r[0] in (0, 1) and r[1] > 0 or r == in_order[-tm_count]]
    groups = [[(0, 0)]] + [[r] for r in in_order if r not in late] + [late]
    mode_fields = None
    for group in groups:
        pieces = [sent[r][1].reshape(fields, own_freqs, 2, orders, MODES, part) for r in group]
        mode_fields = unpack([sent[r][0] for r in group], pieces, owners, mode_fields)
    mode_fields = jnp.transpose(mode_fields, (0, 1, 2, 4, 3, 5))
    own_energy = lax.dynamic_slice_in_dim(energy, me * own_freqs, own_freqs)
    return (mode_fields, jnp.transpose(own_energy, (1, 0, 2)))


def solution(mesh):
    placed = (P("sector", "tm", None, "space"), P(), P("space"), P())
    return jax.shard_map(
        local,
        mesh=mesh,
        in_specs=placed,
        out_specs=(
            P(None, ("sector", "tm"), None, None, None, "space"),
            P(None, ("sector", "tm"), None),
        ),
        check_vma=False,
    )
```

```python
import functools
import math

import jax
import jax.numpy as jnp
from jax import lax
from jax.experimental import pallas as pl
from jax.experimental.pallas import tpu as pltpu
from jax.sharding import PartitionSpec as P

NFFT = 64
NFREQ = 32
MODES = 8
SUBIT = 4
LANES = 128
EPSILON = 1e-06
VMEM_LIMIT = 48 * 1024 * 1024


def time_table(length, freq_count):
    steps_t = jnp.arange(length, dtype=jnp.float32)
    freq_f = jnp.arange(freq_count, dtype=jnp.float32)
    window = 0.5 - 0.5 * jnp.cos(2.0 * math.pi * steps_t / length)
    angles = 2.0 * math.pi * freq_f[:, None] * steps_t[None, :] / length
    both = jnp.stack([window * jnp.cos(angles), -window * jnp.sin(angles)])
    return (both / math.sqrt(length)).astype(jnp.bfloat16)


def order_table(orders, sectors):
    order_m = jnp.arange(orders, dtype=jnp.float32)[:, None]
    sector_s = jnp.arange(sectors, dtype=jnp.float32)[None, :]
    angles = 2.0 * math.pi * order_m * sector_s / sectors
    cosine = jnp.cos(angles)
    sine_part = jnp.sin(angles)
    upper_row = jnp.stack([cosine, sine_part], -1)
    lower_row = jnp.stack([-sine_part, cosine], -1)
    return (jnp.stack([upper_row, lower_row], 1) / math.sqrt(sectors)).astype(jnp.bfloat16)


def half_span(blocks):
    half = blocks // 2
    return half, (half - 1) * (NFFT // 2) + NFFT // 8 + NFFT


def placed_time_basis(block_start, tm_count):
    blocks = block_start.shape[0] // tm_count
    half, span = half_span(blocks)
    basis = time_table(NFFT, NFREQ)
    first = jnp.arange(blocks, dtype=jnp.int32) // half * (half * (NFFT // 2))
    inside = block_start.reshape(tm_count, blocks) - first[None, :]
    place = (
        inside[:, :, None, None] + jnp.arange(NFFT, dtype=jnp.int32)[:, None]
        == jnp.arange(span, dtype=jnp.int32)[None, :]
    ).astype(jnp.bfloat16)
    table = jnp.einsum(
        "eft,jhbtu->jhfebu",
        basis,
        place.reshape(tm_count, 2, half, NFFT, span),
        preferred_element_type=jnp.float32,
    ).astype(jnp.bfloat16)
    return table.reshape(tm_count, 2, NFREQ * 2 * half, span)


def coeff_kernel(sec_count, sec_local, freqs, orders, place_ref, time_ref, azimuth_ref, weight_ref,
                 before_ref, *refs):
    record_refs, (coeff_ref, gram_ref, spectra) = refs[:-3], refs[-3:]
    step = pl.program_id(0)
    tm_count, halves, _, span = time_ref.shape
    rec_len, columns = record_refs[0].shape[1:]
    sectors = spectra.shape[0]
    rows = spectra.shape[2] // NFREQ

    @pl.when(step < sec_local)
    def _():
        for shift in range(sec_count):
            source = lax.rem(place_ref[0] + sec_count - shift, sec_count)
            own = record_refs[shift * tm_count:(shift + 1) * tm_count]
            for h in range(halves):
                first = h * (rec_len - span) // (halves - 1)
                parts = []
                for j in range(tm_count):
                    piece = own[0][0, first:first + span]
                    for x in range(1, tm_count):
                        here = lax.rem(place_ref[1] + tm_count - x, tm_count) == j
                        piece = jnp.where(here, own[x][0, first:first + span], piece)
                    part = jnp.dot(time_ref[j, h], piece, preferred_element_type=jnp.float32)
                    parts.append(part.reshape(NFREQ, rows // tm_count, columns))
                joined = jnp.stack(parts, 1).reshape(NFREQ * rows, columns)
                spectra[source * sec_local + step, h] = joined.astype(jnp.bfloat16)

    @pl.when(step >= sec_local)
    def _():
        half_rows = azimuth_ref.shape[0]
        depth = half_rows // (2 * orders)
        blocks = depth * halves
        wide = orders * blocks
        row = lax.broadcasted_iota(jnp.int32, (wide, wide), 0) % blocks
        column = lax.broadcasted_iota(jnp.int32, (wide, wide), 1) % blocks
        owner = lax.broadcasted_iota(jnp.int32, (blocks, wide), 1) // blocks
        for n in range(freqs):
            at = pl.multiple_of(((step - sec_local) * freqs + n) * rows, rows)
            own = [
                spectra[:, h, pl.ds(at, rows), :].reshape(sectors * rows, columns)
                for h in range(halves)
            ]
            parts = [
                jnp.dot(azimuth_ref[...], x, preferred_element_type=jnp.float32) for x in own
            ]
            parts = [x.reshape(2 * orders, depth, columns) for x in parts]
            coeffs = jnp.stack(parts, 1).reshape(2 * wide, columns).astype(jnp.bfloat16)
            coeff_ref[n] = coeffs
            weighted = (coeffs.astype(jnp.float32) * weight_ref[...]).astype(jnp.bfloat16)
            products = lax.dot_general(
                weighted, coeffs, (((1,), (1,)), ((), ())), preferred_element_type=jnp.float32
            )
            real = products[:wide, :wide] + products[wide:, wide:]
            imag = products[:wide, wide:] - products[wide:, :wide]
            packed = jnp.where(row <= column, real, imag)
            own = packed[:blocks]
            for m in range(1, orders):
                own = jnp.where(owner == m, packed[m * blocks:(m + 1) * blocks], own)
            gram_ref[n] = before_ref[n] + own


def coeffs_and_gram(place, arrived, sec_count, time_basis, azimuth, weight, before):
    sec_local, rec_len, columns = arrived[0].shape
    sectors = sec_count * sec_local
    tm_count, halves = time_basis.shape[:2]
    blocks, wide = before.shape[1:]
    rows = azimuth.shape[1] // sectors
    steps = 4
    freqs = NFREQ // steps
    later = lambda i: jnp.maximum(i - sec_local, 0)
    early = lambda i: jnp.minimum(i, sec_local - 1)
    flops = 2 * columns * (
        sectors * time_basis.size + NFREQ * halves * azimuth.size + NFREQ * 4 * wide * wide
    )
    piece = pl.BlockSpec((1, rec_len, columns), lambda i, _: (early(i), 0, 0))
    return pl.pallas_call(
        functools.partial(coeff_kernel, sec_count, sec_local, freqs, wide // blocks),
        grid_spec=pltpu.PrefetchScalarGridSpec(
            num_scalar_prefetch=1,
            grid=(sec_local + steps,),
            in_specs=[
                pl.BlockSpec(time_basis.shape, lambda i, _: (0, 0, 0, 0)),
                pl.BlockSpec(azimuth.shape, lambda i, _: (0, 0)),
                pl.BlockSpec(weight.shape, lambda i, _: (0, 0)),
                pl.BlockSpec((freqs, blocks, wide), lambda i, _: (later(i), 0, 0)),
            ] + [piece] * len(arrived),
            out_specs=[
                pl.BlockSpec((freqs, 2 * wide, columns), lambda i, _: (later(i), 0, 0)),
                pl.BlockSpec((freqs, blocks, wide), lambda i, _: (later(i), 0, 0)),
            ],
            scratch_shapes=[pltpu.VMEM((sectors, halves, NFREQ * rows, columns), jnp.bfloat16)],
        ),
        out_shape=[
            jax.ShapeDtypeStruct((NFREQ, 2 * wide, columns), jnp.bfloat16),
            jax.ShapeDtypeStruct(before.shape, jnp.float32),
        ],
        compiler_params=pltpu.CompilerParams(vmem_limit_bytes=VMEM_LIMIT),
        cost_estimate=pl.CostEstimate(
            flops=flops,
            bytes_accessed=2 * columns * (sectors * tm_count * rec_len + NFREQ * 2 * wide),
            transcendentals=0,
        ),
        name="coeffs_and_gram",
    )(place, time_basis, azimuth, weight, before, *arrived)


def subspace_kernel(cell_total, first, packed_ref, basis_ref, energy_ref):
    size, _, pairs = packed_ref.shape
    row = lax.broadcasted_iota(jnp.int32, (size, pairs), 0)
    column_re, column_im = [], []
    for q in range(size):
        down, along = packed_ref[q], packed_ref[:, q, :]
        column_re.append(jnp.where(row <= q, down, along))
        column_im.append(jnp.where(row > q, down, jnp.where(row == q, 0.0, -along)))

    def image_of(vec_re, vec_im):
        out_re, out_im = [], []
        for j in range(MODES):
            sum_re = jnp.zeros_like(column_re[0])
            sum_im = jnp.zeros_like(column_re[0])
            for q in range(size):
                at_re, at_im = vec_re[j][q:q + 1], vec_im[j][q:q + 1]
                sum_re += column_re[q] * at_re - column_im[q] * at_im
                sum_im += column_re[q] * at_im + column_im[q] * at_re
            out_re.append(sum_re)
            out_im.append(sum_im)
        return out_re, out_im

    total = lambda x: jnp.sum(x, 0, keepdims=True)
    vec_re = [column_re[q] for q in first]
    vec_im = [column_im[q] for q in first]
    for sweep in range(SUBIT):
        if sweep > 0:
            vec_re, vec_im = image_of(vec_re, vec_im)
        vec_re, vec_im = list(vec_re), list(vec_im)
        for i in range(MODES):
            scale = 1.0 / jnp.sqrt(total(vec_re[i] * vec_re[i] + vec_im[i] * vec_im[i]) + EPSILON)
            own_re, own_im = vec_re[i] * scale, vec_im[i] * scale
            vec_re[i], vec_im[i] = own_re, own_im
            for j in range(i + 1, MODES):
                proj_re = total(own_re * vec_re[j] + own_im * vec_im[j])
                proj_im = total(own_re * vec_im[j] - own_im * vec_re[j])
                vec_re[j] = vec_re[j] - (proj_re * own_re - proj_im * own_im)
                vec_im[j] = vec_im[j] - (proj_re * own_im + proj_im * own_re)
    image_re, image_im = image_of(vec_re, vec_im)
    for j in range(MODES):
        basis_ref[0, j] = vec_re[j]
        basis_ref[1, j] = vec_im[j]
        energy_ref[j:j + 1] = total(vec_re[j] * image_re[j] + vec_im[j] * image_im[j]) / cell_total


def subspace(packed, first, cell_total):
    size, _, pairs = packed.shape
    return pl.pallas_call(
        functools.partial(subspace_kernel, float(cell_total), first),
        out_shape=[
            jax.ShapeDtypeStruct((2, MODES, size, pairs), jnp.float32),
            jax.ShapeDtypeStruct((MODES, pairs), jnp.float32),
        ],
        name="subspace",
    )(packed)


def mix_kernel(orders, fields, owner_ref, mixing_ref, spread_ref, factor_ref, root_ref, *refs):
    out_ref = refs[-1]
    freqs, own_rows, _ = mixing_ref.shape
    rows = 2 * own_rows
    total = spread_ref.shape[2]
    blocks = total // (2 * orders)
    row = lax.broadcasted_iota(jnp.int32, (rows, total), 0) % own_rows // (own_rows // orders)
    column = lax.broadcasted_iota(jnp.int32, (rows, total), 1) // blocks % orders
    factor = jnp.transpose(factor_ref[0])
    for n in range(freqs):
        wide = jnp.concatenate(
            [
                jnp.dot(mixing_ref[n], spread_ref[d], preferred_element_type=jnp.float32)
                for d in range(2)
            ],
            0,
        )
        wide = jnp.where(row == column, wide, 0.0).astype(jnp.bfloat16)
        scale = factor[:, n:n + 1] * root_ref[...]
        for k in range(fields):
            mixed = jnp.dot(wide, refs[k][n], preferred_element_type=jnp.float32)
            out_ref[k, n] = (mixed * scale).astype(jnp.bfloat16)


def mix(owner, coeffs, mixing, spread, factor, root_weight, owners, orders, after):
    rows = coeffs[0].shape[1]
    own_rows, depth = mixing.shape[1:]
    out_rows = 2 * own_rows
    columns = root_weight.shape[1]
    freqs, fields = NFREQ // owners, len(coeffs)
    return pl.pallas_call(
        functools.partial(mix_kernel, orders, fields),
        grid_spec=pltpu.PrefetchScalarGridSpec(
            num_scalar_prefetch=1,
            grid=(1,),
            in_specs=[
                pl.BlockSpec((freqs, own_rows, depth), lambda i, at: (at[0], 0, 0)),
                pl.BlockSpec(spread.shape, lambda i, at: (0, 0, 0)),
                pl.BlockSpec((1, freqs, out_rows), lambda i, at: (at[0], 0, 0)),
                pl.BlockSpec(root_weight.shape, lambda i, at: (0, 0)),
            ] + [
                pl.BlockSpec((freqs, rows, x.shape[2]), lambda i, at: (at[0], 0, 0)) for x in coeffs
            ] + [pl.BlockSpec(memory_space=pl.ANY)] * len(after),
            out_specs=pl.BlockSpec((fields, freqs, out_rows, columns), lambda i, at: (0, 0, 0, 0)),
        ),
        out_shape=jax.ShapeDtypeStruct((fields, freqs, out_rows, columns), jnp.bfloat16),
        compiler_params=pltpu.CompilerParams(vmem_limit_bytes=VMEM_LIMIT),
        cost_estimate=pl.CostEstimate(
            flops=2 * freqs * out_rows * rows * fields * columns,
            bytes_accessed=2 * freqs * (rows + out_rows) * fields * columns,
            transcendentals=0,
        ),
        name="mix",
    )(jnp.reshape(owner, (1,)), mixing, spread, factor, root_weight, *coeffs, *after)


def take_kernel(place_ref, record_ref, out_ref):
    out_ref[...] = record_ref[:, 0]


def take(by_field, k, owner, owners):
    sec_local, _, rec_len, cells = by_field.shape
    count = cells // owners
    if count % LANES:
        return lax.dynamic_slice_in_dim(by_field[:, k], owner * count, count, 2)
    return pl.pallas_call(
        take_kernel,
        grid_spec=pltpu.PrefetchScalarGridSpec(
            num_scalar_prefetch=1,
            grid=(1,),
            in_specs=[
                pl.BlockSpec((sec_local, 1, rec_len, count), lambda i, at: (0, k, 0, at[0]))
            ],
            out_specs=pl.BlockSpec((sec_local, rec_len, count), lambda i, at: (0, 0, 0)),
        ),
        out_shape=jax.ShapeDtypeStruct((sec_local, rec_len, count), by_field.dtype),
        compiler_params=pltpu.CompilerParams(vmem_limit_bytes=VMEM_LIMIT),
        cost_estimate=pl.CostEstimate(
            flops=0, bytes_accessed=4 * sec_local * rec_len * count, transcendentals=0
        ),
        name="take",
    )(jnp.reshape(owner, (1,)), by_field)


def unpack_kernel(count, owner_ref, *refs):
    out_ref = refs[-1]
    step = pl.program_id(0)
    for n in range(count):

        @pl.when(step == n)
        def _():
            for k in range(refs[n].shape[0]):
                for f in range(refs[n].shape[1]):
                    for d in range(refs[n].shape[2]):
                        out_ref[:, f, d, k] = refs[n][k, f, d]


def unpack(sources, pieces, owners, whole):
    fields, freqs, two, orders, modes, part = pieces[0].shape
    shape = (orders, freqs, two, fields, modes, owners * part)
    if part % LANES:
        whole = jnp.zeros(shape, pieces[0].dtype) if whole is None else whole
        for owner, piece in zip(sources, pieces):
            piece = jnp.transpose(piece, (3, 1, 2, 0, 4, 5))
            whole = lax.dynamic_update_slice_in_dim(whole, piece, owner * part, 5)
        return whole
    count = len(pieces)
    inputs = list(pieces) if whole is None else list(pieces) + [whole]
    in_specs = [
        pl.BlockSpec(pieces[0].shape, lambda i, at: (0, 0, 0, 0, 0, 0)) for _ in pieces
    ] + [pl.BlockSpec(memory_space=pl.ANY)]
    return pl.pallas_call(
        functools.partial(unpack_kernel, count),
        grid_spec=pltpu.PrefetchScalarGridSpec(
            num_scalar_prefetch=1,
            grid=(count,),
            in_specs=in_specs[:len(inputs)],
            out_specs=pl.BlockSpec(shape[:5] + (part,), lambda i, at: (0, 0, 0, 0, 0, at[i])),
        ),
        out_shape=jax.ShapeDtypeStruct(shape, pieces[0].dtype),
        input_output_aliases={} if whole is None else {1 + count: 0},
        compiler_params=pltpu.CompilerParams(vmem_limit_bytes=VMEM_LIMIT),
        cost_estimate=pl.CostEstimate(
            flops=0, bytes_accessed=4 * count * pieces[0].size, transcendentals=0
        ),
        name="unpack",
    )(jnp.stack(sources), *inputs)


def local(records, block_start, slab_index, weight_table):
    sec_local, rec_len, fields, cell_local = records.shape
    sec_count = lax.axis_size("sector")
    tm_count = lax.axis_size("tm")
    space_count = lax.axis_size("space")
    owners = sec_count * tm_count
    owner_axes = ("sector", "tm")
    sectors = sec_local * sec_count
    orders = sectors // 2
    blocks = block_start.shape[0]
    depth = 2 * blocks
    part = cell_local // owners
    own_freqs = NFREQ // owners
    me = lax.axis_index("sector") * tm_count + lax.axis_index("tm")

    by_field = jnp.transpose(records, (0, 2, 1, 3))
    sec_at, tm_at = lax.axis_index("sector"), lax.axis_index("tm")
    shifts = [(z, x) for z in range(sec_count) for x in range(tm_count)]
    in_order = sorted(
        [r for r in shifts if r != (0, 0)], key=lambda r: (r[0] == 0, abs(2 * r[0] - sec_count), r)
    )

    def owner_after(z, x):
        return (sec_at + z) % sec_count * tm_count + (tm_at + x) % tm_count

    def send(piece, z, x):
        if (z, x) == (0, 0):
            return piece
        hops = [
            (a * tm_count + j, (a + z) % sec_count * tm_count + (j + x) % tm_count)
            for a in range(sec_count)
            for j in range(tm_count)
        ]
        return lax.ppermute(piece, owner_axes, hops)

    arrived = []
    for k in range(fields):
        got = {r: send(take(by_field, k, owner_after(*r), owners), *r) for r in in_order + [(0, 0)]}
        arrived.append([got[r] for r in shifts])

    time_basis = placed_time_basis(block_start, tm_count)
    half, _ = half_span(blocks // tm_count)
    halves = blocks // tm_count // half
    azimuth = jnp.einsum(
        "mcse,ij,bd->cmibsjed",
        order_table(orders, sectors),
        jnp.eye(tm_count, dtype=jnp.bfloat16),
        jnp.eye(half, dtype=jnp.bfloat16),
    ).reshape(2 * orders * tm_count * half, sectors * tm_count * 2 * half)
    place = [
        (b // half % halves * tm_count + b // (half * halves)) * half + b % half
        for b in range(blocks)
    ]
    own_slab = lax.dynamic_slice_in_dim(slab_index, me * part, part)
    weight = jnp.sum(
        jnp.where(
            own_slab[None, :] == jnp.arange(weight_table.shape[0], dtype=jnp.int32)[:, None],
            weight_table[:, None],
            0.0,
        ),
        0,
        keepdims=True,
    )

    gram = jnp.zeros((NFREQ, blocks, orders * blocks), jnp.float32)

    coeffs = []
    for k in range(fields):
        own, gram = coeffs_and_gram(
            jnp.stack([sec_at, tm_at]), arrived[k], sec_count, time_basis, azimuth, weight, gram
        )
        coeffs.append(own)

    if own_freqs % space_count == 0:
        axes = owner_axes + ("space",)
    else:
        gram = lax.psum(gram, "space")
        axes = owner_axes
    solvers = math.prod(lax.axis_size(a) for a in axes)
    solved = NFREQ // solvers
    gram = gram.reshape((solvers, solved) + gram.shape[1:])
    gram = lax.all_to_all(gram, axes, split_axis=0, concat_axis=0, tiled=True)
    gram = jnp.sum(gram, 0).reshape(solved, blocks, orders, blocks)
    gram = jnp.transpose(gram, (3, 1, 0, 2)).reshape(blocks, blocks, solved * orders)
    basis, energy = subspace(gram, tuple(place[:MODES]), fields * cell_local * space_count)

    short = basis.astype(jnp.bfloat16).reshape(2, MODES, blocks, solved, orders)
    mixing = jnp.transpose(short, (3, 4, 1, 0, 2)).reshape(solved, orders * MODES * depth)
    energy = jnp.transpose(energy.reshape(MODES, solved, orders), (1, 2, 0)).reshape(solved, -1)
    high = energy.astype(jnp.bfloat16)
    rest = energy - high.astype(jnp.float32)
    middle = rest.astype(jnp.bfloat16)
    low = (rest - middle.astype(jnp.float32)).astype(jnp.bfloat16)
    packet = jnp.concatenate([mixing, high, middle, low], 1)
    width = -(-packet.shape[1] // LANES) * LANES
    packet = jnp.pad(packet, ((0, 0), (0, width - packet.shape[1])))
    packet = packet.reshape(1, solved, width // LANES, LANES)
    packet = jnp.broadcast_to(packet, (solvers,) + packet.shape[1:])
    packet = lax.all_to_all(packet, axes, split_axis=0, concat_axis=0, tiled=True)
    packet = packet.reshape(NFREQ, width)
    count = orders * MODES
    mixing = packet[:, :orders * MODES * depth].reshape(NFREQ, orders * MODES, depth)
    tail = packet[:, orders * MODES * depth:].astype(jnp.float32)
    energy = (tail[:, :count] + tail[:, count:2 * count]) + tail[:, 2 * count:3 * count]
    factor = lax.rsqrt(energy)
    factor = jnp.concatenate([factor, factor], 1).reshape(owners, own_freqs, orders * 2 * MODES)
    energy = energy.reshape(NFREQ, orders, MODES)
    root_weight = jnp.sqrt(weight)
    signs = jnp.array([[[1, 0], [0, -1]], [[0, 1], [1, 0]]], jnp.bfloat16)
    spread = jnp.broadcast_to(
        signs[:, :, None, :, None, None]
        * jnp.eye(blocks, dtype=jnp.bfloat16)[None, None, :, None, None, :],
        (2, 2, blocks, 2, orders, blocks),
    ).reshape(2, depth, depth * orders)

    coeffs = [pltpu.with_memory_space_constraint(x, pltpu.HBM) for x in coeffs]
    sent = {}
    before = ()
    for z, x in in_order + [(0, 0)]:
        piece = mix(
            owner_after(z, x), coeffs, mixing, spread, factor, root_weight, owners, orders, before
        )
        before = (piece,)
        sent[z, x] = owner_after(-z, -x), send(piece, z, x)
    late = [r for r in in_order if r[0] in (0, 1) and r[1] > 0 or r == in_order[-tm_count]]
    groups = [[(0, 0)]] + [[r] for r in in_order if r not in late] + [late]
    mode_fields = None
    for group in groups:
        pieces = [sent[r][1].reshape(fields, own_freqs, 2, orders, MODES, part) for r in group]
        mode_fields = unpack([sent[r][0] for r in group], pieces, owners, mode_fields)
    mode_fields = jnp.transpose(mode_fields, (0, 1, 2, 4, 3, 5))
    own_energy = lax.dynamic_slice_in_dim(energy, me * own_freqs, own_freqs)
    return (mode_fields, jnp.transpose(own_energy, (1, 0, 2)))


def solution(mesh):
    placed = (P("sector", "tm", None, "space"), P(), P("space"), P())
    return jax.shard_map(
        local,
        mesh=mesh,
        in_specs=placed,
        out_specs=(
            P(None, ("sector", "tm"), None, None, None, "space"),
            P(None, ("sector", "tm"), None),
        ),
        check_vma=False,
    )
```

```python
import functools
import math

import jax
import jax.numpy as jnp
from jax import lax
from jax.experimental import pallas as pl
from jax.experimental.pallas import tpu as pltpu
from jax.sharding import PartitionSpec as P

NFFT = 64
NFREQ = 32
MODES = 8
SUBIT = 4
LANES = 128
EPSILON = 1e-06
VMEM_LIMIT = 48 * 1024 * 1024


def time_table(length, freq_count):
    steps_t = jnp.arange(length, dtype=jnp.float32)
    freq_f = jnp.arange(freq_count, dtype=jnp.float32)
    window = 0.5 - 0.5 * jnp.cos(2.0 * math.pi * steps_t / length)
    angles = 2.0 * math.pi * freq_f[:, None] * steps_t[None, :] / length
    both = jnp.stack([window * jnp.cos(angles), -window * jnp.sin(angles)])
    return (both / math.sqrt(length)).astype(jnp.bfloat16)


def order_table(orders, sectors):
    order_m = jnp.arange(orders, dtype=jnp.float32)[:, None]
    sector_s = jnp.arange(sectors, dtype=jnp.float32)[None, :]
    angles = 2.0 * math.pi * order_m * sector_s / sectors
    cosine = jnp.cos(angles)
    sine_part = jnp.sin(angles)
    upper_row = jnp.stack([cosine, sine_part], -1)
    lower_row = jnp.stack([-sine_part, cosine], -1)
    return (jnp.stack([upper_row, lower_row], 1) / math.sqrt(sectors)).astype(jnp.bfloat16)


def half_span(blocks):
    half = blocks // 2
    return half, (half - 1) * (NFFT // 2) + NFFT // 8 + NFFT


def placed_time_basis(block_start, tm_count):
    blocks = block_start.shape[0] // tm_count
    half, span = half_span(blocks)
    basis = time_table(NFFT, NFREQ)
    first = jnp.arange(blocks, dtype=jnp.int32) // half * (half * (NFFT // 2))
    inside = block_start.reshape(tm_count, blocks) - first[None, :]
    place = (
        inside[:, :, None, None] + jnp.arange(NFFT, dtype=jnp.int32)[:, None]
        == jnp.arange(span, dtype=jnp.int32)[None, :]
    ).astype(jnp.bfloat16)
    table = jnp.einsum(
        "eft,jhbtu->jhfebu",
        basis,
        place.reshape(tm_count, 2, half, NFFT, span),
        preferred_element_type=jnp.float32,
    ).astype(jnp.bfloat16)
    return table.reshape(tm_count, 2, NFREQ * 2 * half, span)


def coeff_kernel(sec_count, sec_local, freqs, orders, place_ref, time_ref, azimuth_ref, weight_ref,
                 before_ref, *refs):
    record_refs, (coeff_ref, gram_ref, spectra) = refs[:-3], refs[-3:]
    step = pl.program_id(0)
    tm_count, halves, _, span = time_ref.shape
    rec_len, columns = record_refs[0].shape[1:]
    sectors = spectra.shape[0]
    rows = spectra.shape[2] // NFREQ

    @pl.when(step < sec_local)
    def _():
        for shift in range(sec_count):
            source = lax.rem(place_ref[0] + sec_count - shift, sec_count)
            own = record_refs[shift * tm_count:(shift + 1) * tm_count]
            for h in range(halves):
                first = h * (rec_len - span) // (halves - 1)
                parts = []
                for j in range(tm_count):
                    piece = own[0][0, first:first + span]
                    for x in range(1, tm_count):
                        here = lax.rem(place_ref[1] + tm_count - x, tm_count) == j
                        piece = jnp.where(here, own[x][0, first:first + span], piece)
                    part = jnp.dot(time_ref[j, h], piece, preferred_element_type=jnp.float32)
                    parts.append(part.reshape(NFREQ, rows // tm_count, columns))
                joined = jnp.stack(parts, 1).reshape(NFREQ * rows, columns)
                spectra[source * sec_local + step, h] = joined.astype(jnp.bfloat16)

    @pl.when(step >= sec_local)
    def _():
        half_rows = azimuth_ref.shape[0]
        depth = half_rows // (2 * orders)
        blocks = depth * halves
        wide = orders * blocks
        row = lax.broadcasted_iota(jnp.int32, (wide, wide), 0) % blocks
        column = lax.broadcasted_iota(jnp.int32, (wide, wide), 1) % blocks
        owner = lax.broadcasted_iota(jnp.int32, (blocks, wide), 1) // blocks
        for n in range(freqs):
            at = pl.multiple_of(((step - sec_local) * freqs + n) * rows, rows)
            own = [
                spectra[:, h, pl.ds(at, rows), :].reshape(sectors * rows, columns)
                for h in range(halves)
            ]
            parts = [
                jnp.dot(azimuth_ref[...], x, preferred_element_type=jnp.float32) for x in own
            ]
            parts = [x.reshape(2 * orders, depth, columns) for x in parts]
            coeffs = jnp.stack(parts, 1).reshape(2 * wide, columns).astype(jnp.bfloat16)
            coeff_ref[n] = coeffs
            weighted = (coeffs.astype(jnp.float32) * weight_ref[...]).astype(jnp.bfloat16)
            products = lax.dot_general(
                weighted, coeffs, (((1,), (1,)), ((), ())), preferred_element_type=jnp.float32
            )
            real = products[:wide, :wide] + products[wide:, wide:]
            imag = products[:wide, wide:] - products[wide:, :wide]
            packed = jnp.where(row <= column, real, imag)
            own = packed[:blocks]
            for m in range(1, orders):
                own = jnp.where(owner == m, packed[m * blocks:(m + 1) * blocks], own)
            gram_ref[n] = before_ref[n] + own


def coeffs_and_gram(place, arrived, sec_count, time_basis, azimuth, weight, before):
    sec_local, rec_len, columns = arrived[0].shape
    sectors = sec_count * sec_local
    tm_count, halves = time_basis.shape[:2]
    blocks, wide = before.shape[1:]
    rows = azimuth.shape[1] // sectors
    steps = 4
    freqs = NFREQ // steps
    later = lambda i: jnp.maximum(i - sec_local, 0)
    early = lambda i: jnp.minimum(i, sec_local - 1)
    flops = 2 * columns * (
        sectors * time_basis.size + NFREQ * halves * azimuth.size + NFREQ * 4 * wide * wide
    )
    piece = pl.BlockSpec((1, rec_len, columns), lambda i, _: (early(i), 0, 0))
    return pl.pallas_call(
        functools.partial(coeff_kernel, sec_count, sec_local, freqs, wide // blocks),
        grid_spec=pltpu.PrefetchScalarGridSpec(
            num_scalar_prefetch=1,
            grid=(sec_local + steps,),
            in_specs=[
                pl.BlockSpec(time_basis.shape, lambda i, _: (0, 0, 0, 0)),
                pl.BlockSpec(azimuth.shape, lambda i, _: (0, 0)),
                pl.BlockSpec(weight.shape, lambda i, _: (0, 0)),
                pl.BlockSpec((freqs, blocks, wide), lambda i, _: (later(i), 0, 0)),
            ] + [piece] * len(arrived),
            out_specs=[
                pl.BlockSpec((freqs, 2 * wide, columns), lambda i, _: (later(i), 0, 0)),
                pl.BlockSpec((freqs, blocks, wide), lambda i, _: (later(i), 0, 0)),
            ],
            scratch_shapes=[pltpu.VMEM((sectors, halves, NFREQ * rows, columns), jnp.bfloat16)],
        ),
        out_shape=[
            jax.ShapeDtypeStruct((NFREQ, 2 * wide, columns), jnp.bfloat16),
            jax.ShapeDtypeStruct(before.shape, jnp.float32),
        ],
        compiler_params=pltpu.CompilerParams(vmem_limit_bytes=VMEM_LIMIT),
        cost_estimate=pl.CostEstimate(
            flops=flops,
            bytes_accessed=2 * columns * (sectors * tm_count * rec_len + NFREQ * 2 * wide),
            transcendentals=0,
        ),
        name="coeffs_and_gram",
    )(place, time_basis, azimuth, weight, before, *arrived)


def subspace_kernel(cell_total, first, packed_ref, basis_ref, energy_ref):
    size, _, pairs = packed_ref.shape
    row = lax.broadcasted_iota(jnp.int32, (size, pairs), 0)
    column_re, column_im = [], []
    for q in range(size):
        down, along = packed_ref[q], packed_ref[:, q, :]
        column_re.append(jnp.where(row <= q, down, along))
        column_im.append(jnp.where(row > q, down, jnp.where(row == q, 0.0, -along)))

    def image_of(vec_re, vec_im):
        out_re, out_im = [], []
        for j in range(MODES):
            sum_re = jnp.zeros_like(column_re[0])
            sum_im = jnp.zeros_like(column_re[0])
            for q in range(size):
                at_re, at_im = vec_re[j][q:q + 1], vec_im[j][q:q + 1]
                sum_re += column_re[q] * at_re - column_im[q] * at_im
                sum_im += column_re[q] * at_im + column_im[q] * at_re
            out_re.append(sum_re)
            out_im.append(sum_im)
        return out_re, out_im

    total = lambda x: jnp.sum(x, 0, keepdims=True)
    vec_re = [column_re[q] for q in first]
    vec_im = [column_im[q] for q in first]
    for sweep in range(SUBIT):
        if sweep > 0:
            vec_re, vec_im = image_of(vec_re, vec_im)
        vec_re, vec_im = list(vec_re), list(vec_im)
        for i in range(MODES):
            scale = 1.0 / jnp.sqrt(total(vec_re[i] * vec_re[i] + vec_im[i] * vec_im[i]) + EPSILON)
            own_re, own_im = vec_re[i] * scale, vec_im[i] * scale
            vec_re[i], vec_im[i] = own_re, own_im
            for j in range(i + 1, MODES):
                proj_re = total(own_re * vec_re[j] + own_im * vec_im[j])
                proj_im = total(own_re * vec_im[j] - own_im * vec_re[j])
                vec_re[j] = vec_re[j] - (proj_re * own_re - proj_im * own_im)
                vec_im[j] = vec_im[j] - (proj_re * own_im + proj_im * own_re)
    image_re, image_im = image_of(vec_re, vec_im)
    for j in range(MODES):
        basis_ref[0, j] = vec_re[j]
        basis_ref[1, j] = vec_im[j]
        energy_ref[j:j + 1] = total(vec_re[j] * image_re[j] + vec_im[j] * image_im[j]) / cell_total


def subspace(packed, first, cell_total):
    size, _, pairs = packed.shape
    return pl.pallas_call(
        functools.partial(subspace_kernel, float(cell_total), first),
        out_shape=[
            jax.ShapeDtypeStruct((2, MODES, size, pairs), jnp.float32),
            jax.ShapeDtypeStruct((MODES, pairs), jnp.float32),
        ],
        name="subspace",
    )(packed)


def mix_kernel(orders, fields, owner_ref, mixing_ref, spread_ref, factor_ref, root_ref, *refs):
    out_ref = refs[-1]
    freqs, own_rows, _ = mixing_ref.shape
    rows = 2 * own_rows
    total = spread_ref.shape[2]
    blocks = total // (2 * orders)
    row = lax.broadcasted_iota(jnp.int32, (rows, total), 0) % own_rows // (own_rows // orders)
    column = lax.broadcasted_iota(jnp.int32, (rows, total), 1) // blocks % orders
    factor = jnp.transpose(factor_ref[0])
    for n in range(freqs):
        wide = jnp.concatenate(
            [
                jnp.dot(mixing_ref[n], spread_ref[d], preferred_element_type=jnp.float32)
                for d in range(2)
            ],
            0,
        )
        wide = jnp.where(row == column, wide, 0.0).astype(jnp.bfloat16)
        scale = factor[:, n:n + 1] * root_ref[...]
        for k in range(fields):
            mixed = jnp.dot(wide, refs[k][n], preferred_element_type=jnp.float32)
            out_ref[k, n] = (mixed * scale).astype(jnp.bfloat16)


def mix(owner, coeffs, mixing, spread, factor, root_weight, owners, orders, after):
    rows = coeffs[0].shape[1]
    own_rows, depth = mixing.shape[1:]
    out_rows = 2 * own_rows
    columns = root_weight.shape[1]
    freqs, fields = NFREQ // owners, len(coeffs)
    return pl.pallas_call(
        functools.partial(mix_kernel, orders, fields),
        grid_spec=pltpu.PrefetchScalarGridSpec(
            num_scalar_prefetch=1,
            grid=(1,),
            in_specs=[
                pl.BlockSpec((freqs, own_rows, depth), lambda i, at: (at[0], 0, 0)),
                pl.BlockSpec(spread.shape, lambda i, at: (0, 0, 0)),
                pl.BlockSpec((1, freqs, out_rows), lambda i, at: (at[0], 0, 0)),
                pl.BlockSpec(root_weight.shape, lambda i, at: (0, 0)),
            ] + [
                pl.BlockSpec((freqs, rows, x.shape[2]), lambda i, at: (at[0], 0, 0)) for x in coeffs
            ] + [pl.BlockSpec(memory_space=pl.ANY)] * len(after),
            out_specs=pl.BlockSpec((fields, freqs, out_rows, columns), lambda i, at: (0, 0, 0, 0)),
        ),
        out_shape=jax.ShapeDtypeStruct((fields, freqs, out_rows, columns), jnp.bfloat16),
        compiler_params=pltpu.CompilerParams(vmem_limit_bytes=VMEM_LIMIT),
        cost_estimate=pl.CostEstimate(
            flops=2 * freqs * out_rows * rows * fields * columns,
            bytes_accessed=2 * freqs * (rows + out_rows) * fields * columns,
            transcendentals=0,
        ),
        name="mix",
    )(jnp.reshape(owner, (1,)), mixing, spread, factor, root_weight, *coeffs, *after)


def take_kernel(place_ref, record_ref, out_ref):
    out_ref[...] = record_ref[:, 0]


def take(by_field, k, owner, owners):
    sec_local, _, rec_len, cells = by_field.shape
    count = cells // owners
    if count % LANES:
        return lax.dynamic_slice_in_dim(by_field[:, k], owner * count, count, 2)
    return pl.pallas_call(
        take_kernel,
        grid_spec=pltpu.PrefetchScalarGridSpec(
            num_scalar_prefetch=1,
            grid=(1,),
            in_specs=[
                pl.BlockSpec((sec_local, 1, rec_len, count), lambda i, at: (0, k, 0, at[0]))
            ],
            out_specs=pl.BlockSpec((sec_local, rec_len, count), lambda i, at: (0, 0, 0)),
        ),
        out_shape=jax.ShapeDtypeStruct((sec_local, rec_len, count), by_field.dtype),
        compiler_params=pltpu.CompilerParams(vmem_limit_bytes=VMEM_LIMIT),
        cost_estimate=pl.CostEstimate(
            flops=0, bytes_accessed=4 * sec_local * rec_len * count, transcendentals=0
        ),
        name="take",
    )(jnp.reshape(owner, (1,)), by_field)


def unpack_kernel(count, owner_ref, *refs):
    out_ref = refs[-1]
    step = pl.program_id(0)
    for n in range(count):

        @pl.when(step == n)
        def _():
            for k in range(refs[n].shape[0]):
                for f in range(refs[n].shape[1]):
                    for d in range(refs[n].shape[2]):
                        out_ref[:, f, d, k] = refs[n][k, f, d]


def unpack(sources, pieces, owners, whole):
    fields, freqs, two, orders, modes, part = pieces[0].shape
    shape = (orders, freqs, two, fields, modes, owners * part)
    if part % LANES:
        whole = jnp.zeros(shape, pieces[0].dtype) if whole is None else whole
        for owner, piece in zip(sources, pieces):
            piece = jnp.transpose(piece, (3, 1, 2, 0, 4, 5))
            whole = lax.dynamic_update_slice_in_dim(whole, piece, owner * part, 5)
        return whole
    count = len(pieces)
    inputs = list(pieces) if whole is None else list(pieces) + [whole]
    in_specs = [
        pl.BlockSpec(pieces[0].shape, lambda i, at: (0, 0, 0, 0, 0, 0)) for _ in pieces
    ] + [pl.BlockSpec(memory_space=pl.ANY)]
    return pl.pallas_call(
        functools.partial(unpack_kernel, count),
        grid_spec=pltpu.PrefetchScalarGridSpec(
            num_scalar_prefetch=1,
            grid=(count,),
            in_specs=in_specs[:len(inputs)],
            out_specs=pl.BlockSpec(shape[:5] + (part,), lambda i, at: (0, 0, 0, 0, 0, at[i])),
        ),
        out_shape=jax.ShapeDtypeStruct(shape, pieces[0].dtype),
        input_output_aliases={} if whole is None else {1 + count: 0},
        compiler_params=pltpu.CompilerParams(vmem_limit_bytes=VMEM_LIMIT),
        cost_estimate=pl.CostEstimate(
            flops=0, bytes_accessed=4 * count * pieces[0].size, transcendentals=0
        ),
        name="unpack",
    )(jnp.stack(sources), *inputs)


def local(records, block_start, slab_index, weight_table):
    sec_local, rec_len, fields, cell_local = records.shape
    sec_count = lax.axis_size("sector")
    tm_count = lax.axis_size("tm")
    space_count = lax.axis_size("space")
    owners = sec_count * tm_count
    owner_axes = ("sector", "tm")
    sectors = sec_local * sec_count
    orders = sectors // 2
    blocks = block_start.shape[0]
    depth = 2 * blocks
    part = cell_local // owners
    own_freqs = NFREQ // owners
    me = lax.axis_index("sector") * tm_count + lax.axis_index("tm")

    by_field = jnp.transpose(records, (0, 2, 1, 3))
    sec_at, tm_at = lax.axis_index("sector"), lax.axis_index("tm")
    shifts = [(z, x) for z in range(sec_count) for x in range(tm_count)]
    in_order = sorted(
        [r for r in shifts if r != (0, 0)], key=lambda r: (r[0] == 0, abs(2 * r[0] - sec_count), r)
    )

    def owner_after(z, x):
        return (sec_at + z) % sec_count * tm_count + (tm_at + x) % tm_count

    def send(piece, z, x):
        if (z, x) == (0, 0):
            return piece
        hops = [
            (a * tm_count + j, (a + z) % sec_count * tm_count + (j + x) % tm_count)
            for a in range(sec_count)
            for j in range(tm_count)
        ]
        return lax.ppermute(piece, owner_axes, hops)

    arrived = []
    for k in range(fields):
        got = {r: send(take(by_field, k, owner_after(*r), owners), *r) for r in in_order + [(0, 0)]}
        arrived.append([got[r] for r in shifts])

    time_basis = placed_time_basis(block_start, tm_count)
    half, _ = half_span(blocks // tm_count)
    halves = blocks // tm_count // half
    azimuth = jnp.einsum(
        "mcse,ij,bd->cmibsjed",
        order_table(orders, sectors),
        jnp.eye(tm_count, dtype=jnp.bfloat16),
        jnp.eye(half, dtype=jnp.bfloat16),
    ).reshape(2 * orders * tm_count * half, sectors * tm_count * 2 * half)
    place = [
        (b // half % halves * tm_count + b // (half * halves)) * half + b % half
        for b in range(blocks)
    ]
    own_slab = lax.dynamic_slice_in_dim(slab_index, me * part, part)
    weight = jnp.sum(
        jnp.where(
            own_slab[None, :] == jnp.arange(weight_table.shape[0], dtype=jnp.int32)[:, None],
            weight_table[:, None],
            0.0,
        ),
        0,
        keepdims=True,
    )

    gram = jnp.zeros((NFREQ, blocks, orders * blocks), jnp.float32)

    coeffs = []
    for k in range(fields):
        own, gram = coeffs_and_gram(
            jnp.stack([sec_at, tm_at]), arrived[k], sec_count, time_basis, azimuth, weight, gram
        )
        coeffs.append(own)

    if own_freqs % space_count == 0:
        axes = owner_axes + ("space",)
    else:
        gram = lax.psum(gram, "space")
        axes = owner_axes
    solvers = math.prod(lax.axis_size(a) for a in axes)
    solved = NFREQ // solvers
    gram = gram.reshape((solvers, solved) + gram.shape[1:])
    gram = lax.all_to_all(gram, axes, split_axis=0, concat_axis=0, tiled=True)
    gram = jnp.sum(gram, 0).reshape(solved, blocks, orders, blocks)
    gram = jnp.transpose(gram, (3, 1, 0, 2)).reshape(blocks, blocks, solved * orders)
    basis, energy = subspace(gram, tuple(place[:MODES]), fields * cell_local * space_count)

    short = basis.astype(jnp.bfloat16).reshape(2, MODES, blocks, solved, orders)
    mixing = jnp.transpose(short, (3, 4, 1, 0, 2)).reshape(solved, orders * MODES * depth)
    energy = jnp.transpose(energy.reshape(MODES, solved, orders), (1, 2, 0)).reshape(solved, -1)
    high = energy.astype(jnp.bfloat16)
    rest = energy - high.astype(jnp.float32)
    middle = rest.astype(jnp.bfloat16)
    low = (rest - middle.astype(jnp.float32)).astype(jnp.bfloat16)
    packet = jnp.concatenate([mixing, high, middle, low], 1)
    width = -(-packet.shape[1] // LANES) * LANES
    packet = jnp.pad(packet, ((0, 0), (0, width - packet.shape[1])))
    packet = packet.reshape(1, solved, width // LANES, LANES)
    packet = jnp.broadcast_to(packet, (solvers,) + packet.shape[1:])
    packet = lax.all_to_all(packet, axes, split_axis=0, concat_axis=0, tiled=True)
    packet = packet.reshape(NFREQ, width)
    count = orders * MODES
    mixing = packet[:, :orders * MODES * depth].reshape(NFREQ, orders * MODES, depth)
    tail = packet[:, orders * MODES * depth:].astype(jnp.float32)
    energy = (tail[:, :count] + tail[:, count:2 * count]) + tail[:, 2 * count:3 * count]
    factor = lax.rsqrt(energy)
    factor = jnp.concatenate([factor, factor], 1).reshape(owners, own_freqs, orders * 2 * MODES)
    energy = energy.reshape(NFREQ, orders, MODES)
    root_weight = jnp.sqrt(weight)
    signs = jnp.array([[[1, 0], [0, -1]], [[0, 1], [1, 0]]], jnp.bfloat16)
    spread = jnp.broadcast_to(
        signs[:, :, None, :, None, None]
        * jnp.eye(blocks, dtype=jnp.bfloat16)[None, None, :, None, None, :],
        (2, 2, blocks, 2, orders, blocks),
    ).reshape(2, depth, depth * orders)

    paired = not (sec_count & (sec_count - 1) or tm_count & (tm_count - 1))

    def exchange(piece, z, x):
        if not paired or (z, x) == (0, 0):
            return owner_after(-z, -x), send(piece, z, x)
        hops = [
            (a * tm_count + j, (a ^ z) * tm_count + (j ^ x))
            for a in range(sec_count)
            for j in range(tm_count)
        ]
        return (sec_at ^ z) * tm_count + (tm_at ^ x), lax.ppermute(piece, owner_axes, hops)

    coeffs = [pltpu.with_memory_space_constraint(x, pltpu.HBM) for x in coeffs]
    far = [r for r in shifts if r[0] >= max(sec_count // 2, 1)]
    near = sorted([r for r in shifts if r not in far and r != (0, 0)], key=lambda r: (r[0] == 0, r))
    sent = {}
    before = ()
    in_turn = near[:1] + far[:1] + near[1:] + far[1:]
    for z, x in in_turn + [(0, 0)]:
        owner = (sec_at ^ z) * tm_count + (tm_at ^ x) if paired else owner_after(z, x)
        piece = mix(owner, coeffs, mixing, spread, factor, root_weight, owners, orders, before)
        before = (piece,)
        sent[z, x] = exchange(piece, z, x)
    mode_fields = None
    for group in ([(0, 0)], in_turn[:1], in_turn[1:2], in_turn[2:]):
        pieces = [sent[r][1].reshape(fields, own_freqs, 2, orders, MODES, part) for r in group]
        mode_fields = unpack([sent[r][0] for r in group], pieces, owners, mode_fields)
    mode_fields = jnp.transpose(mode_fields, (0, 1, 2, 4, 3, 5))
    own_energy = lax.dynamic_slice_in_dim(energy, me * own_freqs, own_freqs)
    return (mode_fields, jnp.transpose(own_energy, (1, 0, 2)))


def solution(mesh):
    placed = (P("sector", "tm", None, "space"), P(), P("space"), P())
    return jax.shard_map(
        local,
        mesh=mesh,
        in_specs=placed,
        out_specs=(
            P(None, ("sector", "tm"), None, None, None, "space"),
            P(None, ("sector", "tm"), None),
        ),
        check_vma=False,
    )
```

```python
import functools
import math

import jax
import jax.numpy as jnp
from jax import lax
from jax.experimental import pallas as pl
from jax.experimental.pallas import tpu as pltpu
from jax.sharding import PartitionSpec as P

NFFT = 64
NFREQ = 32
MODES = 8
SUBIT = 4
LANES = 128
EPSILON = 1e-06
VMEM_LIMIT = 48 * 1024 * 1024


def time_table(length, freq_count):
    steps_t = jnp.arange(length, dtype=jnp.float32)
    freq_f = jnp.arange(freq_count, dtype=jnp.float32)
    window = 0.5 - 0.5 * jnp.cos(2.0 * math.pi * steps_t / length)
    angles = 2.0 * math.pi * freq_f[:, None] * steps_t[None, :] / length
    both = jnp.stack([window * jnp.cos(angles), -window * jnp.sin(angles)])
    return (both / math.sqrt(length)).astype(jnp.bfloat16)


def order_table(orders, sectors):
    order_m = jnp.arange(orders, dtype=jnp.float32)[:, None]
    sector_s = jnp.arange(sectors, dtype=jnp.float32)[None, :]
    angles = 2.0 * math.pi * order_m * sector_s / sectors
    cosine = jnp.cos(angles)
    sine_part = jnp.sin(angles)
    upper_row = jnp.stack([cosine, sine_part], -1)
    lower_row = jnp.stack([-sine_part, cosine], -1)
    return (jnp.stack([upper_row, lower_row], 1) / math.sqrt(sectors)).astype(jnp.bfloat16)


def half_span(blocks):
    half = blocks // 2
    return half, (half - 1) * (NFFT // 2) + NFFT // 8 + NFFT


def placed_time_basis(block_start, tm_count):
    blocks = block_start.shape[0] // tm_count
    half, span = half_span(blocks)
    basis = time_table(NFFT, NFREQ)
    first = jnp.arange(blocks, dtype=jnp.int32) // half * (half * (NFFT // 2))
    inside = block_start.reshape(tm_count, blocks) - first[None, :]
    place = (
        inside[:, :, None, None] + jnp.arange(NFFT, dtype=jnp.int32)[:, None]
        == jnp.arange(span, dtype=jnp.int32)[None, :]
    ).astype(jnp.bfloat16)
    table = jnp.einsum(
        "eft,jhbtu->jhfebu",
        basis,
        place.reshape(tm_count, 2, half, NFFT, span),
        preferred_element_type=jnp.float32,
    ).astype(jnp.bfloat16)
    return table.reshape(tm_count, 2, NFREQ * 2 * half, span)


def coeff_kernel(sec_count, sec_local, freqs, orders, place_ref, time_ref, azimuth_ref, weight_ref,
                 before_ref, *refs):
    record_refs, (coeff_ref, gram_ref, spectra) = refs[:-3], refs[-3:]
    step = pl.program_id(0)
    tm_count, halves, _, span = time_ref.shape
    together, rec_len, columns = record_refs[0].shape
    early_steps = sec_local // together
    sectors = spectra.shape[0]
    rows = spectra.shape[2] // NFREQ

    @pl.when(step < early_steps)
    def _():
        for shift, s in [(shift, s) for shift in range(sec_count) for s in range(together)]:
            source = lax.rem(place_ref[0] + sec_count - shift, sec_count)
            own = record_refs[shift * tm_count:(shift + 1) * tm_count]
            for h in range(halves):
                first = h * (rec_len - span) // (halves - 1)
                parts = []
                for j in range(tm_count):
                    piece = own[0][s, first:first + span]
                    for x in range(1, tm_count):
                        here = lax.rem(place_ref[1] + tm_count - x, tm_count) == j
                        piece = jnp.where(here, own[x][s, first:first + span], piece)
                    part = jnp.dot(time_ref[j, h], piece, preferred_element_type=jnp.float32)
                    parts.append(part.reshape(NFREQ, rows // tm_count, columns))
                joined = jnp.stack(parts, 1).reshape(NFREQ * rows, columns)
                spectra[source * sec_local + step * together + s, h] = joined.astype(jnp.bfloat16)

    @pl.when(step >= early_steps)
    def _():
        half_rows = azimuth_ref.shape[0]
        depth = half_rows // (2 * orders)
        blocks = depth * halves
        wide = orders * blocks
        row = lax.broadcasted_iota(jnp.int32, (wide, wide), 0) % blocks
        column = lax.broadcasted_iota(jnp.int32, (wide, wide), 1) % blocks
        owner = lax.broadcasted_iota(jnp.int32, (blocks, wide), 1) // blocks
        for n in range(freqs):
            at = pl.multiple_of(((step - early_steps) * freqs + n) * rows, rows)
            own = [
                spectra[:, h, pl.ds(at, rows), :].reshape(sectors * rows, columns)
                for h in range(halves)
            ]
            parts = [
                jnp.dot(azimuth_ref[...], x, preferred_element_type=jnp.float32) for x in own
            ]
            parts = [x.reshape(2 * orders, depth, columns) for x in parts]
            coeffs = jnp.stack(parts, 1).reshape(2 * wide, columns).astype(jnp.bfloat16)
            coeff_ref[n] = coeffs
            weighted = (coeffs.astype(jnp.float32) * weight_ref[...]).astype(jnp.bfloat16)
            products = lax.dot_general(
                weighted, coeffs, (((1,), (1,)), ((), ())), preferred_element_type=jnp.float32
            )
            real = products[:wide, :wide] + products[wide:, wide:]
            imag = products[:wide, wide:] - products[wide:, :wide]
            packed = jnp.where(row <= column, real, imag)
            own = packed[:blocks]
            for m in range(1, orders):
                own = jnp.where(owner == m, packed[m * blocks:(m + 1) * blocks], own)
            gram_ref[n] = before_ref[n] + own


def coeffs_and_gram(place, arrived, sec_count, time_basis, azimuth, weight, before):
    sec_local, rec_len, columns = arrived[0].shape
    sectors = sec_count * sec_local
    tm_count, halves = time_basis.shape[:2]
    blocks, wide = before.shape[1:]
    rows = azimuth.shape[1] // sectors
    together = 2 if sec_local % 2 == 0 else 1
    early_steps = sec_local // together
    steps = 2
    freqs = NFREQ // steps
    later = lambda i: jnp.maximum(i - early_steps, 0)
    early = lambda i: jnp.minimum(i, early_steps - 1)
    flops = 2 * columns * (
        sectors * time_basis.size + NFREQ * halves * azimuth.size + NFREQ * 4 * wide * wide
    )
    piece = pl.BlockSpec((together, rec_len, columns), lambda i, _: (early(i), 0, 0))
    return pl.pallas_call(
        functools.partial(coeff_kernel, sec_count, sec_local, freqs, wide // blocks),
        grid_spec=pltpu.PrefetchScalarGridSpec(
            num_scalar_prefetch=1,
            grid=(early_steps + steps,),
            in_specs=[
                pl.BlockSpec(time_basis.shape, lambda i, _: (0, 0, 0, 0)),
                pl.BlockSpec(azimuth.shape, lambda i, _: (0, 0)),
                pl.BlockSpec(weight.shape, lambda i, _: (0, 0)),
                pl.BlockSpec((freqs, blocks, wide), lambda i, _: (later(i), 0, 0)),
            ] + [piece] * len(arrived),
            out_specs=[
                pl.BlockSpec((freqs, 2 * wide, columns), lambda i, _: (later(i), 0, 0)),
                pl.BlockSpec((freqs, blocks, wide), lambda i, _: (later(i), 0, 0)),
            ],
            scratch_shapes=[pltpu.VMEM((sectors, halves, NFREQ * rows, columns), jnp.bfloat16)],
        ),
        out_shape=[
            jax.ShapeDtypeStruct((NFREQ, 2 * wide, columns), jnp.bfloat16),
            jax.ShapeDtypeStruct(before.shape, jnp.float32),
        ],
        compiler_params=pltpu.CompilerParams(vmem_limit_bytes=VMEM_LIMIT),
        cost_estimate=pl.CostEstimate(
            flops=flops,
            bytes_accessed=2 * columns * (sectors * tm_count * rec_len + NFREQ * 2 * wide),
            transcendentals=0,
        ),
        name="coeffs_and_gram",
    )(place, time_basis, azimuth, weight, before, *arrived)


def subspace_kernel(cell_total, first, packed_ref, basis_ref, energy_ref):
    size, _, pairs = packed_ref.shape
    row = lax.broadcasted_iota(jnp.int32, (size, pairs), 0)
    column_re, column_im = [], []
    for q in range(size):
        down, along = packed_ref[q], packed_ref[:, q, :]
        column_re.append(jnp.where(row <= q, down, along))
        column_im.append(jnp.where(row > q, down, jnp.where(row == q, 0.0, -along)))

    def image_of(vec_re, vec_im):
        out_re, out_im = [], []
        for j in range(MODES):
            sum_re = jnp.zeros_like(column_re[0])
            sum_im = jnp.zeros_like(column_re[0])
            for q in range(size):
                at_re, at_im = vec_re[j][q:q + 1], vec_im[j][q:q + 1]
                sum_re += column_re[q] * at_re - column_im[q] * at_im
                sum_im += column_re[q] * at_im + column_im[q] * at_re
            out_re.append(sum_re)
            out_im.append(sum_im)
        return out_re, out_im

    total = lambda x: jnp.sum(x, 0, keepdims=True)
    vec_re = [column_re[q] for q in first]
    vec_im = [column_im[q] for q in first]
    for sweep in range(SUBIT):
        if sweep > 0:
            vec_re, vec_im = image_of(vec_re, vec_im)
        vec_re, vec_im = list(vec_re), list(vec_im)
        for i in range(MODES):
            scale = 1.0 / jnp.sqrt(total(vec_re[i] * vec_re[i] + vec_im[i] * vec_im[i]) + EPSILON)
            own_re, own_im = vec_re[i] * scale, vec_im[i] * scale
            vec_re[i], vec_im[i] = own_re, own_im
            for j in range(i + 1, MODES):
                proj_re = total(own_re * vec_re[j] + own_im * vec_im[j])
                proj_im = total(own_re * vec_im[j] - own_im * vec_re[j])
                vec_re[j] = vec_re[j] - (proj_re * own_re - proj_im * own_im)
                vec_im[j] = vec_im[j] - (proj_re * own_im + proj_im * own_re)
    image_re, image_im = image_of(vec_re, vec_im)
    for j in range(MODES):
        basis_ref[0, j] = vec_re[j]
        basis_ref[1, j] = vec_im[j]
        energy_ref[j:j + 1] = total(vec_re[j] * image_re[j] + vec_im[j] * image_im[j]) / cell_total


def subspace(packed, first, cell_total):
    size, _, pairs = packed.shape
    return pl.pallas_call(
        functools.partial(subspace_kernel, float(cell_total), first),
        out_shape=[
            jax.ShapeDtypeStruct((2, MODES, size, pairs), jnp.float32),
            jax.ShapeDtypeStruct((MODES, pairs), jnp.float32),
        ],
        name="subspace",
    )(packed)


def mix_kernel(orders, fields, owner_ref, mixing_ref, spread_ref, factor_ref, root_ref, *refs):
    out_ref = refs[-1]
    freqs, own_rows, _ = mixing_ref.shape
    rows = 2 * own_rows
    total = spread_ref.shape[2]
    blocks = total // (2 * orders)
    row = lax.broadcasted_iota(jnp.int32, (rows, total), 0) % own_rows // (own_rows // orders)
    column = lax.broadcasted_iota(jnp.int32, (rows, total), 1) // blocks % orders
    factor = jnp.transpose(factor_ref[0])
    for n in range(freqs):
        wide = jnp.concatenate(
            [
                jnp.dot(mixing_ref[n], spread_ref[d], preferred_element_type=jnp.float32)
                for d in range(2)
            ],
            0,
        )
        wide = jnp.where(row == column, wide, 0.0).astype(jnp.bfloat16)
        scale = factor[:, n:n + 1] * root_ref[...]
        for k in range(fields):
            mixed = jnp.dot(wide, refs[k][n], preferred_element_type=jnp.float32)
            out_ref[k, n] = (mixed * scale).astype(jnp.bfloat16)


def mix(owner, coeffs, mixing, spread, factor, root_weight, owners, orders, after):
    rows = coeffs[0].shape[1]
    own_rows, depth = mixing.shape[1:]
    out_rows = 2 * own_rows
    columns = root_weight.shape[1]
    freqs, fields = NFREQ // owners, len(coeffs)
    return pl.pallas_call(
        functools.partial(mix_kernel, orders, fields),
        grid_spec=pltpu.PrefetchScalarGridSpec(
            num_scalar_prefetch=1,
            grid=(1,),
            in_specs=[
                pl.BlockSpec((freqs, own_rows, depth), lambda i, at: (at[0], 0, 0)),
                pl.BlockSpec(spread.shape, lambda i, at: (0, 0, 0)),
                pl.BlockSpec((1, freqs, out_rows), lambda i, at: (at[0], 0, 0)),
                pl.BlockSpec(root_weight.shape, lambda i, at: (0, 0)),
            ] + [
                pl.BlockSpec((freqs, rows, x.shape[2]), lambda i, at: (at[0], 0, 0)) for x in coeffs
            ] + [pl.BlockSpec(memory_space=pl.ANY)] * len(after),
            out_specs=pl.BlockSpec((fields, freqs, out_rows, columns), lambda i, at: (0, 0, 0, 0)),
        ),
        out_shape=jax.ShapeDtypeStruct((fields, freqs, out_rows, columns), jnp.bfloat16),
        compiler_params=pltpu.CompilerParams(vmem_limit_bytes=VMEM_LIMIT),
        cost_estimate=pl.CostEstimate(
            flops=2 * freqs * out_rows * rows * fields * columns,
            bytes_accessed=2 * freqs * (rows + out_rows) * fields * columns,
            transcendentals=0,
        ),
        name="mix",
    )(jnp.reshape(owner, (1,)), mixing, spread, factor, root_weight, *coeffs, *after)


def take_kernel(place_ref, record_ref, out_ref):
    out_ref[...] = record_ref[:, 0]


def take(by_field, k, owner, owners):
    sec_local, _, rec_len, cells = by_field.shape
    count = cells // owners
    if count % LANES:
        return lax.dynamic_slice_in_dim(by_field[:, k], owner * count, count, 2)
    return pl.pallas_call(
        take_kernel,
        grid_spec=pltpu.PrefetchScalarGridSpec(
            num_scalar_prefetch=1,
            grid=(1,),
            in_specs=[
                pl.BlockSpec((sec_local, 1, rec_len, count), lambda i, at: (0, k, 0, at[0]))
            ],
            out_specs=pl.BlockSpec((sec_local, rec_len, count), lambda i, at: (0, 0, 0)),
        ),
        out_shape=jax.ShapeDtypeStruct((sec_local, rec_len, count), by_field.dtype),
        compiler_params=pltpu.CompilerParams(vmem_limit_bytes=VMEM_LIMIT),
        cost_estimate=pl.CostEstimate(
            flops=0, bytes_accessed=4 * sec_local * rec_len * count, transcendentals=0
        ),
        name="take",
    )(jnp.reshape(owner, (1,)), by_field)


def unpack_kernel(count, owner_ref, *refs):
    out_ref = refs[-1]
    step = pl.program_id(0)
    for n in range(count):

        @pl.when(step == n)
        def _():
            for k in range(refs[n].shape[0]):
                for f in range(refs[n].shape[1]):
                    for d in range(refs[n].shape[2]):
                        out_ref[:, f, d, k] = refs[n][k, f, d]


def unpack(sources, pieces, owners, whole):
    fields, freqs, two, orders, modes, part = pieces[0].shape
    shape = (orders, freqs, two, fields, modes, owners * part)
    if part % LANES:
        whole = jnp.zeros(shape, pieces[0].dtype) if whole is None else whole
        for owner, piece in zip(sources, pieces):
            piece = jnp.transpose(piece, (3, 1, 2, 0, 4, 5))
            whole = lax.dynamic_update_slice_in_dim(whole, piece, owner * part, 5)
        return whole
    count = len(pieces)
    inputs = list(pieces) if whole is None else list(pieces) + [whole]
    in_specs = [
        pl.BlockSpec(pieces[0].shape, lambda i, at: (0, 0, 0, 0, 0, 0)) for _ in pieces
    ] + [pl.BlockSpec(memory_space=pl.ANY)]
    return pl.pallas_call(
        functools.partial(unpack_kernel, count),
        grid_spec=pltpu.PrefetchScalarGridSpec(
            num_scalar_prefetch=1,
            grid=(count,),
            in_specs=in_specs[:len(inputs)],
            out_specs=pl.BlockSpec(shape[:5] + (part,), lambda i, at: (0, 0, 0, 0, 0, at[i])),
        ),
        out_shape=jax.ShapeDtypeStruct(shape, pieces[0].dtype),
        input_output_aliases={} if whole is None else {1 + count: 0},
        compiler_params=pltpu.CompilerParams(vmem_limit_bytes=VMEM_LIMIT),
        cost_estimate=pl.CostEstimate(
            flops=0, bytes_accessed=4 * count * pieces[0].size, transcendentals=0
        ),
        name="unpack",
    )(jnp.stack(sources), *inputs)


def local(records, block_start, slab_index, weight_table):
    sec_local, rec_len, fields, cell_local = records.shape
    sec_count = lax.axis_size("sector")
    tm_count = lax.axis_size("tm")
    space_count = lax.axis_size("space")
    owners = sec_count * tm_count
    owner_axes = ("sector", "tm")
    sectors = sec_local * sec_count
    orders = sectors // 2
    blocks = block_start.shape[0]
    depth = 2 * blocks
    part = cell_local // owners
    own_freqs = NFREQ // owners
    me = lax.axis_index("sector") * tm_count + lax.axis_index("tm")

    by_field = jnp.transpose(records, (0, 2, 1, 3))
    sec_at, tm_at = lax.axis_index("sector"), lax.axis_index("tm")
    shifts = [(z, x) for z in range(sec_count) for x in range(tm_count)]
    in_order = sorted(
        [r for r in shifts if r != (0, 0)], key=lambda r: (r[0] == 0, abs(2 * r[0] - sec_count), r)
    )

    def owner_after(z, x):
        return (sec_at + z) % sec_count * tm_count + (tm_at + x) % tm_count

    def send(piece, z, x):
        if (z, x) == (0, 0):
            return piece
        hops = [
            (a * tm_count + j, (a + z) % sec_count * tm_count + (j + x) % tm_count)
            for a in range(sec_count)
            for j in range(tm_count)
        ]
        return lax.ppermute(piece, owner_axes, hops)

    arrived = []
    for k in range(fields):
        got = {r: send(take(by_field, k, owner_after(*r), owners), *r) for r in in_order + [(0, 0)]}
        arrived.append([got[r] for r in shifts])

    time_basis = placed_time_basis(block_start, tm_count)
    half, _ = half_span(blocks // tm_count)
    halves = blocks // tm_count // half
    azimuth = jnp.einsum(
        "mcse,ij,bd->cmibsjed",
        order_table(orders, sectors),
        jnp.eye(tm_count, dtype=jnp.bfloat16),
        jnp.eye(half, dtype=jnp.bfloat16),
    ).reshape(2 * orders * tm_count * half, sectors * tm_count * 2 * half)
    place = [
        (b // half % halves * tm_count + b // (half * halves)) * half + b % half
        for b in range(blocks)
    ]
    own_slab = lax.dynamic_slice_in_dim(slab_index, me * part, part)
    weight = jnp.sum(
        jnp.where(
            own_slab[None, :] == jnp.arange(weight_table.shape[0], dtype=jnp.int32)[:, None],
            weight_table[:, None],
            0.0,
        ),
        0,
        keepdims=True,
    )

    gram = jnp.zeros((NFREQ, blocks, orders * blocks), jnp.float32)

    coeffs = []
    for k in range(fields):
        own, gram = coeffs_and_gram(
            jnp.stack([sec_at, tm_at]), arrived[k], sec_count, time_basis, azimuth, weight, gram
        )
        coeffs.append(own)

    if own_freqs % space_count == 0:
        axes = owner_axes + ("space",)
    else:
        gram = lax.psum(gram, "space")
        axes = owner_axes
    solvers = math.prod(lax.axis_size(a) for a in axes)
    solved = NFREQ // solvers
    gram = gram.reshape((solvers, solved) + gram.shape[1:])
    gram = lax.all_to_all(gram, axes, split_axis=0, concat_axis=0, tiled=True)
    gram = jnp.sum(gram, 0).reshape(solved, blocks, orders, blocks)
    gram = jnp.transpose(gram, (3, 1, 0, 2)).reshape(blocks, blocks, solved * orders)
    basis, energy = subspace(gram, tuple(place[:MODES]), fields * cell_local * space_count)

    short = basis.astype(jnp.bfloat16).reshape(2, MODES, blocks, solved, orders)
    mixing = jnp.transpose(short, (3, 4, 1, 0, 2)).reshape(solved, orders * MODES * depth)
    energy = jnp.transpose(energy.reshape(MODES, solved, orders), (1, 2, 0)).reshape(solved, -1)
    high = energy.astype(jnp.bfloat16)
    rest = energy - high.astype(jnp.float32)
    middle = rest.astype(jnp.bfloat16)
    low = (rest - middle.astype(jnp.float32)).astype(jnp.bfloat16)
    packet = jnp.concatenate([mixing, high, middle, low], 1)
    width = -(-packet.shape[1] // LANES) * LANES
    packet = jnp.pad(packet, ((0, 0), (0, width - packet.shape[1])))
    packet = packet.reshape(1, solved, width // LANES, LANES)
    packet = jnp.broadcast_to(packet, (solvers,) + packet.shape[1:])
    packet = lax.all_to_all(packet, axes, split_axis=0, concat_axis=0, tiled=True)
    packet = packet.reshape(NFREQ, width)
    count = orders * MODES
    mixing = packet[:, :orders * MODES * depth].reshape(NFREQ, orders * MODES, depth)
    tail = packet[:, orders * MODES * depth:].astype(jnp.float32)
    energy = (tail[:, :count] + tail[:, count:2 * count]) + tail[:, 2 * count:3 * count]
    factor = lax.rsqrt(energy)
    factor = jnp.concatenate([factor, factor], 1).reshape(owners, own_freqs, orders * 2 * MODES)
    energy = energy.reshape(NFREQ, orders, MODES)
    root_weight = jnp.sqrt(weight)
    signs = jnp.array([[[1, 0], [0, -1]], [[0, 1], [1, 0]]], jnp.bfloat16)
    spread = jnp.broadcast_to(
        signs[:, :, None, :, None, None]
        * jnp.eye(blocks, dtype=jnp.bfloat16)[None, None, :, None, None, :],
        (2, 2, blocks, 2, orders, blocks),
    ).reshape(2, depth, depth * orders)

    coeffs = [pltpu.with_memory_space_constraint(x, pltpu.HBM) for x in coeffs]
    sent = {}
    before = ()
    for z, x in in_order + [(0, 0)]:
        piece = mix(
            owner_after(z, x), coeffs, mixing, spread, factor, root_weight, owners, orders, before
        )
        before = (piece,)
        sent[z, x] = owner_after(-z, -x), send(piece, z, x)
    late = [r for r in in_order if r[0] in (0, 1) and r[1] > 0 or r == in_order[-tm_count]]
    groups = [[(0, 0)]] + [[r] for r in in_order if r not in late] + [late]
    mode_fields = None
    for group in groups:
        pieces = [sent[r][1].reshape(fields, own_freqs, 2, orders, MODES, part) for r in group]
        mode_fields = unpack([sent[r][0] for r in group], pieces, owners, mode_fields)
    mode_fields = jnp.transpose(mode_fields, (0, 1, 2, 4, 3, 5))
    own_energy = lax.dynamic_slice_in_dim(energy, me * own_freqs, own_freqs)
    return (mode_fields, jnp.transpose(own_energy, (1, 0, 2)))


def solution(mesh):
    placed = (P("sector", "tm", None, "space"), P(), P("space"), P())
    return jax.shard_map(
        local,
        mesh=mesh,
        in_specs=placed,
        out_specs=(
            P(None, ("sector", "tm"), None, None, None, "space"),
            P(None, ("sector", "tm"), None),
        ),
        check_vma=False,
    )
```

```python
import functools
import math

import jax
import jax.numpy as jnp
from jax import lax
from jax.experimental import pallas as pl
from jax.experimental.pallas import tpu as pltpu
from jax.sharding import PartitionSpec as P

NFFT = 64
NFREQ = 32
MODES = 8
SUBIT = 4
LANES = 128
EPSILON = 1e-06
VMEM_LIMIT = 48 * 1024 * 1024


def time_table(length, freq_count):
    steps_t = jnp.arange(length, dtype=jnp.float32)
    freq_f = jnp.arange(freq_count, dtype=jnp.float32)
    window = 0.5 - 0.5 * jnp.cos(2.0 * math.pi * steps_t / length)
    angles = 2.0 * math.pi * freq_f[:, None] * steps_t[None, :] / length
    both = jnp.stack([window * jnp.cos(angles), -window * jnp.sin(angles)])
    return (both / math.sqrt(length)).astype(jnp.bfloat16)


def order_table(orders, sectors):
    order_m = jnp.arange(orders, dtype=jnp.float32)[:, None]
    sector_s = jnp.arange(sectors, dtype=jnp.float32)[None, :]
    angles = 2.0 * math.pi * order_m * sector_s / sectors
    cosine = jnp.cos(angles)
    sine_part = jnp.sin(angles)
    upper_row = jnp.stack([cosine, sine_part], -1)
    lower_row = jnp.stack([-sine_part, cosine], -1)
    return (jnp.stack([upper_row, lower_row], 1) / math.sqrt(sectors)).astype(jnp.bfloat16)


def half_span(blocks):
    half = blocks // 2
    return half, (half - 1) * (NFFT // 2) + NFFT // 8 + NFFT


def placed_time_basis(block_start, tm_count):
    blocks = block_start.shape[0] // tm_count
    half, span = half_span(blocks)
    basis = time_table(NFFT, NFREQ)
    first = jnp.arange(blocks, dtype=jnp.int32) // half * (half * (NFFT // 2))
    inside = block_start.reshape(tm_count, blocks) - first[None, :]
    place = (
        inside[:, :, None, None] + jnp.arange(NFFT, dtype=jnp.int32)[:, None]
        == jnp.arange(span, dtype=jnp.int32)[None, :]
    ).astype(jnp.bfloat16)
    table = jnp.einsum(
        "eft,jhbtu->jhfebu",
        basis,
        place.reshape(tm_count, 2, half, NFFT, span),
        preferred_element_type=jnp.float32,
    ).astype(jnp.bfloat16)
    return table.reshape(tm_count, 2, NFREQ * 2 * half, span)


def coeff_kernel(sec_count, sec_local, freqs, orders, place_ref, time_ref, azimuth_ref, weight_ref,
                 before_ref, *refs):
    record_refs, (coeff_ref, gram_ref, spectra) = refs[:-3], refs[-3:]
    step = pl.program_id(0)
    tm_count, halves, _, span = time_ref.shape
    together, rec_len, columns = record_refs[0].shape
    early_steps = sec_local // together
    sectors = spectra.shape[0]
    rows = spectra.shape[2] // NFREQ

    @pl.when(step < early_steps)
    def _():
        for shift, s in [(shift, s) for shift in range(sec_count) for s in range(together)]:
            source = lax.rem(place_ref[0] + sec_count - shift, sec_count)
            own = record_refs[shift * tm_count:(shift + 1) * tm_count]
            for h in range(halves):
                first = h * (rec_len - span) // (halves - 1)
                parts = []
                for j in range(tm_count):
                    piece = own[0][s, first:first + span]
                    for x in range(1, tm_count):
                        here = lax.rem(place_ref[1] + tm_count - x, tm_count) == j
                        piece = jnp.where(here, own[x][s, first:first + span], piece)
                    part = jnp.dot(time_ref[j, h], piece, preferred_element_type=jnp.float32)
                    parts.append(part.reshape(NFREQ, rows // tm_count, columns))
                joined = jnp.stack(parts, 1).reshape(NFREQ * rows, columns)
                spectra[source * sec_local + step * together + s, h] = joined.astype(jnp.bfloat16)

    @pl.when(step >= early_steps)
    def _():
        half_rows = azimuth_ref.shape[0]
        depth = half_rows // (2 * orders)
        blocks = depth * halves
        wide = orders * blocks
        row = lax.broadcasted_iota(jnp.int32, (wide, wide), 0) % blocks
        column = lax.broadcasted_iota(jnp.int32, (wide, wide), 1) % blocks
        owner = lax.broadcasted_iota(jnp.int32, (blocks, wide), 1) // blocks
        for n in range(freqs):
            at = pl.multiple_of(((step - early_steps) * freqs + n) * rows, rows)
            own = [
                spectra[:, h, pl.ds(at, rows), :].reshape(sectors * rows, columns)
                for h in range(halves)
            ]
            parts = [
                jnp.dot(azimuth_ref[...], x, preferred_element_type=jnp.float32) for x in own
            ]
            parts = [x.reshape(2 * orders, depth, columns) for x in parts]
            coeffs = jnp.stack(parts, 1).reshape(2 * wide, columns).astype(jnp.bfloat16)
            coeff_ref[n] = coeffs
            weighted = (coeffs.astype(jnp.float32) * weight_ref[...]).astype(jnp.bfloat16)
            products = lax.dot_general(
                weighted, coeffs, (((1,), (1,)), ((), ())), preferred_element_type=jnp.float32
            )
            real = products[:wide, :wide] + products[wide:, wide:]
            imag = products[:wide, wide:] - products[wide:, :wide]
            packed = jnp.where(row <= column, real, imag)
            own = packed[:blocks]
            for m in range(1, orders):
                own = jnp.where(owner == m, packed[m * blocks:(m + 1) * blocks], own)
            gram_ref[n] = before_ref[n] + own


def coeffs_and_gram(place, arrived, sec_count, time_basis, azimuth, weight, before):
    sec_local, rec_len, columns = arrived[0].shape
    sectors = sec_count * sec_local
    tm_count, halves = time_basis.shape[:2]
    blocks, wide = before.shape[1:]
    rows = azimuth.shape[1] // sectors
    together = 2 if sec_local % 2 == 0 else 1
    early_steps = sec_local // together
    steps = 2
    freqs = NFREQ // steps
    later = lambda i: jnp.maximum(i - early_steps, 0)
    early = lambda i: jnp.minimum(i, early_steps - 1)
    flops = 2 * columns * (
        sectors * time_basis.size + NFREQ * halves * azimuth.size + NFREQ * 4 * wide * wide
    )
    piece = pl.BlockSpec((together, rec_len, columns), lambda i, _: (early(i), 0, 0))
    return pl.pallas_call(
        functools.partial(coeff_kernel, sec_count, sec_local, freqs, wide // blocks),
        grid_spec=pltpu.PrefetchScalarGridSpec(
            num_scalar_prefetch=1,
            grid=(early_steps + steps,),
            in_specs=[
                pl.BlockSpec(time_basis.shape, lambda i, _: (0, 0, 0, 0)),
                pl.BlockSpec(azimuth.shape, lambda i, _: (0, 0)),
                pl.BlockSpec(weight.shape, lambda i, _: (0, 0)),
                pl.BlockSpec((freqs, blocks, wide), lambda i, _: (later(i), 0, 0)),
            ] + [piece] * len(arrived),
            out_specs=[
                pl.BlockSpec((freqs, 2 * wide, columns), lambda i, _: (later(i), 0, 0)),
                pl.BlockSpec((freqs, blocks, wide), lambda i, _: (later(i), 0, 0)),
            ],
            scratch_shapes=[pltpu.VMEM((sectors, halves, NFREQ * rows, columns), jnp.bfloat16)],
        ),
        out_shape=[
            jax.ShapeDtypeStruct((NFREQ, 2 * wide, columns), jnp.bfloat16),
            jax.ShapeDtypeStruct(before.shape, jnp.float32),
        ],
        compiler_params=pltpu.CompilerParams(vmem_limit_bytes=VMEM_LIMIT),
        cost_estimate=pl.CostEstimate(
            flops=flops,
            bytes_accessed=2 * columns * (sectors * tm_count * rec_len + NFREQ * 2 * wide),
            transcendentals=0,
        ),
        name="coeffs_and_gram",
    )(place, time_basis, azimuth, weight, before, *arrived)


def subspace_kernel(cell_total, first, packed_ref, basis_ref, energy_ref):
    size, _, pairs = packed_ref.shape
    row = lax.broadcasted_iota(jnp.int32, (size, pairs), 0)
    column_re, column_im = [], []
    for q in range(size):
        down, along = packed_ref[q], packed_ref[:, q, :]
        column_re.append(jnp.where(row <= q, down, along))
        column_im.append(jnp.where(row > q, down, jnp.where(row == q, 0.0, -along)))

    def image_of(vec_re, vec_im):
        out_re, out_im = [], []
        for j in range(MODES):
            sum_re = jnp.zeros_like(column_re[0])
            sum_im = jnp.zeros_like(column_re[0])
            for q in range(size):
                at_re, at_im = vec_re[j][q:q + 1], vec_im[j][q:q + 1]
                sum_re += column_re[q] * at_re - column_im[q] * at_im
                sum_im += column_re[q] * at_im + column_im[q] * at_re
            out_re.append(sum_re)
            out_im.append(sum_im)
        return out_re, out_im

    total = lambda x: jnp.sum(x, 0, keepdims=True)
    vec_re = [column_re[q] for q in first]
    vec_im = [column_im[q] for q in first]
    for sweep in range(SUBIT):
        if sweep > 0:
            vec_re, vec_im = image_of(vec_re, vec_im)
        vec_re, vec_im = list(vec_re), list(vec_im)
        for i in range(MODES):
            scale = 1.0 / jnp.sqrt(total(vec_re[i] * vec_re[i] + vec_im[i] * vec_im[i]) + EPSILON)
            own_re, own_im = vec_re[i] * scale, vec_im[i] * scale
            vec_re[i], vec_im[i] = own_re, own_im
            for j in range(i + 1, MODES):
                proj_re = total(own_re * vec_re[j] + own_im * vec_im[j])
                proj_im = total(own_re * vec_im[j] - own_im * vec_re[j])
                vec_re[j] = vec_re[j] - (proj_re * own_re - proj_im * own_im)
                vec_im[j] = vec_im[j] - (proj_re * own_im + proj_im * own_re)
    image_re, image_im = image_of(vec_re, vec_im)
    for j in range(MODES):
        basis_ref[0, j] = vec_re[j]
        basis_ref[1, j] = vec_im[j]
        energy_ref[j:j + 1] = total(vec_re[j] * image_re[j] + vec_im[j] * image_im[j]) / cell_total


def subspace(packed, first, cell_total):
    size, _, pairs = packed.shape
    return pl.pallas_call(
        functools.partial(subspace_kernel, float(cell_total), first),
        out_shape=[
            jax.ShapeDtypeStruct((2, MODES, size, pairs), jnp.float32),
            jax.ShapeDtypeStruct((MODES, pairs), jnp.float32),
        ],
        name="subspace",
    )(packed)


def mix_kernel(orders, fields, owner_ref, mixing_ref, spread_ref, factor_ref, root_ref, *refs):
    out_ref = refs[-1]
    freqs, own_rows, _ = mixing_ref.shape
    rows = 2 * own_rows
    total = spread_ref.shape[2]
    blocks = total // (2 * orders)
    row = lax.broadcasted_iota(jnp.int32, (rows, total), 0) % own_rows // (own_rows // orders)
    column = lax.broadcasted_iota(jnp.int32, (rows, total), 1) // blocks % orders
    factor = jnp.transpose(factor_ref[0])
    for n in range(freqs):
        wide = jnp.concatenate(
            [
                jnp.dot(mixing_ref[n], spread_ref[d], preferred_element_type=jnp.float32)
                for d in range(2)
            ],
            0,
        )
        wide = jnp.where(row == column, wide, 0.0).astype(jnp.bfloat16)
        scale = factor[:, n:n + 1] * root_ref[...]
        for k in range(fields):
            mixed = jnp.dot(wide, refs[k][n], preferred_element_type=jnp.float32)
            out_ref[k, n] = (mixed * scale).astype(jnp.bfloat16)


def mix(owner, coeffs, mixing, spread, factor, root_weight, owners, orders, after):
    rows = coeffs[0].shape[1]
    own_rows, depth = mixing.shape[1:]
    out_rows = 2 * own_rows
    columns = root_weight.shape[1]
    freqs, fields = NFREQ // owners, len(coeffs)
    return pl.pallas_call(
        functools.partial(mix_kernel, orders, fields),
        grid_spec=pltpu.PrefetchScalarGridSpec(
            num_scalar_prefetch=1,
            grid=(1,),
            in_specs=[
                pl.BlockSpec((freqs, own_rows, depth), lambda i, at: (at[0], 0, 0)),
                pl.BlockSpec(spread.shape, lambda i, at: (0, 0, 0)),
                pl.BlockSpec((1, freqs, out_rows), lambda i, at: (at[0], 0, 0)),
                pl.BlockSpec(root_weight.shape, lambda i, at: (0, 0)),
            ] + [
                pl.BlockSpec((freqs, rows, x.shape[2]), lambda i, at: (at[0], 0, 0)) for x in coeffs
            ] + [pl.BlockSpec(memory_space=pl.ANY)] * len(after),
            out_specs=pl.BlockSpec((fields, freqs, out_rows, columns), lambda i, at: (0, 0, 0, 0)),
        ),
        out_shape=jax.ShapeDtypeStruct((fields, freqs, out_rows, columns), jnp.bfloat16),
        compiler_params=pltpu.CompilerParams(vmem_limit_bytes=VMEM_LIMIT),
        cost_estimate=pl.CostEstimate(
            flops=2 * freqs * out_rows * rows * fields * columns,
            bytes_accessed=2 * freqs * (rows + out_rows) * fields * columns,
            transcendentals=0,
        ),
        name="mix",
    )(jnp.reshape(owner, (1,)), mixing, spread, factor, root_weight, *coeffs, *after)


def take_kernel(place_ref, record_ref, out_ref):
    out_ref[...] = record_ref[:, 0]


def take(by_field, k, owner, owners):
    sec_local, _, rec_len, cells = by_field.shape
    count = cells // owners
    if count % LANES:
        return lax.dynamic_slice_in_dim(by_field[:, k], owner * count, count, 2)
    return pl.pallas_call(
        take_kernel,
        grid_spec=pltpu.PrefetchScalarGridSpec(
            num_scalar_prefetch=1,
            grid=(1,),
            in_specs=[
                pl.BlockSpec((sec_local, 1, rec_len, count), lambda i, at: (0, k, 0, at[0]))
            ],
            out_specs=pl.BlockSpec((sec_local, rec_len, count), lambda i, at: (0, 0, 0)),
        ),
        out_shape=jax.ShapeDtypeStruct((sec_local, rec_len, count), by_field.dtype),
        compiler_params=pltpu.CompilerParams(vmem_limit_bytes=VMEM_LIMIT),
        cost_estimate=pl.CostEstimate(
            flops=0, bytes_accessed=4 * sec_local * rec_len * count, transcendentals=0
        ),
        name="take",
    )(jnp.reshape(owner, (1,)), by_field)


def unpack_kernel(count, owner_ref, *refs):
    out_ref = refs[-1]
    step = pl.program_id(0)
    for n in range(count):

        @pl.when(step == n)
        def _():
            for k in range(refs[n].shape[0]):
                for f in range(refs[n].shape[1]):
                    for d in range(refs[n].shape[2]):
                        out_ref[:, f, d, k] = refs[n][k, f, d]


def unpack(sources, pieces, owners, whole):
    fields, freqs, two, orders, modes, part = pieces[0].shape
    shape = (orders, freqs, two, fields, modes, owners * part)
    if part % LANES:
        whole = jnp.zeros(shape, pieces[0].dtype) if whole is None else whole
        for owner, piece in zip(sources, pieces):
            piece = jnp.transpose(piece, (3, 1, 2, 0, 4, 5))
            whole = lax.dynamic_update_slice_in_dim(whole, piece, owner * part, 5)
        return whole
    count = len(pieces)
    inputs = list(pieces) if whole is None else list(pieces) + [whole]
    in_specs = [
        pl.BlockSpec(pieces[0].shape, lambda i, at: (0, 0, 0, 0, 0, 0)) for _ in pieces
    ] + [pl.BlockSpec(memory_space=pl.ANY)]
    return pl.pallas_call(
        functools.partial(unpack_kernel, count),
        grid_spec=pltpu.PrefetchScalarGridSpec(
            num_scalar_prefetch=1,
            grid=(count,),
            in_specs=in_specs[:len(inputs)],
            out_specs=pl.BlockSpec(shape[:5] + (part,), lambda i, at: (0, 0, 0, 0, 0, at[i])),
        ),
        out_shape=jax.ShapeDtypeStruct(shape, pieces[0].dtype),
        input_output_aliases={} if whole is None else {1 + count: 0},
        compiler_params=pltpu.CompilerParams(vmem_limit_bytes=VMEM_LIMIT),
        cost_estimate=pl.CostEstimate(
            flops=0, bytes_accessed=4 * count * pieces[0].size, transcendentals=0
        ),
        name="unpack",
    )(jnp.stack(sources), *inputs)


def local(records, block_start, slab_index, weight_table):
    sec_local, rec_len, fields, cell_local = records.shape
    sec_count = lax.axis_size("sector")
    tm_count = lax.axis_size("tm")
    space_count = lax.axis_size("space")
    owners = sec_count * tm_count
    owner_axes = ("sector", "tm")
    sectors = sec_local * sec_count
    orders = sectors // 2
    blocks = block_start.shape[0]
    depth = 2 * blocks
    part = cell_local // owners
    own_freqs = NFREQ // owners
    me = lax.axis_index("sector") * tm_count + lax.axis_index("tm")

    by_field = jnp.transpose(records, (0, 2, 1, 3))
    sec_at, tm_at = lax.axis_index("sector"), lax.axis_index("tm")
    shifts = [(z, x) for z in range(sec_count) for x in range(tm_count)]
    in_order = sorted(
        [r for r in shifts if r != (0, 0)], key=lambda r: (r[0] == 0, abs(2 * r[0] - sec_count), r)
    )

    def owner_after(z, x):
        return (sec_at + z) % sec_count * tm_count + (tm_at + x) % tm_count

    def send(piece, z, x):
        if (z, x) == (0, 0):
            return piece
        hops = [
            (a * tm_count + j, (a + z) % sec_count * tm_count + (j + x) % tm_count)
            for a in range(sec_count)
            for j in range(tm_count)
        ]
        return lax.ppermute(piece, owner_axes, hops)

    arrived = []
    for k in range(fields):
        got = {r: send(take(by_field, k, owner_after(*r), owners), *r) for r in in_order + [(0, 0)]}
        arrived.append([got[r] for r in shifts])

    time_basis = placed_time_basis(block_start, tm_count)
    half, _ = half_span(blocks // tm_count)
    halves = blocks // tm_count // half
    azimuth = jnp.einsum(
        "mcse,ij,bd->cmibsjed",
        order_table(orders, sectors),
        jnp.eye(tm_count, dtype=jnp.bfloat16),
        jnp.eye(half, dtype=jnp.bfloat16),
    ).reshape(2 * orders * tm_count * half, sectors * tm_count * 2 * half)
    place = [
        (b // half % halves * tm_count + b // (half * halves)) * half + b % half
        for b in range(blocks)
    ]
    own_slab = lax.dynamic_slice_in_dim(slab_index, me * part, part)
    weight = jnp.sum(
        jnp.where(
            own_slab[None, :] == jnp.arange(weight_table.shape[0], dtype=jnp.int32)[:, None],
            weight_table[:, None],
            0.0,
        ),
        0,
        keepdims=True,
    )

    gram = jnp.zeros((NFREQ, blocks, orders * blocks), jnp.float32)

    coeffs = []
    for k in range(fields):
        own, gram = coeffs_and_gram(
            jnp.stack([sec_at, tm_at]), arrived[k], sec_count, time_basis, azimuth, weight, gram
        )
        coeffs.append(own)

    if own_freqs % space_count == 0:
        axes = owner_axes + ("space",)
    else:
        gram = lax.psum(gram, "space")
        axes = owner_axes
    solvers = math.prod(lax.axis_size(a) for a in axes)
    solved = NFREQ // solvers
    gram = gram.reshape((solvers, solved) + gram.shape[1:])
    gram = lax.all_to_all(gram, axes, split_axis=0, concat_axis=0, tiled=True)
    gram = jnp.sum(gram, 0).reshape(solved, blocks, orders, blocks)
    gram = jnp.transpose(gram, (3, 1, 0, 2)).reshape(blocks, blocks, solved * orders)
    basis, energy = subspace(gram, tuple(place[:MODES]), fields * cell_local * space_count)

    short = basis.astype(jnp.bfloat16).reshape(2, MODES, blocks, solved, orders)
    mixing = jnp.transpose(short, (3, 4, 1, 0, 2)).reshape(solved, orders * MODES * depth)
    energy = jnp.transpose(energy.reshape(MODES, solved, orders), (1, 2, 0)).reshape(solved, -1)
    high = energy.astype(jnp.bfloat16)
    rest = energy - high.astype(jnp.float32)
    middle = rest.astype(jnp.bfloat16)
    low = (rest - middle.astype(jnp.float32)).astype(jnp.bfloat16)
    packet = jnp.concatenate([mixing, high, middle, low], 1)
    width = -(-packet.shape[1] // LANES) * LANES
    packet = jnp.pad(packet, ((0, 0), (0, width - packet.shape[1])))
    packet = packet.reshape(1, solved, width // LANES, LANES)
    packet = jnp.broadcast_to(packet, (solvers,) + packet.shape[1:])
    packet = lax.all_to_all(packet, axes, split_axis=0, concat_axis=0, tiled=True)
    packet = packet.reshape(NFREQ, width)
    count = orders * MODES
    mixing = packet[:, :orders * MODES * depth].reshape(NFREQ, orders * MODES, depth)
    tail = packet[:, orders * MODES * depth:].astype(jnp.float32)
    energy = (tail[:, :count] + tail[:, count:2 * count]) + tail[:, 2 * count:3 * count]
    factor = lax.rsqrt(energy)
    factor = jnp.concatenate([factor, factor], 1).reshape(owners, own_freqs, orders * 2 * MODES)
    energy = energy.reshape(NFREQ, orders, MODES)
    root_weight = jnp.sqrt(weight)
    signs = jnp.array([[[1, 0], [0, -1]], [[0, 1], [1, 0]]], jnp.bfloat16)
    spread = jnp.broadcast_to(
        signs[:, :, None, :, None, None]
        * jnp.eye(blocks, dtype=jnp.bfloat16)[None, None, :, None, None, :],
        (2, 2, blocks, 2, orders, blocks),
    ).reshape(2, depth, depth * orders)

    coeffs = [pltpu.with_memory_space_constraint(x, pltpu.HBM) for x in coeffs]
    sent = {}
    before = ()
    for z, x in in_order + [(0, 0)]:
        piece = mix(
            owner_after(z, x), coeffs, mixing, spread, factor, root_weight, owners, orders, before
        )
        before = (piece,)
        sent[z, x] = owner_after(-z, -x), send(piece, z, x)
    late = [r for r in in_order if r[0] == 0 or r == in_order[-tm_count]]
    groups = [[(0, 0)]] + [[r] for r in in_order if r not in late] + [late]
    mode_fields = None
    for group in groups:
        pieces = [sent[r][1].reshape(fields, own_freqs, 2, orders, MODES, part) for r in group]
        mode_fields = unpack([sent[r][0] for r in group], pieces, owners, mode_fields)
    mode_fields = jnp.transpose(mode_fields, (0, 1, 2, 4, 3, 5))
    own_energy = lax.dynamic_slice_in_dim(energy, me * own_freqs, own_freqs)
    return (mode_fields, jnp.transpose(own_energy, (1, 0, 2)))


def solution(mesh):
    placed = (P("sector", "tm", None, "space"), P(), P("space"), P())
    return jax.shard_map(
        local,
        mesh=mesh,
        in_specs=placed,
        out_specs=(
            P(None, ("sector", "tm"), None, None, None, "space"),
            P(None, ("sector", "tm"), None),
        ),
        check_vma=False,
    )
```
